32 devices in a mesh: head: 2 (over core), dp: 16 (over z, y, x).
Axes of the slice: x: 2, y: 2, z: 4, core: 2. Of those that a mesh axis runs over, the one named last changes fastest.
Arguments:
- tokens: bfloat16 [16384, 768], P(('dp', 'head')), may hold values from -6 to 6
- segment_ids: int32 [16384], P('dp'), may hold values from 0 to 7, as said below
- routes: int32 [16384, 1], P('dp'), may hold values from 0 to 15; in each aligned block of 512 rows (0 to 511, 512 to 1023, ...) at most 64 rows name the same one
- norm_gains: bfloat16 [4, 768], replicated, may hold values from 0.5 to 1.5
- qkv_one: bfloat16 [3, 768, 768], P(None, None, 'head'), may hold values from -0.21875 to 0.21875
- out_one: bfloat16 [768, 768], P('head'), may hold values from -0.625 to 0.625
- up_one: bfloat16 [768, 3072], P(None, 'head'), may hold values from -0.21875 to 0.21875
- down_one: bfloat16 [3072, 768], P('head'), may hold values from -0.21875 to 0.21875
- qkv_two: bfloat16 [3, 768, 768], P(None, None, 'head'), may hold values from -0.21875 to 0.21875
- out_two: bfloat16 [768, 768], P('head'), may hold values from -0.625 to 0.625
- expert_up: bfloat16 [16, 768, 3072], P('dp', None, 'head'), may hold values from -0.21875 to 0.21875
- expert_down: bfloat16 [16, 3072, 768], P('dp', 'head'), may hold values from -0.21875 to 0.21875
- centroids: bfloat16 [16, 768], P('dp'), may hold values from -0.15625 to 0.15625
- cotangent: bfloat16 [16384, 768], P(('dp', 'head')), may hold values from -6 to 6
Outputs:
- first_out: bfloat16 [16384, 768], P(('dp', 'head'))
- second_out: bfloat16 [16384, 768], P(('dp', 'head'))
- input_grad: float32 [16384, 768], P(('dp', 'head'))
- gains_grad: float32 [4, 768], replicated
- qkv_one_grad: float32 [3, 768, 768], P(None, None, 'head')
- out_one_grad: float32 [768, 768], P('head')
- up_one_grad: float32 [768, 3072], P(None, 'head')
- down_one_grad: float32 [3072, 768], P('head')
- qkv_two_grad: float32 [3, 768, 768], P(None, None, 'head')
- out_two_grad: float32 [768, 768], P('head')
- expert_up_grad: float32 [16, 768, 3072], P('dp', None, 'head')
- expert_down_grad: float32 [16, 3072, 768], P('dp', 'head')
- centroids_grad: float32 [16, 768], P('dp')
The draws below stay inside these ranges and needn't reach their ends.
Inputs may be any that keep to these rules, and one draw needn't show every extreme that they name: `segment_ids`: within each 1024-token row the ids start at 0 and rise by one at each of 7 document starts; no document starts at positions 385 to 640. `routes`: in each aligned block of 512 rows (the rows of one device) no expert is named by more than 64 rows, a bound that some block reaches; every expert is named somewhere.
All inputs are finite; a program needn't handle non-finite values.
Results may differ from the reference program's by a relative error of at most 0.025.
Values may be sent and summed in bfloat16 or wider, within the bound.
No kernel may reach another device: no remote copies, remote signals or barrier semaphores. Data moves between devices by JAX's collectives and lax.ppermute only.
A program may use at most 256 MiB of HBM per device.

```python
import math
import jax
import jax.numpy as jnp
import numpy as np
from jax import lax

D = 768
HEADS = 12
HEAD_DIM = 64
FF = 3072
HDIM = 768
EXPERTS = 16
TOK_DEV = 512
LEN = 1024
TOKENS = 16384
CAP = 64
DOCS = 8


def draw_segment_ids(key, part):
    row_total = TOKENS // LEN
    row_keys = jax.random.split(key, row_total)
    position = jnp.arange(LEN, dtype=jnp.int32)
    lower_edge = LEN // 2 - LEN // 8
    upper_edge = LEN // 2 + LEN // 8
    allowed = (position > 0) & ((position <= lower_edge) | (position > upper_edge))

    def one_row(row_key):
        priority = jax.random.permutation(row_key, LEN).astype(jnp.int32)
        scored = jnp.where(allowed, priority + LEN, priority)
        starts = lax.top_k(scored, DOCS - 1)[1].astype(jnp.int32)
        return jnp.sum((position[:, None] >= starts[None, :]).astype(jnp.int32), axis=1)
    return jax.vmap(one_row)(row_keys).reshape(TOKENS).astype(jnp.int32)


def block_levels(stream_key, extent, cuts, low, high):
    def one(axis_at, shards_of):
        steps = jax.random.uniform(jax.random.fold_in(jax.random.fold_in(stream_key, 6), axis_at), (shards_of,), jnp.float32, low / len(cuts), high / len(cuts))
        return jnp.repeat(jnp.exp(steps), extent[axis_at] // shards_of).reshape((-1,) + (1,) * (len(extent) - axis_at - 1))

    factor_of = one(*cuts[0])
    for cut in cuts[1:]:
        factor_of = factor_of * one(*cut)
    return factor_of


def deal_out(key, own, number, rows, amount, top, bound, skew):
    ranking = jax.random.permutation(key, amount)
    heavy_load, common = shares(amount, rows * top, bound, skew, True), shares(amount, rows * top, bound, skew, False)
    places = jnp.arange(amount)

    def named(sizes, rotation):
        used = int((sizes > 0).sum())
        fixed = max(1, used // 4)
        moved = fixed + (places - fixed + rotation * (used - fixed)) % max(1, amount - fixed)
        return jnp.zeros((amount,), jnp.int32).at[ranking[jnp.where(places < fixed, places, moved)]].set(jnp.asarray(sizes, jnp.int32))

    sizes = jnp.where(number % 4 == 0, named(heavy_load, number // 4), named(common, number - number // 4 - 1))
    mixed = jax.random.permutation(jax.random.fold_in(own, 3), amount)
    source_of, taker = mixed[0:amount // 2 * 2:2], mixed[1:amount // 2 * 2:2]
    margin = jnp.minimum(sizes[source_of] - 1, bound - sizes[taker]) // 2
    margin = jnp.where((source_of == ranking[0]) | (taker == ranking[0]) | (sizes[taker] == 0), 0, jnp.maximum(margin, 0))
    moved = jax.random.randint(jax.random.fold_in(own, 4), (amount // 2,), 0, 1 << 20) % (margin + 1)
    sizes = sizes.at[source_of].add(-moved).at[taker].add(moved)
    labels = jnp.searchsorted(jnp.cumsum(sizes), jnp.arange(rows * top), side="right").astype(jnp.int32)
    table = labels.reshape(top, rows).T
    table = table[jax.random.permutation(jax.random.fold_in(own, 1), rows)]
    rotation = jax.random.randint(jax.random.fold_in(own, 2), (rows, 1), 0, top)
    return jnp.take_along_axis(table, (jnp.arange(top)[None, :] + rotation) % top, axis=1)


def shares(amount, total, bound, skew, full):
    weights = [(1 << 20) // math.isqrt(standing ** skew) + 1 for standing in range(1, amount + 1)]
    largest = bound if full else min(bound, max(-(-total // amount), total * weights[0] // sum(weights)))
    least = 1 if total - largest >= amount - 1 else 0
    counts, spare = [largest] + [least] * (amount - 1), total - largest - least * (amount - 1)
    while spare > 0:
        candidates = [i for i in range(1, amount) if counts[i] < largest] or [i for i in range(1, amount) if counts[i] < bound]
        pool, remaining = sum([weights[i] for i in candidates]), spare
        for i in candidates:
            more = min(bound - counts[i], max(1, remaining * weights[i] // pool), spare)
            counts[i] = counts[i] + more
            spare = spare - more
    return np.array(counts)


def scatter_about(key, extent, width, limit, cuts=(), kind=jnp.bfloat16):
    drawn = jax.random.normal(key, extent, jnp.float32) * width
    if len(cuts) > 0:
        drawn = block_levels(key, extent, cuts, -0.22, 0.18) * drawn
    return jnp.clip(drawn, min=-limit, max=limit).astype(kind)


def setup_inputs(seed: int = 0) -> dict:
    keys = jax.random.split(jax.random.key(seed), 15)
    tokens = scatter_about(keys[0], (TOKENS, D), 1.0, 6.0, ((0, 32),))
    segment_ids = draw_segment_ids(jax.random.fold_in(keys[14], 71), 0)
    routes_keys = jax.random.split(jax.random.fold_in(keys[2], 1), TOKENS // TOK_DEV)
    routes_turns = jax.random.permutation(jax.random.fold_in(keys[2], 3), TOKENS // TOK_DEV)
    routes = jax.vmap(lambda own, number: deal_out(jax.random.fold_in(keys[2], 2), own, number, TOK_DEV, EXPERTS, 1, CAP, 1))(routes_keys, routes_turns).reshape((TOKENS, 1))
    norm_gains = jnp.clip(1.0 + 0.1 * jax.random.normal(keys[3], (4, D), jnp.float32), 0.5, 1.5).astype(jnp.bfloat16)
    qkv_one = scatter_about(keys[4], (3, D, HDIM), D ** -0.5, 0.21875, ((2, 2),))
    out_one = scatter_about(keys[5], (HDIM, D), (HDIM // 8) ** -0.5, 0.625, ((0, 2),))
    up_one = scatter_about(keys[6], (D, FF), D ** -0.5, 0.21875, ((1, 2),))
    down_one = scatter_about(keys[7], (FF, D), (FF // 4) ** -0.5, 0.21875, ((0, 2),))
    qkv_two = scatter_about(keys[8], (3, D, HDIM), D ** -0.5, 0.21875, ((2, 2),))
    out_two = scatter_about(keys[9], (HDIM, D), (HDIM // 8) ** -0.5, 0.625, ((0, 2),))
    expert_up = scatter_about(keys[10], (EXPERTS, D, FF), D ** -0.5, 0.21875, ((0, 16), (2, 2)))
    expert_down = scatter_about(keys[11], (EXPERTS, FF, D), (FF // 4) ** -0.5, 0.21875, ((0, 16), (1, 2)))
    centroids = scatter_about(keys[12], (EXPERTS, D), (2 * D) ** -0.5, 0.15625, ((0, 16),))
    cotangent = scatter_about(keys[13], (TOKENS, D), 1.0, 6.0, ((0, 32),))
    return dict(tokens=tokens, segment_ids=segment_ids, routes=routes, norm_gains=norm_gains, qkv_one=qkv_one, out_one=out_one, up_one=up_one, down_one=down_one, qkv_two=qkv_two, out_two=out_two, expert_up=expert_up, expert_down=expert_down, centroids=centroids, cotangent=cotangent)


@jax.custom_vjp
def low(v):
    return lax.optimization_barrier(v.astype(jnp.bfloat16)).astype(jnp.float32)

@jax.custom_vjp
def low_back(v):
    return v

def low_keep(v):
    return (low(v), None)

def low_pass(kept, grad):
    return (grad,)

def back_keep(v):
    return (v, None)

def back_low(kept, grad):
    return (low(grad),)
low.defvjp(low_keep, low_pass)
low_back.defvjp(back_keep, back_low)
highest = lax.Precision.HIGHEST
norm_epsilon = 1e-05
masked_score = -1e+30

def layer_norm(residual, gain_row):
    centered = residual - lax.optimization_barrier(jnp.mean(residual, axis=-1, keepdims=True))
    variance = lax.optimization_barrier(jnp.mean(centered * centered, axis=-1, keepdims=True))
    return centered * lax.rsqrt(variance + norm_epsilon) * gain_row

def attend(pieces):
    queries, key_rows, value_rows, segments = pieces
    raw_scores = jnp.einsum('qhd,khd->hqk', queries, key_rows, precision=highest)
    scores = low_back(raw_scores * (1.0 / math.sqrt(HEAD_DIM)))
    position = jnp.arange(LEN, dtype=jnp.int32)
    allowed = (position[None, :] <= position[:, None]) & (segments[None, :] == segments[:, None])
    scores = jnp.where(allowed[None], scores, masked_score)
    row_max = lax.optimization_barrier(jnp.max(scores, axis=-1, keepdims=True))
    weights = jnp.exp(scores - row_max)
    weights = weights / lax.optimization_barrier(jnp.sum(weights, axis=-1, keepdims=True))
    return jnp.einsum('hqk,khd->qhd', low(weights), value_rows, precision=highest)

def attention_block(residual, gain_row, qkv_weight, out_weight, segment_ids):
    normed = low(layer_norm(residual, gain_row))
    projected = low_back(low(jnp.einsum('td,cde->cte', normed, qkv_weight, precision=highest)))
    row_total = residual.shape[0] // LEN
    shaped = projected.reshape(3, row_total, LEN, HEADS, HEAD_DIM)
    mixture = lax.map(jax.checkpoint(attend), (shaped[0], shaped[1], shaped[2], segment_ids.reshape(row_total, LEN)))
    mixture = low_back(low(mixture.reshape(residual.shape[0], HEADS * HEAD_DIM)))
    branch = low_back(jnp.dot(mixture, out_weight, precision=highest))
    return residual + branch

def dense_block(residual, gain_row, up_weight, down_weight):
    normed = low(layer_norm(residual, gain_row))
    hidden = low_back(jnp.dot(normed, up_weight, precision=highest))
    active = low(jax.nn.gelu(hidden, approximate=False))
    branch = low_back(jnp.dot(active, down_weight, precision=highest))
    return residual + branch

def expert_slots(routes):
    chosen = routes[:, 0]
    blocks = chosen.reshape(-1, TOK_DEV)
    matches = (blocks[:, :, None] == jnp.arange(EXPERTS, dtype=jnp.int32)[None, None, :]).astype(jnp.int32)
    before = jnp.cumsum(matches, axis=1) - matches
    slot_rank = lax.optimization_barrier(jnp.sum(before * matches, axis=2))
    block_number = jnp.arange(blocks.shape[0], dtype=jnp.int32)[:, None]
    flat_slots = blocks * (blocks.shape[0] * CAP) + block_number * CAP + slot_rank
    return flat_slots.reshape(-1).astype(jnp.int32)

def expert_block(residual, gain_row, flat_slots, centroid_rows, up_weight, down_weight):
    normed = low(layer_norm(residual, gain_row))
    per_expert = residual.shape[0] // TOK_DEV * CAP
    buffer = jnp.zeros((EXPERTS * per_expert, D), jnp.float32).at[flat_slots].set(normed)
    buffer = buffer.reshape(EXPERTS, per_expert, D)
    scores = jnp.einsum('esd,ed->es', buffer, centroid_rows, precision=highest)
    gating = jax.nn.sigmoid(scores)
    hidden = low_back(jnp.einsum('esd,edf->esf', buffer, up_weight, precision=highest))
    active = low(jax.nn.gelu(hidden, approximate=False))
    output = low_back(jnp.einsum('esf,efd->esd', active, down_weight, precision=highest))
    branch = low_back(gating[:, :, None] * output)
    return residual + branch.reshape(EXPERTS * per_expert, D)[flat_slots]

def reference(tokens, segment_ids, routes, norm_gains, qkv_one, out_one, up_one, down_one, qkv_two, out_two, expert_up, expert_down, centroids, cotangent):
    flat_slots = expert_slots(routes)

    def forward(residual, gain_rows, qkv_first, out_first, up_first, down_first, qkv_second, out_second, upward, downward, centroid_rows):
        first = attention_block(residual, gain_rows[0], qkv_first, out_first, segment_ids)
        first = dense_block(first, gain_rows[1], up_first, down_first)
        second = attention_block(first, gain_rows[2], qkv_second, out_second, segment_ids)
        second = expert_block(second, gain_rows[3], flat_slots, centroid_rows, upward, downward)
        return (second, first)
    primals = [value.astype(jnp.float32) for value in (tokens, norm_gains, qkv_one, out_one, up_one, down_one, qkv_two, out_two, expert_up, expert_down, centroids)]
    second, pullback, first = jax.vjp(forward, *primals, has_aux=True)
    grads = pullback(cotangent.astype(jnp.float32))
    return (first.astype(jnp.bfloat16), second.astype(jnp.bfloat16), grads[0], grads[1], grads[2], grads[3], grads[4], grads[5], grads[6], grads[7], grads[8], grads[9], grads[10])
```

```python
import functools

import jax
import jax.numpy as jnp
from jax import lax
from jax.experimental import pallas as pl
from jax.experimental.pallas import tpu as pltpu
from jax.sharding import PartitionSpec as P

BF = jnp.bfloat16
F32 = jnp.float32
EPS = 1e-05
MASKED = -1e30
BLK = 256
HEAD_DIM = 64
SWAP = [(0, 1), (1, 0)]
VLIM = 56 * 1024 * 1024


def mm(a, b):
    return lax.dot_general(a, b, (((1,), (0,)), ((), ())), preferred_element_type=F32)


def mm_nt(a, b):
    return lax.dot_general(a, b, (((1,), (1,)), ((), ())), preferred_element_type=F32)


def mm_tn(a, b):
    return lax.dot_general(a, b, (((0,), (0,)), ((), ())), preferred_element_type=F32)


def norm_stats(x):
    c = x - jnp.mean(x, axis=-1, keepdims=True)
    r = lax.rsqrt(jnp.mean(c * c, axis=-1, keepdims=True) + EPS)
    return c * r, r


def norm_back(x, gain, dn):
    xh, r = norm_stats(x)
    dxh = dn * gain
    a = jnp.mean(dxh, axis=-1, keepdims=True)
    b = jnp.mean(dxh * xh, axis=-1, keepdims=True)
    return r * (dxh - a - xh * b), jnp.sum(dn * xh, axis=0, keepdims=True)


def gelu_pair(u):
    z = jnp.abs(u) * 0.7071067811865476
    t = 1.0 / (1.0 + 0.3275911 * z)
    ex = jnp.exp(-(z * z))
    poly = t * (
        0.254829592
        + t * (-0.284496736 + t * (1.421413741 + t * (-1.453152027 + t * 1.061405429)))
    )
    tail = 0.5 * poly * ex
    phi = jnp.where(u >= 0.0, 1.0 - tail, tail)
    return u * phi, phi + u * (ex * 0.3989422804014327)


def mask_bias(segc, segr, b, keys):
    row = lax.broadcasted_iota(jnp.int32, (BLK, keys), 0) + b * BLK
    col = lax.broadcasted_iota(jnp.int32, (BLK, keys), 1)
    return jnp.where((segc == segr[:, :keys]) & (col <= row), 0.0, MASKED)


def half_lane(hh):
    lane = lax.broadcasted_iota(jnp.int32, (BLK, 128), 1)
    return (lane >= 64) if hh else (lane < 64)


def attn_fwd_kernel(blocks, split, h_ref, *refs):
    if split:
        own, peer, g, wqkv, wo, segc, segr = refs[:7]
        outs = refs[7:]
    else:
        xr, pa, pb, g, wqkv, wo, segc, segr = refs[:8]
        outs = refs[8:]
    x_out, n_out, qkv_out, o_out, lse_out, p_out, ks, vs = outs
    i = pl.program_id(0)
    if split:
        mine = (i // (blocks // 2)) == h_ref[0]
        x = jnp.where(mine, own[...].astype(F32), peer[...].astype(F32))
    else:
        x = xr[...] + pa[...].astype(F32) + pb[...].astype(F32)
    x_out[...] = x
    xh, _ = norm_stats(x)
    n = (xh * g[...]).astype(BF)
    n_out[...] = n
    q = (mm(n, wqkv[0]).astype(BF).astype(F32) * 0.125).astype(BF)
    k = mm(n, wqkv[1]).astype(BF)
    v = mm(n, wqkv[2]).astype(BF)
    qkv_out[0] = q
    qkv_out[1] = k
    qkv_out[2] = v
    rows = pl.ds(pl.multiple_of(i * BLK, BLK), BLK)
    ks[rows, :] = k
    vs[rows, :] = v
    pairs = q.shape[1] // 128
    for b in range(blocks):

        @pl.when(i == b)
        def _(b=b):
            keys = BLK * (b + 1)
            bias = mask_bias(segc[...], segr[...], b, keys)
            lse = jnp.zeros((BLK, 128), F32)
            lanes = lax.broadcasted_iota(jnp.int32, (BLK, 128), 1)
            total = jnp.zeros((BLK, wo.shape[1]), F32)
            for pr in range(pairs):
                cols = slice(pr * 128, pr * 128 + 128)
                qp = qkv_out[0, :, cols]
                kp = ks[0:keys, cols]
                vp = vs[0:keys, cols]
                res = []
                for hh in range(2):
                    qh = jnp.where(half_lane(hh), qp, jnp.zeros_like(qp))
                    s = mm_nt(qh, kp) + bias
                    m = jnp.max(s, axis=-1, keepdims=True)
                    e = jnp.exp(s - m)
                    l = jnp.sum(e, axis=-1, keepdims=True)
                    res.append(mm(e.astype(BF), vp) * (1.0 / l))
                    lse = jnp.where(lanes == pr * 2 + hh, m + jnp.log(l), lse)
                ob = jnp.where(half_lane(0), res[0], res[1]).astype(BF)
                o_out[:, cols] = ob
                total = total + mm(ob, wo[cols, :])
            lse_out[...] = lse
            p_out[...] = total.astype(BF)


def attn_bwd_kernel(blocks, split, h_ref, *refs):
    if split:
        dro, drp, dno, dnp_ = refs[:4]
    else:
        drr, dna, dnb = refs[:3]
    rest = refs[4 if split else 3 :]
    xn, gn, qr, kf, vf, orf, lser, wqkv, wo, segc, segr = rest[:11]
    dr_out, da_out, dqkv_out, dn_out, dg_out, dks, dvs = rest[11:]
    i = pl.program_id(0)
    blk = blocks - 1 - i
    if split:
        mine = (blk // (blocks // 2)) == h_ref[0]
        dr = jnp.where(mine, dro[...].astype(F32), drp[...].astype(F32))
        dn = jnp.where(mine, dno[...].astype(F32), dnp_[...].astype(F32))
    else:
        dr = drr[...]
        dn = dna[...].astype(F32) + dnb[...].astype(F32)
    dx, dg = norm_back(xn[...], gn[...], dn)
    dr = dr + dx
    dr_out[...] = dr
    da = dr.astype(BF)
    da_out[...] = da

    @pl.when(i == 0)
    def _():
        dks[...] = jnp.zeros_like(dks)
        dvs[...] = jnp.zeros_like(dvs)
        dg_out[...] = jnp.zeros_like(dg_out)

    dg_out[...] += jnp.broadcast_to(dg, dg_out.shape)
    do = mm_nt(da, wo[...]).astype(BF)
    pairs = wo.shape[0] // 128
    for b in range(blocks):

        @pl.when(blk == b)
        def _(b=b):
            keys = BLK * (b + 1)
            here = slice(b * BLK, b * BLK + BLK)
            bias = mask_bias(segc[...], segr[...], b, keys)
            lse = lser[...]
            for pr in range(pairs):
                cols = slice(pr * 128, pr * 128 + 128)
                qp = qr[0, :, cols]
                kp = kf[0, 0:keys, cols]
                vp = vf[0, 0:keys, cols]
                dop = do[:, cols]
                prod = dop.astype(F32) * orf[:, cols].astype(F32)
                dqs, dss, ps, qs, dos = [], [], [], [], []
                for hh in range(2):
                    hm = half_lane(hh)
                    qh = jnp.where(hm, qp, jnp.zeros_like(qp))
                    doh = jnp.where(hm, dop, jnp.zeros_like(dop))
                    delta = jnp.sum(jnp.where(hm, prod, 0.0), axis=-1, keepdims=True)
                    h = pr * 2 + hh
                    p = jnp.exp(mm_nt(qh, kp) + bias - lse[:, h : h + 1])
                    dp = mm_nt(doh, vp)
                    ds = (p * (dp - delta)).astype(BF)
                    dqs.append(mm(ds, kp))
                    dks[0:keys, cols] += mm_tn(ds, qh)
                    dvs[0:keys, cols] += mm_tn(p.astype(BF), doh)
                dq = jnp.where(half_lane(0), dqs[0], dqs[1]) * 0.125
                dqkv_out[0, :, cols] = dq.astype(BF)
            dqkv_out[1] = dks[here, :].astype(BF)
            dqkv_out[2] = dvs[here, :].astype(BF)

    dn_out[...] = (
        mm_nt(dqkv_out[0], wqkv[0]) + mm_nt(dqkv_out[1], wqkv[1]) + mm_nt(dqkv_out[2], wqkv[2])
    ).astype(BF)


def dense_fwd_kernel(xr, pa, pb, g, up, down, x_out, n_out, act_out, gp_out, p_out):
    x = xr[...] + pa[...].astype(F32) + pb[...].astype(F32)
    x_out[...] = x
    xh, _ = norm_stats(x)
    n = (xh * g[...]).astype(BF)
    n_out[...] = n
    act, gp = gelu_pair(mm(n, up[...]))
    act = act.astype(BF)
    act_out[...] = act
    gp_out[...] = gp.astype(BF)
    p_out[...] = mm(act, down[...]).astype(BF)


def dense_bwd_kernel(drr, dna, dnb, xn, gn, gp, up, down, dr_out, df_out, du_out, dn_out, dg_out):
    dx, dg = norm_back(xn[...], gn[...], dna[...].astype(F32) + dnb[...].astype(F32))
    dr = drr[...] + dx
    dr_out[...] = dr
    df = dr.astype(BF)
    df_out[...] = df

    @pl.when(pl.program_id(0) == 0)
    def _():
        dg_out[...] = jnp.zeros_like(dg_out)

    dg_out[...] += jnp.broadcast_to(dg, dg_out.shape)
    du = (mm_nt(df, down[...]) * gp[...].astype(F32)).astype(BF)
    du_out[...] = du
    dn_out[...] = mm_nt(du, up[...]).astype(BF)


def final_kernel(h_ref, drr, dna, dnb, xo, xp, gn, dr_out, dg_out):
    i = pl.program_id(0)
    mine = i >= 2
    x = jnp.where(mine, xo[...].astype(F32), xp[...].astype(F32))
    dx, dg = norm_back(x, gn[...], dna[...].astype(F32) + dnb[...].astype(F32))
    dr_out[...] = drr[...] + dx

    @pl.when(i == 0)
    def _():
        dg_out[...] = jnp.zeros_like(dg_out)

    dg_out[...] += jnp.broadcast_to(dg, dg_out.shape)


def spread_kernel(rows_ref, slot_ref, out_ref):
    count = out_ref.shape[0]
    place = lax.broadcasted_iota(jnp.int32, (count, rows_ref.shape[0]), 0)
    place = place + pl.program_id(0) * count
    hot = (place == slot_ref[...]).astype(F32).astype(BF)
    out_ref[...] = mm(hot, rows_ref[...]).astype(BF)


def route_kernel(h_ref, xr, pa, pb, g, slot_ref, x_out, send_out, ms):
    i = pl.program_id(0)
    x = xr[...] + pa[...].astype(F32) + pb[...].astype(F32)
    x_out[...] = x

    @pl.when(i >= 2)
    def _():
        xh, _ = norm_stats(x)
        rows = pl.ds(pl.multiple_of((i - 2) * BLK, BLK), BLK)
        ms[rows, :] = (xh * g[...]).astype(BF)

    @pl.when(i == 3)
    def _():
        count = send_out.shape[0]
        place = lax.broadcasted_iota(jnp.int32, (count, ms.shape[0]), 0)
        hot = (place == slot_ref[...]).astype(F32).astype(BF)
        send_out[...] = mm(hot, ms[...]).astype(BF)


def collect_kernel(table, slot_ref, out_ref):
    count = table.shape[0]
    place = lax.broadcasted_iota(jnp.int32, (out_ref.shape[0], count), 1)
    hot = (place == slot_ref[...]).astype(F32).astype(BF)
    out_ref[...] = mm(hot, table[...]).astype(BF)


def collect_add_kernel(h_ref, table, slot_ref, x_ref, out_ref):
    count = table.shape[0]
    place = lax.broadcasted_iota(jnp.int32, (out_ref.shape[0], count), 1)
    hot = (place == slot_ref[...]).astype(F32).astype(BF)
    out_ref[...] = (x_ref[...] + mm(hot, table[...])).astype(BF)


def expert_kernel(
    half, mo, mp, go, gp_, cen, up, down,
    yo, yp, dmo, dmp, m_all, dy_all, ae_all, due_all, dc_out,
):
    i = pl.program_id(0)
    first = i < half
    m = jnp.where(first, mo[...], mp[...])
    gb = jnp.where(first, go[...], gp_[...]).astype(F32)
    mf = m.astype(F32)
    cf = cen[...].astype(F32)
    gate = jax.nn.sigmoid(jnp.sum(mf * cf, axis=-1, keepdims=True))
    act, gd = gelu_pair(mm(m, up[0]))
    act = act.astype(BF)
    y = mm(act, down[0])
    dscore = jnp.sum(gb * y, axis=-1, keepdims=True) * gate * (1.0 - gate)
    dy = (gate * gb).astype(BF)
    due = (mm_nt(dy, down[0]) * gd).astype(BF)
    dm = (mm_nt(due, up[0]) + dscore * cf).astype(BF)
    gy = (gate * y).astype(BF)
    m_all[...] = m
    dy_all[...] = dy
    ae_all[...] = act
    due_all[...] = due

    @pl.when(i == 0)
    def _():
        dc_out[...] = jnp.zeros_like(dc_out)

    dc_out[...] += jnp.broadcast_to(jnp.sum(dscore * mf, axis=0, keepdims=True), dc_out.shape)

    @pl.when(first)
    def _():
        yo[...] = gy
        dmo[...] = dm

    @pl.when(jnp.logical_not(first))
    def _():
        yp[...] = gy
        dmp[...] = dm


def shape(dims, kind):
    return jax.ShapeDtypeStruct(dims, kind)


def fixed(dims):
    zero = (0,) * len(dims)
    return pl.BlockSpec(dims, lambda *a: zero, pipeline_mode=pl.Buffered(1))


def rows_spec(width, index=lambda i: i):
    return pl.BlockSpec((BLK, width), lambda i, *a: (index(i), 0))


PARAMS = pltpu.CompilerParams(vmem_limit_bytes=VLIM, dimension_semantics=("arbitrary",))


def call(kernel, grid, in_specs, out_specs, outs, scratch, flops, moved, args, prefetch=None):
    cost = pl.CostEstimate(flops=int(flops), bytes_accessed=int(moved), transcendentals=0)
    if prefetch is None:
        spec = pl.GridSpec(
            grid=grid, in_specs=in_specs, out_specs=out_specs, scratch_shapes=scratch
        )
    else:
        spec = pltpu.PrefetchScalarGridSpec(
            num_scalar_prefetch=1,
            grid=grid,
            in_specs=in_specs,
            out_specs=out_specs,
            scratch_shapes=scratch,
        )
        args = (prefetch,) + tuple(args)
    return pl.pallas_call(
        kernel, grid_spec=spec, out_shape=outs, compiler_params=PARAMS, cost_estimate=cost
    )(*args)


def attention_forward(h, inputs, split, gain, wqkv, wo, segc, segr):
    length, d = segc.shape[0], wqkv.shape[1]
    c = wqkv.shape[2]
    blocks = length // BLK
    if split:
        ins = [rows_spec(d, lambda i: i % (blocks // 2))] * 2
    else:
        ins = [rows_spec(d)] * 3
    ins += [
        fixed((1, d)),
        fixed((3, d, c)),
        fixed((c, d)),
        pl.BlockSpec((BLK, 1), lambda i, *a: (i, 0)),
        fixed((1, length)),
    ]
    outs = [
        (rows_spec(d), shape((length, d), F32)),
        (rows_spec(d), shape((length, d), BF)),
        (pl.BlockSpec((3, BLK, c), lambda i, *a: (0, i, 0)), shape((3, length, c), BF)),
        (rows_spec(c), shape((length, c), BF)),
        (rows_spec(128), shape((length, 128), F32)),
        (rows_spec(d), shape((length, d), BF)),
    ]
    scratch = [pltpu.VMEM((length, c), BF), pltpu.VMEM((length, c), BF)]
    flops = 2 * length * d * c * 4 + 4 * length * length * c
    return call(
        functools.partial(attn_fwd_kernel, blocks, split),
        (blocks,),
        ins,
        [o[0] for o in outs],
        [o[1] for o in outs],
        scratch,
        flops * 2,
        length * d * 20,
        (*inputs, gain, wqkv, wo, segc, segr),
        prefetch=h,
    )


def attention_backward(h, inputs, split, xn, gn, saved, wqkv, wo, segc, segr):
    qkv, o, lse = saved
    length, d = segc.shape[0], wqkv.shape[1]
    c = wqkv.shape[2]
    blocks = length // BLK
    back = lambda i: blocks - 1 - i
    if split:
        ins = [rows_spec(d, lambda i: back(i) % (blocks // 2))] * 4
    else:
        ins = [rows_spec(d, back)] * 3
    part = lambda n: pl.BlockSpec(
        (1, length, c), lambda i, *a: (n, 0, 0), pipeline_mode=pl.Buffered(1)
    )
    ins += [
        rows_spec(d, back),
        fixed((1, d)),
        pl.BlockSpec((1, BLK, c), lambda i, *a: (0, back(i), 0)),
        part(1),
        part(2),
        rows_spec(c, back),
        rows_spec(128, back),
        fixed((3, d, c)),
        fixed((c, d)),
        pl.BlockSpec((BLK, 1), lambda i, *a: (back(i), 0)),
        fixed((1, length)),
    ]
    outs = [
        (rows_spec(d, back), shape((length, d), F32)),
        (rows_spec(d, back), shape((length, d), BF)),
        (pl.BlockSpec((3, BLK, c), lambda i, *a: (0, back(i), 0)), shape((3, length, c), BF)),
        (rows_spec(d, back), shape((length, d), BF)),
        (fixed((8, d)), shape((8, d), F32)),
    ]
    scratch = [pltpu.VMEM((length, c), F32), pltpu.VMEM((length, c), F32)]
    flops = 2 * length * d * c * 4 + 10 * length * length * c
    return call(
        functools.partial(attn_bwd_kernel, blocks, split),
        (blocks,),
        ins,
        [s[0] for s in outs],
        [s[1] for s in outs],
        scratch,
        flops * 2,
        length * d * 20,
        (*inputs, xn, gn, qkv, qkv, qkv, o, lse, wqkv, wo, segc, segr),
        prefetch=h,
    )


def dense_forward(x, pa, pb, gain, up, down):
    length, d = x.shape
    f = up.shape[1]
    return call(
        dense_fwd_kernel,
        (length // BLK,),
        [rows_spec(d)] * 3 + [fixed((1, d)), fixed((d, f)), fixed((f, d))],
        [rows_spec(d), rows_spec(d), rows_spec(f), rows_spec(f), rows_spec(d)],
        [
            shape((length, d), F32),
            shape((length, d), BF),
            shape((length, f), BF),
            shape((length, f), BF),
            shape((length, d), BF),
        ],
        [],
        4 * length * d * f,
        length * d * 20 + 4 * d * f,
        (x, pa, pb, gain, up, down),
    )


def dense_backward(dr, dna, dnb, xn, gn, gp, up, down):
    length, d = dr.shape
    f = up.shape[1]
    return call(
        dense_bwd_kernel,
        (length // BLK,),
        [rows_spec(d)] * 4
        + [fixed((1, d)), rows_spec(f), fixed((d, f)), fixed((f, d))],
        [rows_spec(d), rows_spec(d), rows_spec(f), rows_spec(d), fixed((8, d))],
        [
            shape((length, d), F32),
            shape((length, d), BF),
            shape((length, f), BF),
            shape((length, d), BF),
            shape((8, d), F32),
        ],
        [],
        4 * length * d * f,
        length * d * 20 + 4 * d * f,
        (dr, dna, dnb, xn, gn, gp, up, down),
    )


def own_last(blocks):
    return lambda i, h: lax.rem(i + (blocks // 2) * (1 - h[0]), blocks)


def final_step(h, dr, dna, dnb, xo, xp, gn):
    length, d = dr.shape
    blocks = length // BLK
    place = own_last(blocks)
    spec = pl.BlockSpec((BLK, d), lambda i, h: (place(i, h), 0))
    late = lambda i, h: (jnp.maximum(i - blocks // 2, 0), 0)
    return call(
        final_kernel,
        (blocks,),
        [spec] * 3
        + [pl.BlockSpec((BLK, d), late)]
        + [pl.BlockSpec((BLK, d), lambda i, h: (lax.rem(i, blocks // 2), 0)), fixed((1, d))],
        [pl.BlockSpec((BLK, d), late), fixed((8, d))],
        [shape((length // 2, d), F32), shape((8, d), F32)],
        [],
        length * d * 40,
        length * d * 14,
        (dr, dna, dnb, xo, xp, gn),
        prefetch=h,
    )


def route_step(h, x, pa, pb, gain, slot_row, slots):
    length, d = x.shape
    blocks = length // BLK
    place = own_last(blocks)
    spec = pl.BlockSpec((BLK, d), lambda i, h: (place(i, h), 0))
    return call(
        route_kernel,
        (blocks,),
        [spec] * 3 + [fixed((1, d)), fixed((1, length // 2))],
        [spec, fixed((slots, d))],
        [shape((length, d), F32), shape((slots, d), BF)],
        [pltpu.VMEM((length // 2, d), BF)],
        length * slots * d,
        length * d * 14,
        (x, pa, pb, gain, slot_row),
        prefetch=h,
    )


def spread(rows, slot_row, slots):
    count, d = rows.shape
    return call(
        spread_kernel,
        (slots // BLK,),
        [fixed((count, d)), fixed((1, count))],
        [rows_spec(d)],
        [shape((slots, d), BF)],
        [],
        2 * count * slots * d,
        4 * slots * d,
        (rows, slot_row),
    )[0]


def collect(table, slot_col):
    slots, d = table.shape
    count = slot_col.shape[0]
    return call(
        collect_kernel,
        (count // BLK,),
        [fixed((slots, d)), pl.BlockSpec((BLK, 1), lambda i, *a: (i, 0))],
        [rows_spec(d)],
        [shape((count, d), BF)],
        [],
        2 * count * slots * d,
        4 * slots * d,
        (table, slot_col),
    )[0]


def collect_add(h, table, slot_col, x):
    slots, d = table.shape
    count = slot_col.shape[0]
    per = count // BLK
    return call(
        collect_add_kernel,
        (per,),
        [
            fixed((slots, d)),
            pl.BlockSpec((BLK, 1), lambda i, *a: (i, 0)),
            pl.BlockSpec((BLK, d), lambda i, h: (h[0] * per + i, 0)),
        ],
        [rows_spec(d)],
        [shape((count, d), BF)],
        [],
        2 * count * slots * d,
        8 * slots * d,
        (table, slot_col, x),
        prefetch=h,
    )[0]


def expert_step(mo, mp, go, gp, cen, up, down):
    rows, d = mo.shape
    f = up.shape[2]
    half = rows // BLK
    lo = lambda i: jnp.minimum(i, half - 1)
    hi = lambda i: jnp.maximum(i - half, 0)
    return call(
        functools.partial(expert_kernel, half),
        (2 * half,),
        [rows_spec(d, lo), rows_spec(d, hi), rows_spec(d, lo), rows_spec(d, hi)]
        + [fixed((1, d)), fixed((1, d, f)), fixed((1, f, d))],
        [rows_spec(d, lo), rows_spec(d, hi), rows_spec(d, lo), rows_spec(d, hi)]
        + [rows_spec(d), rows_spec(d), rows_spec(f), rows_spec(f), fixed((8, d))],
        [shape((rows, d), BF)] * 4
        + [shape((2 * rows, d), BF)] * 2
        + [shape((2 * rows, f), BF)] * 2
        + [shape((8, d), F32)],
        [],
        16 * rows * d * f,
        rows * d * 24 + rows * f * 8,
        (mo, mp, go, gp, cen, up, down),
    )


def slot_index(chosen, capacity, experts):
    rows = chosen.shape[0]
    matches = chosen[:, None] == jnp.arange(experts, dtype=jnp.int32)[None, :]
    position = jnp.arange(rows, dtype=jnp.int32)
    earlier = (position[None, :] < position[:, None]).astype(BF)
    before = jnp.dot(earlier, matches.astype(BF), preferred_element_type=F32)
    rank = jnp.sum(jnp.where(matches, before, 0.0), axis=1).astype(jnp.int32)
    return chosen * capacity + rank


def swap(v):
    return lax.ppermute(v, "head", SWAP)


def exchange_half(v, bit, pairs):
    half = v.shape[0] // 2
    out = lax.dynamic_slice_in_dim(v, (1 - bit) * half, half, 0)
    return lax.dynamic_slice_in_dim(v, bit * half, half, 0) + lax.ppermute(out, "dp", pairs)


def regather(v, bit, pairs):
    other = lax.ppermute(v, "dp", pairs)
    both = jnp.concatenate([v, v], axis=0)
    return lax.dynamic_update_slice_in_dim(both, other, (1 - bit) * v.shape[0], 0)


def reduce_all(v, steps):
    if steps is None:
        return lax.psum(v, "dp")
    me = lax.axis_index("dp")
    half = v.shape[0] // 2
    pairs = {s: [(i, i ^ s) for i in range(16)] for s in (1, 2, 4, 8)}
    bits = {s: (me // s) % 2 for s in (1, 2, 4, 8)}
    a, b = v[:half], v[half:]
    a, b = exchange_half(a, bits[1], pairs[1]), exchange_half(b, bits[2], pairs[2])
    a, b = exchange_half(a, bits[2], pairs[2]), exchange_half(b, bits[1], pairs[1])
    c = jnp.concatenate([a, b], axis=0)
    c = exchange_half(c, bits[4], pairs[4])
    c = exchange_half(c, bits[8], pairs[8])
    c = regather(c, bits[8], pairs[8])
    c = regather(c, bits[4], pairs[4])
    quarter = c.shape[0] // 2
    a, b = c[:quarter], c[quarter:]
    a, b = regather(a, bits[2], pairs[2]), regather(b, bits[1], pairs[1])
    a, b = regather(a, bits[1], pairs[1]), regather(b, bits[2], pairs[2])
    return jnp.concatenate([a, b], axis=0)


def body(
    steps,
    tokens,
    segment_ids,
    routes,
    norm_gains,
    qkv_one,
    out_one,
    up_one,
    down_one,
    qkv_two,
    out_two,
    expert_up,
    expert_down,
    centroids,
    cotangent,
):
    count, d = tokens.shape
    side = lax.axis_index("head")
    h = side.astype(jnp.int32).reshape(1)
    experts = lax.axis_size("dp") * expert_up.shape[0]
    capacity = 2 * count // experts
    slots = experts * capacity
    gains = norm_gains.astype(F32)
    gain = [gains[j : j + 1] for j in range(4)]
    segc, segr = segment_ids[:, None], segment_ids[None, :]

    chosen = lax.dynamic_slice_in_dim(routes[:, 0], side * count, count, 0)
    flat = slot_index(chosen, capacity, experts)
    slot_row, slot_col = flat[None, :], flat[:, None]

    def travel(v):
        box = v.reshape(experts, capacity, d)
        return lax.all_to_all(box, "dp", 0, 0, tiled=True).reshape(slots, d)

    tokens_peer = swap(tokens)
    x0, n1, qkv1, o1, lse1, p1 = attention_forward(
        h, (tokens, tokens_peer), True, gain[0], qkv_one, out_one, segc, segr
    )
    p1r = swap(p1)
    cot_peer = swap(cotangent)
    grad_own = travel(spread(cotangent, slot_row, slots))
    grad_peer = swap(grad_own)
    x1, n2, act, gp, p2 = dense_forward(x0, p1, p1r, gain[1], up_one, down_one)
    p2r = swap(p2)
    first, n3, qkv2, o2, lse2, p3 = attention_forward(
        h, (x1, p2, p2r), False, gain[2], qkv_two, out_two, segc, segr
    )
    p3r = swap(p3)
    x2, sent = route_step(h, first, p3, p3r, gain[3], slot_row, slots)
    m_own = travel(sent)
    m_peer = swap(m_own)
    yo, yp, dmo, dmp, m_all, dy_all, ae_all, due_all, dc = expert_step(
        m_own, m_peer, grad_own, grad_peer, centroids, expert_up, expert_down
    )
    dm_sum = (dmo.astype(F32) + swap(dmp).astype(F32)).astype(BF)
    dm_own = collect(travel(dm_sum), slot_col)
    dm_peer = swap(dm_own)
    up_grad = mm_tn(m_all, due_all)[None]
    down_grad = mm_tn(ae_all, dy_all)[None]
    dc = dc[:1]
    cen_grad = dc + swap(dc)

    dr2, da2, dqkv2, dn2, dg3 = attention_backward(
        h,
        (cotangent, cot_peer, dm_own, dm_peer),
        True,
        x2,
        gain[3],
        (qkv2, o2, lse2),
        qkv_two,
        out_two,
        segc,
        segr,
    )
    dn2r = swap(dn2)

    def attention_grads(n, dqkv, o, da):
        w = [mm_tn(n, dqkv[j]).astype(BF) for j in range(3)]
        wo = mm_tn(o, da).astype(BF)
        c = wo.shape[0]
        return jnp.concatenate([*w, wo[:, :c], wo[:, c:]], axis=0)

    def split_grads(total):
        total = total.astype(F32)
        c = total.shape[1]
        wo = jnp.concatenate([total[3 * d : 3 * d + c], total[3 * d + c :]], axis=1)
        return total[: 3 * d].reshape(3, d, c), wo

    qkv_second, out_second = split_grads(reduce_all(attention_grads(n3, dqkv2, o2, da2), steps))
    y_sum = (yo.astype(F32) + swap(yp).astype(F32)).astype(BF)
    second = collect_add(h, travel(y_sum), slot_col, x2)

    dr1, df, du, dnd, dg2 = dense_backward(dr2, dn2, dn2r, first, gain[2], gp, up_one, down_one)
    dndr = swap(dnd)
    f = du.shape[1]
    w_up = mm_tn(n2, du).astype(BF)
    w_down = mm_tn(act, df).astype(BF)
    dense_total = jnp.concatenate([w_up[:, : f // 2], w_up[:, f // 2 :], w_down], axis=0)
    dense_total = reduce_all(dense_total, steps).astype(F32)
    up_first = jnp.concatenate([dense_total[:d], dense_total[d : 2 * d]], axis=1)
    down_first = dense_total[2 * d :]

    dr0, da1, dqkv1, dn1, dg1 = attention_backward(
        h,
        (dr1, dnd, dndr),
        False,
        x1,
        gain[1],
        (qkv1, o1, lse1),
        qkv_one,
        out_one,
        segc,
        segr,
    )
    dn1r = swap(dn1)
    input_grad, dg0 = final_step(h, dr0, dn1, dn1r, tokens, tokens_peer, gain[0])
    qkv_first, out_first = split_grads(reduce_all(attention_grads(n1, dqkv1, o1, da1), steps))
    gain_grads = jnp.concatenate([dg0[:1], dg1[:1], dg2[:1], dg3[:1]], axis=0)
    gain_grads = lax.psum(gain_grads, "dp")
    first_own = lax.dynamic_slice_in_dim(first, side * count, count, 0).astype(BF)
    return (
        first_own,
        second,
        input_grad,
        gain_grads,
        qkv_first,
        out_first,
        up_first,
        down_first,
        qkv_second,
        out_second,
        up_grad,
        down_grad,
        cen_grad,
    )


def solution(mesh):
    rows = P(("dp", "head"), None)
    shared = (
        P(None, None, "head"),
        P("head", None),
        P(None, "head"),
        P("head", None),
        P(None, None, "head"),
        P("head", None),
        P("dp", None, "head"),
        P("dp", "head", None),
        P("dp", None),
    )
    steps = 16 if mesh.shape["dp"] == 16 else None
    return jax.shard_map(
        functools.partial(body, steps),
        mesh=mesh,
        in_specs=(rows, P("dp"), P("dp", None), P(), *shared, rows),
        out_specs=(rows, rows, rows, P(), *shared),
        check_vma=False,
    )
```

```python
import functools

import jax
import jax.numpy as jnp
from jax import lax
from jax.experimental import pallas as pl
from jax.experimental.pallas import tpu as pltpu
from jax.sharding import PartitionSpec as P

BF = jnp.bfloat16
F32 = jnp.float32
EPS = 1e-05
MASKED = -1e30
BLK = 256
HEAD_DIM = 64
SWAP = [(0, 1), (1, 0)]
VLIM = 56 * 1024 * 1024


def mm(a, b):
    return lax.dot_general(a, b, (((1,), (0,)), ((), ())), preferred_element_type=F32)


def mm_nt(a, b):
    return lax.dot_general(a, b, (((1,), (1,)), ((), ())), preferred_element_type=F32)


def mm_tn(a, b):
    return lax.dot_general(a, b, (((0,), (0,)), ((), ())), preferred_element_type=F32)


def norm_stats(x):
    c = x - jnp.mean(x, axis=-1, keepdims=True)
    r = lax.rsqrt(jnp.mean(c * c, axis=-1, keepdims=True) + EPS)
    return c * r, r


def norm_back(x, gain, dn):
    xh, r = norm_stats(x)
    dxh = dn * gain
    a = jnp.mean(dxh, axis=-1, keepdims=True)
    b = jnp.mean(dxh * xh, axis=-1, keepdims=True)
    return r * (dxh - a - xh * b), jnp.sum(dn * xh, axis=0, keepdims=True)


def gelu_pair(u):
    z = jnp.abs(u) * 0.7071067811865476
    t = 1.0 / (1.0 + 0.3275911 * z)
    ex = jnp.exp(-(z * z))
    poly = t * (
        0.254829592
        + t * (-0.284496736 + t * (1.421413741 + t * (-1.453152027 + t * 1.061405429)))
    )
    tail = 0.5 * poly * ex
    phi = jnp.where(u >= 0.0, 1.0 - tail, tail)
    return u * phi, phi + u * (ex * 0.3989422804014327)


def mask_bias(segc, segr, b, keys):
    row = lax.broadcasted_iota(jnp.int32, (BLK, keys), 0) + b * BLK
    col = lax.broadcasted_iota(jnp.int32, (BLK, keys), 1)
    return jnp.where((segc == segr[:, :keys]) & (col <= row), 0.0, MASKED)


def half_lane(hh):
    lane = lax.broadcasted_iota(jnp.int32, (BLK, 128), 1)
    return (lane >= 64) if hh else (lane < 64)


def attn_fwd_kernel(blocks, split, h_ref, *refs):
    if split:
        own, peer, g, wqkv, wo, segc, segr = refs[:7]
        outs = refs[7:]
    else:
        xr, pa, pb, g, wqkv, wo, segc, segr = refs[:8]
        outs = refs[8:]
    x_out, n_out, qkv_out, o_out, lse_out, p_out, ks, vs = outs
    i = pl.program_id(0)
    if split:
        mine = (i // (blocks // 2)) == h_ref[0]
        x = jnp.where(mine, own[...].astype(F32), peer[...].astype(F32))
    else:
        x = xr[...] + (pa[...].astype(F32) + pb[...].astype(F32))
    x_out[...] = x
    xh, _ = norm_stats(x)
    n = (xh * g[...]).astype(BF)
    n_out[...] = n
    q = (mm(n, wqkv[0]).astype(BF).astype(F32) * 0.125).astype(BF)
    k = mm(n, wqkv[1]).astype(BF)
    v = mm(n, wqkv[2]).astype(BF)
    qkv_out[0] = q
    qkv_out[1] = k
    qkv_out[2] = v
    rows = pl.ds(pl.multiple_of(i * BLK, BLK), BLK)
    ks[rows, :] = k
    vs[rows, :] = v
    pairs = q.shape[1] // 128
    for b in range(blocks):

        @pl.when(i == b)
        def _(b=b):
            keys = BLK * (b + 1)
            bias = mask_bias(segc[...], segr[...], b, keys)
            lse = jnp.zeros((BLK, 128), F32)
            lanes = lax.broadcasted_iota(jnp.int32, (BLK, 128), 1)
            total = jnp.zeros((BLK, wo.shape[1]), F32)
            for pr in range(pairs):
                cols = slice(pr * 128, pr * 128 + 128)
                qp = qkv_out[0, :, cols]
                kp = ks[0:keys, cols]
                vp = vs[0:keys, cols]
                res = []
                for hh in range(2):
                    qh = jnp.where(half_lane(hh), qp, jnp.zeros_like(qp))
                    s = mm_nt(qh, kp) + bias
                    m = jnp.max(s, axis=-1, keepdims=True)
                    e = jnp.exp(s - m)
                    l = jnp.sum(e, axis=-1, keepdims=True)
                    res.append(mm(e.astype(BF), vp) * (1.0 / l))
                    lse = jnp.where(lanes == pr * 2 + hh, m + jnp.log(l), lse)
                ob = jnp.where(half_lane(0), res[0], res[1]).astype(BF)
                o_out[:, cols] = ob
                total = total + mm(ob, wo[cols, :])
            lse_out[...] = lse
            p_out[...] = total.astype(BF)


def attn_bwd_kernel(blocks, split, h_ref, *refs):
    if split:
        dro, drp, dno, dnp_ = refs[:4]
    else:
        drr, dna, dnb = refs[:3]
    rest = refs[4 if split else 3 :]
    xn, gn, qr, kf, vf, orf, lser, wqkv, wo, segc, segr = rest[:11]
    dr_out, da_out, dqk_out, dv_out, dn_out, dg_out, dks, dvs = rest[11:]
    i = pl.program_id(0)
    blk = blocks - 1 - i
    if split:
        mine = (blk // (blocks // 2)) == h_ref[0]
        dr = jnp.where(mine, dro[...].astype(F32), drp[...].astype(F32))
        dn = jnp.where(mine, dno[...].astype(F32), dnp_[...].astype(F32))
    else:
        dr = drr[...]
        dn = dna[...].astype(F32) + dnb[...].astype(F32)
    dx, dg = norm_back(xn[...], gn[...], dn)
    dr = dr + dx
    dr_out[...] = dr
    da = dr.astype(BF)
    da_out[...] = da

    @pl.when(i == 0)
    def _():
        dks[...] = jnp.zeros_like(dks)
        dvs[...] = jnp.zeros_like(dvs)
        dg_out[...] = jnp.zeros_like(dg_out)

    dg_out[...] += jnp.broadcast_to(dg, dg_out.shape)
    do = mm_nt(da, wo[...]).astype(BF)
    pairs = wo.shape[0] // 128
    for b in range(blocks):

        @pl.when(blk == b)
        def _(b=b):
            keys = BLK * (b + 1)
            here = slice(b * BLK, b * BLK + BLK)
            bias = mask_bias(segc[...], segr[...], b, keys)
            lse = lser[...]
            for pr in range(pairs):
                cols = slice(pr * 128, pr * 128 + 128)
                qp = qr[0, :, cols]
                kp = kf[0, 0:keys, cols]
                vp = vf[0, 0:keys, cols]
                dop = do[:, cols]
                prod = dop.astype(F32) * orf[:, cols].astype(F32)
                dqs, dss, ps, qs, dos = [], [], [], [], []
                for hh in range(2):
                    hm = half_lane(hh)
                    qh = jnp.where(hm, qp, jnp.zeros_like(qp))
                    doh = jnp.where(hm, dop, jnp.zeros_like(dop))
                    delta = jnp.sum(jnp.where(hm, prod, 0.0), axis=-1, keepdims=True)
                    h = pr * 2 + hh
                    p = jnp.exp(mm_nt(qh, kp) + bias - lse[:, h : h + 1])
                    dp = mm_nt(doh, vp)
                    ds = (p * (dp - delta)).astype(BF)
                    dqs.append(mm(ds, kp))
                    dks[0:keys, cols] += mm_tn(ds, qh)
                    dvs[0:keys, cols] += mm_tn(p.astype(BF), doh)
                dq = jnp.where(half_lane(0), dqs[0], dqs[1]) * 0.125
                dqk_out[:, cols] = dq.astype(BF)
            dqk_out[:, pairs * 128 :] = dks[here, :].astype(BF)
            dv_out[...] = dvs[here, :].astype(BF)

    c = pairs * 128
    dn_out[...] = (
        mm_nt(dqk_out[:, :c], wqkv[0]) + mm_nt(dqk_out[:, c:], wqkv[1]) + mm_nt(dv_out[...], wqkv[2])
    ).astype(BF)


def dense_fwd_kernel(xr, pa, pb, g, up, down, x_out, n_out, act_out, gp_out, p_out):
    x = xr[...] + (pa[...].astype(F32) + pb[...].astype(F32))
    x_out[...] = x
    xh, _ = norm_stats(x)
    n = (xh * g[...]).astype(BF)
    n_out[...] = n
    act, gp = gelu_pair(mm(n, up[...]))
    act = act.astype(BF)
    act_out[...] = act
    gp_out[...] = gp.astype(BF)
    p_out[...] = mm(act, down[...]).astype(BF)


def dense_bwd_kernel(drr, dna, dnb, xn, gn, gp, up, down, dr_out, df_out, du_out, dn_out, dg_out):
    dx, dg = norm_back(xn[...], gn[...], dna[...].astype(F32) + dnb[...].astype(F32))
    dr = drr[...] + dx
    dr_out[...] = dr
    df = dr.astype(BF)
    df_out[...] = df

    @pl.when(pl.program_id(0) == 0)
    def _():
        dg_out[...] = jnp.zeros_like(dg_out)

    dg_out[...] += jnp.broadcast_to(dg, dg_out.shape)
    du = (mm_nt(df, down[...]) * gp[...].astype(F32)).astype(BF)
    du_out[...] = du
    dn_out[...] = mm_nt(du, up[...]).astype(BF)


def final_kernel(h_ref, drr, dna, dnb, xo, xp, gn, dr_out, dg_out):
    i = pl.program_id(0)
    mine = i >= 2
    x = jnp.where(mine, xo[...].astype(F32), xp[...].astype(F32))
    dx, dg = norm_back(x, gn[...], dna[...].astype(F32) + dnb[...].astype(F32))
    dr_out[...] = drr[...] + dx

    @pl.when(i == 0)
    def _():
        dg_out[...] = jnp.zeros_like(dg_out)

    dg_out[...] += jnp.broadcast_to(dg, dg_out.shape)


def spread_kernel(rows_ref, slot_ref, out_ref):
    count = out_ref.shape[0]
    place = lax.broadcasted_iota(jnp.int32, (count, rows_ref.shape[0]), 0)
    place = place + pl.program_id(0) * count
    hot = (place == slot_ref[...]).astype(F32).astype(BF)
    out_ref[...] = mm(hot, rows_ref[...]).astype(BF)


def route_kernel(h_ref, xr, pa, pb, g, slot_ref, x_out, send_out, ms):
    i = pl.program_id(0)
    x = xr[...] + (pa[...].astype(F32) + pb[...].astype(F32))
    x_out[...] = x

    @pl.when(i >= 2)
    def _():
        xh, _ = norm_stats(x)
        rows = pl.ds(pl.multiple_of((i - 2) * BLK, BLK), BLK)
        ms[rows, :] = (xh * g[...]).astype(BF)

    @pl.when(i == 3)
    def _():
        count = send_out.shape[0]
        place = lax.broadcasted_iota(jnp.int32, (count, ms.shape[0]), 0)
        hot = (place == slot_ref[...]).astype(F32).astype(BF)
        send_out[...] = mm(hot, ms[...]).astype(BF)


def collect_kernel(table, slot_ref, out_ref):
    count = table.shape[0]
    place = lax.broadcasted_iota(jnp.int32, (out_ref.shape[0], count), 1)
    hot = (place == slot_ref[...]).astype(F32).astype(BF)
    out_ref[...] = mm(hot, table[...]).astype(BF)


def collect_add_kernel(h_ref, table, slot_ref, x_ref, out_ref):
    count = table.shape[0]
    place = lax.broadcasted_iota(jnp.int32, (out_ref.shape[0], count), 1)
    hot = (place == slot_ref[...]).astype(F32).astype(BF)
    out_ref[...] = (x_ref[...] + mm(hot, table[...])).astype(BF)


def expert_kernel(
    half, mo, mp, go, gp_, cen, up, down,
    yo, yp, dmo, dmp, m_all, dy_all, ae_all, due_all, dc_out,
):
    i = pl.program_id(0)
    first = i < half
    m = jnp.where(first, mo[...], mp[...])
    gb = jnp.where(first, go[...], gp_[...]).astype(F32)
    mf = m.astype(F32)
    cf = cen[...].astype(F32)
    gate = jax.nn.sigmoid(jnp.sum(mf * cf, axis=-1, keepdims=True))
    act, gd = gelu_pair(mm(m, up[0]))
    act = act.astype(BF)
    y = mm(act, down[0])
    dscore = jnp.sum(gb * y, axis=-1, keepdims=True) * gate * (1.0 - gate)
    dy = (gate * gb).astype(BF)
    due = (mm_nt(dy, down[0]) * gd).astype(BF)
    dm = (mm_nt(due, up[0]) + dscore * cf).astype(BF)
    gy = (gate * y).astype(BF)
    m_all[...] = m
    dy_all[...] = dy
    ae_all[...] = act
    due_all[...] = due

    @pl.when(i == 0)
    def _():
        dc_out[...] = jnp.zeros_like(dc_out)

    dc_out[...] += jnp.broadcast_to(jnp.sum(dscore * mf, axis=0, keepdims=True), dc_out.shape)

    @pl.when(first)
    def _():
        yo[...] = gy
        dmo[...] = dm

    @pl.when(jnp.logical_not(first))
    def _():
        yp[...] = gy
        dmp[...] = dm


def shape(dims, kind):
    return jax.ShapeDtypeStruct(dims, kind)


def fixed(dims):
    zero = (0,) * len(dims)
    return pl.BlockSpec(dims, lambda *a: zero, pipeline_mode=pl.Buffered(1))


def rows_spec(width, index=lambda i: i):
    return pl.BlockSpec((BLK, width), lambda i, *a: (index(i), 0))


PARAMS = pltpu.CompilerParams(vmem_limit_bytes=VLIM, dimension_semantics=("arbitrary",))


def call(kernel, grid, in_specs, out_specs, outs, scratch, flops, moved, args, prefetch=None):
    cost = pl.CostEstimate(flops=int(flops), bytes_accessed=int(moved), transcendentals=0)
    if prefetch is None:
        spec = pl.GridSpec(
            grid=grid, in_specs=in_specs, out_specs=out_specs, scratch_shapes=scratch
        )
    else:
        spec = pltpu.PrefetchScalarGridSpec(
            num_scalar_prefetch=1,
            grid=grid,
            in_specs=in_specs,
            out_specs=out_specs,
            scratch_shapes=scratch,
        )
        args = (prefetch,) + tuple(args)
    return pl.pallas_call(
        kernel, grid_spec=spec, out_shape=outs, compiler_params=PARAMS, cost_estimate=cost
    )(*args)


def attention_forward(h, inputs, split, gain, wqkv, wo, segc, segr):
    length, d = segc.shape[0], wqkv.shape[1]
    c = wqkv.shape[2]
    blocks = length // BLK
    if split:
        ins = [rows_spec(d, lambda i: i % (blocks // 2))] * 2
    else:
        ins = [rows_spec(d)] * 3
    ins += [
        fixed((1, d)),
        fixed((3, d, c)),
        fixed((c, d)),
        pl.BlockSpec((BLK, 1), lambda i, *a: (i, 0)),
        fixed((1, length)),
    ]
    outs = [
        (rows_spec(d), shape((length, d), F32)),
        (rows_spec(d), shape((length, d), BF)),
        (pl.BlockSpec((3, BLK, c), lambda i, *a: (0, i, 0)), shape((3, length, c), BF)),
        (rows_spec(c), shape((length, c), BF)),
        (rows_spec(128), shape((length, 128), F32)),
        (rows_spec(d), shape((length, d), BF)),
    ]
    scratch = [pltpu.VMEM((length, c), BF), pltpu.VMEM((length, c), BF)]
    flops = 2 * length * d * c * 4 + 4 * length * length * c
    return call(
        functools.partial(attn_fwd_kernel, blocks, split),
        (blocks,),
        ins,
        [o[0] for o in outs],
        [o[1] for o in outs],
        scratch,
        flops * 2,
        length * d * 20,
        (*inputs, gain, wqkv, wo, segc, segr),
        prefetch=h,
    )


def attention_backward(h, inputs, split, xn, gn, saved, wqkv, wo, segc, segr):
    qkv, o, lse = saved
    length, d = segc.shape[0], wqkv.shape[1]
    c = wqkv.shape[2]
    blocks = length // BLK
    back = lambda i: blocks - 1 - i
    if split:
        ins = [rows_spec(d, lambda i: back(i) % (blocks // 2))] * 4
    else:
        ins = [rows_spec(d, back)] * 3
    part = lambda n: pl.BlockSpec(
        (1, length, c), lambda i, *a: (n, 0, 0), pipeline_mode=pl.Buffered(1)
    )
    ins += [
        rows_spec(d, back),
        fixed((1, d)),
        pl.BlockSpec((1, BLK, c), lambda i, *a: (0, back(i), 0)),
        part(1),
        part(2),
        rows_spec(c, back),
        rows_spec(128, back),
        fixed((3, d, c)),
        fixed((c, d)),
        pl.BlockSpec((BLK, 1), lambda i, *a: (back(i), 0)),
        fixed((1, length)),
    ]
    outs = [
        (rows_spec(d, back), shape((length, d), F32)),
        (rows_spec(d, back), shape((length, d), BF)),
        (rows_spec(2 * c, back), shape((length, 2 * c), BF)),
        (rows_spec(c, back), shape((length, c), BF)),
        (rows_spec(d, back), shape((length, d), BF)),
        (fixed((8, d)), shape((8, d), F32)),
    ]
    scratch = [pltpu.VMEM((length, c), F32), pltpu.VMEM((length, c), F32)]
    flops = 2 * length * d * c * 4 + 10 * length * length * c
    return call(
        functools.partial(attn_bwd_kernel, blocks, split),
        (blocks,),
        ins,
        [s[0] for s in outs],
        [s[1] for s in outs],
        scratch,
        flops * 2,
        length * d * 20,
        (*inputs, xn, gn, qkv, qkv, qkv, o, lse, wqkv, wo, segc, segr),
        prefetch=h,
    )


def dense_forward(x, pa, pb, gain, up, down):
    length, d = x.shape
    f = up.shape[1]
    return call(
        dense_fwd_kernel,
        (length // BLK,),
        [rows_spec(d)] * 3 + [fixed((1, d)), fixed((d, f)), fixed((f, d))],
        [rows_spec(d), rows_spec(d), rows_spec(f), rows_spec(f), rows_spec(d)],
        [
            shape((length, d), F32),
            shape((length, d), BF),
            shape((length, f), BF),
            shape((length, f), BF),
            shape((length, d), BF),
        ],
        [],
        4 * length * d * f,
        length * d * 20 + 4 * d * f,
        (x, pa, pb, gain, up, down),
    )


def dense_backward(dr, dna, dnb, xn, gn, gp, up, down):
    length, d = dr.shape
    f = up.shape[1]
    return call(
        dense_bwd_kernel,
        (length // BLK,),
        [rows_spec(d)] * 4
        + [fixed((1, d)), rows_spec(f), fixed((d, f)), fixed((f, d))],
        [rows_spec(d), rows_spec(d), rows_spec(f), rows_spec(d), fixed((8, d))],
        [
            shape((length, d), F32),
            shape((length, d), BF),
            shape((length, f), BF),
            shape((length, d), BF),
            shape((8, d), F32),
        ],
        [],
        4 * length * d * f,
        length * d * 20 + 4 * d * f,
        (dr, dna, dnb, xn, gn, gp, up, down),
    )


def own_last(blocks):
    return lambda i, h: lax.rem(i + (blocks // 2) * (1 - h[0]), blocks)


def final_step(h, dr, dna, dnb, xo, xp, gn):
    length, d = dr.shape
    blocks = length // BLK
    place = own_last(blocks)
    spec = pl.BlockSpec((BLK, d), lambda i, h: (place(i, h), 0))
    late = lambda i, h: (jnp.maximum(i - blocks // 2, 0), 0)
    return call(
        final_kernel,
        (blocks,),
        [spec] * 3
        + [pl.BlockSpec((BLK, d), late)]
        + [pl.BlockSpec((BLK, d), lambda i, h: (lax.rem(i, blocks // 2), 0)), fixed((1, d))],
        [pl.BlockSpec((BLK, d), late), fixed((8, d))],
        [shape((length // 2, d), F32), shape((8, d), F32)],
        [],
        length * d * 40,
        length * d * 14,
        (dr, dna, dnb, xo, xp, gn),
        prefetch=h,
    )


def route_step(h, x, pa, pb, gain, slot_row, slots):
    length, d = x.shape
    blocks = length // BLK
    place = own_last(blocks)
    spec = pl.BlockSpec((BLK, d), lambda i, h: (place(i, h), 0))
    return call(
        route_kernel,
        (blocks,),
        [spec] * 3 + [fixed((1, d)), fixed((1, length // 2))],
        [spec, fixed((slots, d))],
        [shape((length, d), F32), shape((slots, d), BF)],
        [pltpu.VMEM((length // 2, d), BF)],
        length * slots * d,
        length * d * 14,
        (x, pa, pb, gain, slot_row),
        prefetch=h,
    )


def spread(rows, slot_row, slots):
    count, d = rows.shape
    return call(
        spread_kernel,
        (slots // BLK,),
        [fixed((count, d)), fixed((1, count))],
        [rows_spec(d)],
        [shape((slots, d), BF)],
        [],
        2 * count * slots * d,
        4 * slots * d,
        (rows, slot_row),
    )[0]


def collect(table, slot_col):
    slots, d = table.shape
    count = slot_col.shape[0]
    return call(
        collect_kernel,
        (count // BLK,),
        [fixed((slots, d)), pl.BlockSpec((BLK, 1), lambda i, *a: (i, 0))],
        [rows_spec(d)],
        [shape((count, d), BF)],
        [],
        2 * count * slots * d,
        4 * slots * d,
        (table, slot_col),
    )[0]


def collect_add(h, table, slot_col, x):
    slots, d = table.shape
    count = slot_col.shape[0]
    per = count // BLK
    return call(
        collect_add_kernel,
        (per,),
        [
            fixed((slots, d)),
            pl.BlockSpec((BLK, 1), lambda i, *a: (i, 0)),
            pl.BlockSpec((BLK, d), lambda i, h: (h[0] * per + i, 0)),
        ],
        [rows_spec(d)],
        [shape((count, d), BF)],
        [],
        2 * count * slots * d,
        8 * slots * d,
        (table, slot_col, x),
        prefetch=h,
    )[0]


def expert_step(mo, mp, go, gp, cen, up, down):
    rows, d = mo.shape
    f = up.shape[2]
    half = rows // BLK
    lo = lambda i: jnp.minimum(i, half - 1)
    hi = lambda i: jnp.maximum(i - half, 0)
    return call(
        functools.partial(expert_kernel, half),
        (2 * half,),
        [rows_spec(d, lo), rows_spec(d, hi), rows_spec(d, lo), rows_spec(d, hi)]
        + [fixed((1, d)), fixed((1, d, f)), fixed((1, f, d))],
        [rows_spec(d, lo), rows_spec(d, hi), rows_spec(d, lo), rows_spec(d, hi)]
        + [rows_spec(d), rows_spec(d), rows_spec(f), rows_spec(f), fixed((8, d))],
        [shape((rows, d), BF)] * 4
        + [shape((2 * rows, d), BF)] * 2
        + [shape((2 * rows, f), BF)] * 2
        + [shape((8, d), F32)],
        [],
        16 * rows * d * f,
        rows * d * 24 + rows * f * 8,
        (mo, mp, go, gp, cen, up, down),
    )


def slot_index(chosen, capacity, experts):
    rows = chosen.shape[0]
    matches = chosen[:, None] == jnp.arange(experts, dtype=jnp.int32)[None, :]
    position = jnp.arange(rows, dtype=jnp.int32)
    earlier = (position[None, :] < position[:, None]).astype(BF)
    before = jnp.dot(earlier, matches.astype(BF), preferred_element_type=F32)
    rank = jnp.sum(jnp.where(matches, before, 0.0), axis=1).astype(jnp.int32)
    return chosen * capacity + rank


def swap(v):
    return lax.ppermute(v, "head", SWAP)


def hop(sends, during=None, inputs=()):
    flat = [v for v, _ in sends]
    flat, inputs = lax.optimization_barrier((flat, inputs))
    got = [
        lax.ppermute(v, "dp", [(i, i ^ s) for i in range(16)])
        for v, (_, s) in zip(flat, sends)
    ]
    result = during(*inputs) if during else inputs
    return lax.optimization_barrier((got, result))


def pick(bit, a, b):
    return jnp.where(bit == 1, a, b)


def total_of(a, b):
    return (a.astype(F32) + b.astype(F32)).astype(BF)


def fold_kernel(plan, bits, *refs):
    at = 0
    outs = refs[sum(n for _, n, _, _ in plan) :]
    for kind, n, place, count in plan:
        ins = refs[at : at + n]
        at += n
        bit = bits[place]
        if kind == "sum":
            outs[0][...] = total_of(ins[0][...], ins[1][...])
            outs = outs[1:]
        elif kind == "cut":
            half = ins[0].shape[0] // 2
            lo, hi = ins[0][:half, :], ins[0][half:, :]
            outs[0][...] = pick(bit, lo, hi)
            outs[1][...] = pick(bit, hi, lo)
            outs = outs[2:]
        elif kind == "split":
            for j in range(n // 2):
                k, g = ins[2 * j], ins[2 * j + 1]
                q = k.shape[0] // 2
                rows = slice(j * q, j * q + q)
                lo = total_of(k[:q, :], g[:q, :])
                hi = total_of(k[q:, :], g[q:, :])
                outs[0][rows, :] = pick(bit, lo, hi)
                outs[1][rows, :] = pick(bit, hi, lo)
            outs = outs[2:]
        else:
            q = ins[0].shape[0] // count
            for j in range(count):
                p, g = ins[0][j * q : j * q + q, :], ins[1][j * q : j * q + q, :]
                outs[j][:q, :] = pick(bit, g, p)
                outs[j][q:, :] = pick(bit, p, g)
            outs = outs[count:]


PLACE = {1: 0, 2: 1, 4: 2, 8: 3}


def whole(arrays):
    return [pl.BlockSpec(a.shape, lambda i, *r, n=len(a.shape): (0,) * n) for a in arrays]


def one_step(kernel, bits, args, outs):
    moved = sum(a.size * a.dtype.itemsize for a in (*args, *outs))
    return call(kernel, (1,), whole(args), whole(outs), outs, [], moved, moved, args, prefetch=bits)


def fold(bits, items):
    plan, args, outs, sizes = [], [], [], []
    for kind, arrays, step, count in items:
        plan.append((kind, len(arrays), PLACE[step], count))
        args += arrays
        rows, width = arrays[0].shape
        if kind == "sum":
            made = [rows]
        elif kind == "cut":
            made = [rows // 2] * 2
        elif kind == "split":
            made = [sum(a.shape[0] for a in arrays) // 4] * 2
        else:
            made = [2 * rows // count] * count
        outs += [shape((r, width), BF) for r in made]
        sizes.append(len(made))
    flat = one_step(functools.partial(fold_kernel, tuple(plan)), bits, args, outs)
    result = []
    for n in sizes:
        result.append(flat[:n])
        flat = flat[n:]
    return result


def grad_rounds(sends, keeps):
    one, two = (1, 2, 4, 8), (2, 1, 8, 4)
    got = yield list(zip(sends, one))
    out = yield [("split", [k, g], s, 1) for k, g, s in zip(keeps, got, two)]
    got = yield [(o[0], s) for o, s in zip(out, two)]
    keeps = [o[1] for o in out]
    out = yield [
        ("split", [keeps[0], got[0], keeps[1], got[1]], 4, 1),
        ("split", [keeps[2], got[2], keeps[3], got[3]], 1, 1),
    ]
    got = yield [(out[0][0], 4), (out[1][0], 1)]
    out = yield [("split", [out[0][1], got[0]], 8, 1), ("split", [out[1][1], got[1]], 2, 1)]
    got = yield [(out[0][0], 8), (out[1][0], 2)]
    out = yield [("sum", [out[0][1], got[0]], 8, 1), ("sum", [out[1][1], got[1]], 2, 1)]
    got = yield [(out[0][0], 8), (out[1][0], 2)]
    out = yield [("raise", [out[0][0], got[0]], 8, 1), ("raise", [out[1][0], got[1]], 2, 1)]
    got = yield [(out[0][0], 4), (out[1][0], 1)]
    out = yield [("raise", [out[0][0], got[0]], 4, 2), ("raise", [out[1][0], got[1]], 1, 2)]
    parts = [*out[0], *out[1]]
    got = yield list(zip(parts, two))
    out = yield [("raise", [p, g], s, 1) for p, g, s in zip(parts, got, two)]
    parts = [o[0] for o in out]
    got = yield list(zip(parts, one))
    return [x for pair in zip(parts, got) for x in pair]


def small_rounds(v):
    for s in (1, 2, 4, 8):
        got = yield [(v, s)]
        v = v + got[0]
        yield []
    return v


class Lane:
    def __init__(self, rounds):
        self.rounds = rounds
        self.value = None
        self.sends = next(rounds)

    def push(self, value):
        try:
            return self.rounds.send(value)
        except StopIteration as stop:
            self.value, self.sends = stop.value, []
            return []


def advance(bits, lanes, during=None, inputs=()):
    got, result = hop([x for lane in lanes for x in lane.sends], during, inputs)
    asked = []
    for lane in lanes:
        count = len(lane.sends)
        asked.append((lane, lane.push(got[:count]) if count else []))
        got = got[count:]
    items = [item for _, group in asked for item in group]
    done = fold(bits, items) if items else []
    for lane, group in asked:
        if lane.value is None:
            lane.sends = lane.push(done[: len(group)]) or []
        done = done[len(group) :]
    return result


def wide(ref_a, ref_b, bit):
    a, b = ref_a[...].astype(F32), ref_b[...].astype(F32)
    return pick(bit, b, a), pick(bit, a, b)


def finish_wide_kernel(bits, xp, xg, yp, yg, ap, ag, bp, bg, up, down, qkv, out):
    lo, hi = wide(xp, xg, bits[0])
    f = lo.shape[1]
    up[:, :f] = lo
    up[:, f:] = hi
    lo, hi = wide(yp, yg, bits[1])
    f = lo.shape[0]
    down[:f, :] = lo
    down[f:, :] = hi
    c = qkv.shape[2]
    for j, block in enumerate(wide(ap, ag, bits[2])):
        n = block.shape[0]
        qkv[0, j * n : j * n + n, :] = block[:, :c]
        qkv[1, j * n : j * n + n, :] = block[:, c:]
    v, o = wide(bp, bg, bits[3])
    n = v.shape[0]
    qkv[2, :n, :] = v[:, :c]
    qkv[2, n:, :] = v[:, c:]
    out[...] = o


def finish_narrow_kernel(bits, xp, xg, yp, yg, ap, ag, bp, bg, qkv, out):
    xl, xh = wide(xp, xg, bits[0])
    yl, yh = wide(yp, yg, bits[1])
    al, ah = wide(ap, ag, bits[2])
    bl, bh = wide(bp, bg, bits[3])
    n = xl.shape[0]
    c = qkv.shape[2]
    for j, block in enumerate((xl, xh, yl, yh)):
        at = slice(j * n, j * n + n)
        qkv[0, at, :] = block[:, :c]
        qkv[1, at, :] = block[:, c:]
    half = qkv.shape[1] // 2
    for j, block in enumerate((al, ah)):
        qkv[2, j * n : j * n + n, :] = block[:, :c]
        qkv[2, half + j * n : half + j * n + n, :] = block[:, c:]
    out[:n, :] = bl
    out[n:, :] = bh


def body(
    steps,
    tokens,
    segment_ids,
    routes,
    norm_gains,
    qkv_one,
    out_one,
    up_one,
    down_one,
    qkv_two,
    out_two,
    expert_up,
    expert_down,
    centroids,
    cotangent,
):
    count, d = tokens.shape
    side = lax.axis_index("head")
    h = side.astype(jnp.int32).reshape(1)
    experts = lax.axis_size("dp") * expert_up.shape[0]
    capacity = 2 * count // experts
    slots = experts * capacity
    gains = norm_gains.astype(F32)
    gain = [gains[j : j + 1] for j in range(4)]
    segc, segr = segment_ids[:, None], segment_ids[None, :]

    chosen = lax.dynamic_slice_in_dim(routes[:, 0], side * count, count, 0)
    flat = slot_index(chosen, capacity, experts)
    slot_row, slot_col = flat[None, :], flat[:, None]

    def travel(v):
        box = v.reshape(experts, capacity, d)
        return lax.all_to_all(box, "dp", 0, 0, tiled=True).reshape(slots, d)

    tokens_peer = swap(tokens)
    x0, n1, qkv1, o1, lse1, p1 = attention_forward(
        h, (tokens, tokens_peer), True, gain[0], qkv_one, out_one, segc, segr
    )
    p1r = swap(p1)
    cot_peer = swap(cotangent)
    grad_own = travel(spread(cotangent, slot_row, slots))
    grad_peer = swap(grad_own)
    x1, n2, act, gp, p2 = dense_forward(x0, p1, p1r, gain[1], up_one, down_one)
    p2r = swap(p2)
    first, n3, qkv2, o2, lse2, p3 = attention_forward(
        h, (x1, p2, p2r), False, gain[2], qkv_two, out_two, segc, segr
    )
    p3r = swap(p3)
    x2, sent = route_step(h, first, p3, p3r, gain[3], slot_row, slots)
    m_own = travel(sent)
    m_peer = swap(m_own)
    yo, yp, dmo, dmp, m_all, dy_all, ae_all, due_all, dc = expert_step(
        m_own, m_peer, grad_own, grad_peer, centroids, expert_up, expert_down
    )
    dm_sum = (dmo.astype(F32) + swap(dmp).astype(F32)).astype(BF)
    up_grad = mm_tn(m_all, due_all)[None]
    down_grad = mm_tn(ae_all, dy_all)[None]
    dm_back, up_grad, down_grad = lax.optimization_barrier((travel(dm_sum), up_grad, down_grad))
    dm_own = collect(dm_back, slot_col)
    dm_peer = swap(dm_own)
    y_sum = (yo.astype(F32) + swap(yp).astype(F32)).astype(BF)
    y_back = travel(y_sum)
    dc = dc[:1]
    cen_grad = dc + swap(dc)

    dr2, da2, dqk2, dv2, dn2, dg3 = attention_backward(
        h,
        (cotangent, cot_peer, dm_own, dm_peer),
        True,
        x2,
        gain[3],
        (qkv2, o2, lse2),
        qkv_two,
        out_two,
        segc,
        segr,
    )
    dn2r = swap(dn2)
    f = up_one.shape[1]
    c = qkv_one.shape[2]

    def grad(a, b):
        return mm_tn(a, b).astype(BF)

    def value_sides(n, dv):
        w = grad(n, dv)
        return jnp.concatenate([w[: d // 2], w[d // 2 :]], axis=1)

    def finish(dr, dna, dnb):
        return final_step(h, dr, dna, dnb, tokens, tokens_peer, gain[0])

    def gather_y(y):
        return collect_add(h, y, slot_col, x2)

    def stack_gains(dg0):
        return jnp.concatenate([dg0[:1], dg1[:1], dg2[:1], dg3[:1]], axis=0)

    def last_attention(dr, dna, dnb):
        return attention_backward(
            h, (dr, dna, dnb), False, x1, gain[1], (qkv1, o1, lse1), qkv_one, out_one, segc, segr
        )

    qk_two = grad(n3, dqk2)
    vo_two = jnp.concatenate([value_sides(n3, dv2), grad(o2, da2)], axis=0)
    if steps is None:
        dr1, df, du, dnd, dg2 = dense_backward(
            dr2, dn2, dn2r, first, gain[2], gp, up_one, down_one
        )
        dr0, da1, dqk1, dv1, dn1, dg1 = last_attention(dr1, dnd, swap(dnd))
        input_grad, dg0 = finish(dr0, dn1, swap(dn1))
        second = gather_y(y_back)
        qk_one = grad(n1, dqk1)
        vo_one = jnp.concatenate([value_sides(n1, dv1), grad(o1, da1)], axis=0)
        up_first, down_first, qk_two, vo_two, qk_one, vo_one, gain_grads = lax.psum(
            (grad(n2, du), grad(act, df), qk_two, vo_two, qk_one, vo_one, stack_gains(dg0)), "dp"
        )

        def unpack(qk, vo):
            v, wo = vo[: d // 2], vo[d // 2 :]
            v = jnp.concatenate([v[:, :c], v[:, c:]], axis=0)
            return jnp.stack([qk[:, :c], qk[:, c:], v]).astype(F32), wo.astype(F32)

        up_first, down_first = up_first.astype(F32), down_first.astype(F32)
        qkv_second, out_second = unpack(qk_two, vo_two)
        qkv_first, out_first = unpack(qk_one, vo_one)
    else:
        me = lax.axis_index("dp")
        bits = jnp.stack([(me // s) % 2 for s in (1, 2, 4, 8)]).astype(jnp.int32)
        cut_two = fold(bits, [("cut", [qk_two], 4, 1), ("cut", [vo_two], 8, 1)])
        cut_two, dr2, dn2, dn2r, y_back = lax.optimization_barrier(
            (cut_two, dr2, dn2, dn2r, y_back)
        )
        dr1, df, du, dnd, dg2 = dense_backward(
            dr2, dn2, dn2r, first, gain[2], gp, up_one, down_one
        )
        dndr = swap(dnd)

        def up_part(bit):
            return grad(n2, lax.dynamic_slice_in_dim(du, bit * (f // 2), f // 2, 1))

        def down_part(bit):
            return grad(lax.dynamic_slice_in_dim(act, bit * (f // 2), f // 2, 1), df)

        sends = [up_part(1 - bits[0]), down_part(1 - bits[1]), cut_two[0][0], cut_two[1][0]]
        keeps = [None, None, cut_two[0][1], cut_two[1][1]]

        def heavy(dr, dna, dnb):
            return last_attention(dr, dna, dnb), up_part(bits[0]), down_part(bits[1])

        got, (last, keeps[0], keeps[1]) = hop(
            list(zip(sends, (1, 2, 4, 8))), heavy, (dr1, dnd, dndr)
        )
        dr0, da1, dqk1, dv1, dn1, dg1 = last
        dn1r = swap(dn1)
        wide_lane = Lane(grad_rounds(sends, keeps))
        cut = fold(bits, wide_lane.push(got))
        wide_lane.sends = wide_lane.push(cut)

        def narrow_grads(n, dqk, dv, o, da):
            half = d // 2
            return (
                grad(n[:, :half], dqk),
                grad(n[:, half:], dqk),
                value_sides(n, dv),
                grad(o, da),
            )

        raw = advance(bits, [wide_lane], narrow_grads, (n1, dqk1, dv1, o1, da1))
        cut = fold(bits, [("cut", [w], s, 1) for w, s in zip(raw, (1, 2, 4, 8))])
        lane = Lane(grad_rounds([x[0] for x in cut], [x[1] for x in cut]))
        input_grad, dg0 = advance(bits, [wide_lane, lane], finish, (dr0, dn1, dn1r))
        gain_lane = Lane(small_rounds(stack_gains(dg0)))
        lanes = [wide_lane, lane, gain_lane]
        second = advance(bits, lanes, gather_y, (y_back,))
        while wide_lane.sends:
            advance(bits, lanes)

        def finish_wide(*parts):
            return one_step(
                finish_wide_kernel,
                bits,
                parts,
                [
                    shape((d, f), F32),
                    shape((f, d), F32),
                    shape((3, d, c), F32),
                    shape((c, d), F32),
                ],
            )

        up_first, down_first, qkv_second, out_second = advance(
            bits, lanes, finish_wide, wide_lane.value
        )
        while lane.sends:
            advance(bits, lanes)
        gain_grads = gain_lane.value
        qkv_first, out_first = one_step(
            finish_narrow_kernel, bits, lane.value, [shape((3, d, c), F32), shape((c, d), F32)]
        )
    first_own = lax.dynamic_slice_in_dim(first, side * count, count, 0).astype(BF)
    return (
        first_own,
        second,
        input_grad,
        gain_grads,
        qkv_first,
        out_first,
        up_first,
        down_first,
        qkv_second,
        out_second,
        up_grad,
        down_grad,
        cen_grad,
    )


def solution(mesh):
    rows = P(("dp", "head"), None)
    shared = (
        P(None, None, "head"),
        P("head", None),
        P(None, "head"),
        P("head", None),
        P(None, None, "head"),
        P("head", None),
        P("dp", None, "head"),
        P("dp", "head", None),
        P("dp", None),
    )
    steps = 16 if mesh.shape["dp"] == 16 else None
    return jax.shard_map(
        functools.partial(body, steps),
        mesh=mesh,
        in_specs=(rows, P("dp"), P("dp", None), P(), *shared, rows),
        out_specs=(rows, rows, rows, P(), *shared),
        check_vma=False,
    )
```

```python
import functools

import jax
import jax.numpy as jnp
from jax import lax
from jax.experimental import pallas as pl
from jax.experimental.pallas import tpu as pltpu
from jax.sharding import PartitionSpec as P

BF = jnp.bfloat16
F32 = jnp.float32
EPS = 1e-05
MASKED = -1e30
BLK = 256
HEAD_DIM = 64
SWAP = [(0, 1), (1, 0)]
VLIM = 56 * 1024 * 1024


def mm(a, b):
    return lax.dot_general(a, b, (((1,), (0,)), ((), ())), preferred_element_type=F32)


def mm_nt(a, b):
    return lax.dot_general(a, b, (((1,), (1,)), ((), ())), preferred_element_type=F32)


def mm_tn(a, b):
    return lax.dot_general(a, b, (((0,), (0,)), ((), ())), preferred_element_type=F32)


def norm_stats(x):
    c = x - jnp.mean(x, axis=-1, keepdims=True)
    r = lax.rsqrt(jnp.mean(c * c, axis=-1, keepdims=True) + EPS)
    return c * r, r


def norm_back(x, gain, dn):
    xh, r = norm_stats(x)
    dxh = dn * gain
    a = jnp.mean(dxh, axis=-1, keepdims=True)
    b = jnp.mean(dxh * xh, axis=-1, keepdims=True)
    return r * (dxh - a - xh * b), jnp.sum(dn * xh, axis=0, keepdims=True)


def gelu_pair(u):
    z = jnp.abs(u) * 0.7071067811865476
    t = 1.0 / (1.0 + 0.3275911 * z)
    ex = jnp.exp(-(z * z))
    poly = t * (
        0.254829592
        + t * (-0.284496736 + t * (1.421413741 + t * (-1.453152027 + t * 1.061405429)))
    )
    tail = 0.5 * poly * ex
    phi = jnp.where(u >= 0.0, 1.0 - tail, tail)
    return u * phi, phi + u * (ex * 0.3989422804014327)


def mask_bias(segc, segr, b, keys):
    row = lax.broadcasted_iota(jnp.int32, (BLK, keys), 0) + b * BLK
    col = lax.broadcasted_iota(jnp.int32, (BLK, keys), 1)
    return jnp.where((segc == segr[:, :keys]) & (col <= row), 0.0, MASKED)


def half_lane(hh):
    lane = lax.broadcasted_iota(jnp.int32, (BLK, 128), 1)
    return (lane >= 64) if hh else (lane < 64)


def attn_fwd_kernel(blocks, split, h_ref, *refs):
    if split:
        own, peer, g, wqkv, wo, segc, segr = refs[:7]
        outs = refs[7:]
    else:
        xr, pa, pb, g, wqkv, wo, segc, segr = refs[:8]
        outs = refs[8:]
    x_out, n_out, qkv_out, o_out, lse_out, p_out, ks, vs = outs
    i = pl.program_id(0)
    if split:
        mine = (i // (blocks // 2)) == h_ref[0]
        x = jnp.where(mine, own[...].astype(F32), peer[...].astype(F32))
    else:
        x = xr[...] + (pa[...].astype(F32) + pb[...].astype(F32))
    x_out[...] = x
    xh, _ = norm_stats(x)
    n = (xh * g[...]).astype(BF)
    n_out[...] = n
    q = (mm(n, wqkv[0]).astype(BF).astype(F32) * 0.125).astype(BF)
    k = mm(n, wqkv[1]).astype(BF)
    v = mm(n, wqkv[2]).astype(BF)
    qkv_out[0] = q
    qkv_out[1] = k
    qkv_out[2] = v
    rows = pl.ds(pl.multiple_of(i * BLK, BLK), BLK)
    ks[rows, :] = k
    vs[rows, :] = v
    pairs = q.shape[1] // 128
    for b in range(blocks):

        @pl.when(i == b)
        def _(b=b):
            keys = BLK * (b + 1)
            bias = mask_bias(segc[...], segr[...], b, keys)
            lse = jnp.zeros((BLK, 128), F32)
            lanes = lax.broadcasted_iota(jnp.int32, (BLK, 128), 1)
            total = jnp.zeros((BLK, wo.shape[1]), F32)
            for pr in range(pairs):
                cols = slice(pr * 128, pr * 128 + 128)
                qp = qkv_out[0, :, cols]
                kp = ks[0:keys, cols]
                vp = vs[0:keys, cols]
                res = []
                for hh in range(2):
                    qh = jnp.where(half_lane(hh), qp, jnp.zeros_like(qp))
                    s = mm_nt(qh, kp) + bias
                    m = jnp.max(s, axis=-1, keepdims=True)
                    e = jnp.exp(s - m)
                    l = jnp.sum(e, axis=-1, keepdims=True)
                    res.append(mm(e.astype(BF), vp) * (1.0 / l))
                    lse = jnp.where(lanes == pr * 2 + hh, m + jnp.log(l), lse)
                ob = jnp.where(half_lane(0), res[0], res[1]).astype(BF)
                o_out[:, cols] = ob
                total = total + mm(ob, wo[cols, :])
            lse_out[...] = lse
            p_out[...] = total.astype(BF)


def attn_bwd_kernel(blocks, split, h_ref, *refs):
    if split:
        dro, drp, dno, dnp_ = refs[:4]
    else:
        drr, dna, dnb = refs[:3]
    rest = refs[4 if split else 3 :]
    xn, gn, qr, kf, vf, orf, lser, wqkv, wo, segc, segr = rest[:11]
    dr_out, da_out, dqk_out, dv_out, dn_out, dg_out, dks, dvs = rest[11:]
    i = pl.program_id(0)
    blk = blocks - 1 - i
    if split:
        mine = (blk // (blocks // 2)) == h_ref[0]
        dr = jnp.where(mine, dro[...].astype(F32), drp[...].astype(F32))
        dn = jnp.where(mine, dno[...].astype(F32), dnp_[...].astype(F32))
    else:
        dr = drr[...]
        dn = dna[...].astype(F32) + dnb[...].astype(F32)
    dx, dg = norm_back(xn[...], gn[...], dn)
    dr = dr + dx
    dr_out[...] = dr
    da = dr.astype(BF)
    da_out[...] = da

    @pl.when(i == 0)
    def _():
        dks[...] = jnp.zeros_like(dks)
        dvs[...] = jnp.zeros_like(dvs)
        dg_out[...] = jnp.zeros_like(dg_out)

    dg_out[...] += jnp.broadcast_to(dg, dg_out.shape)
    do = mm_nt(da, wo[...]).astype(BF)
    pairs = wo.shape[0] // 128
    for b in range(blocks):

        @pl.when(blk == b)
        def _(b=b):
            keys = BLK * (b + 1)
            here = slice(b * BLK, b * BLK + BLK)
            bias = mask_bias(segc[...], segr[...], b, keys)
            lse = lser[...]
            for pr in range(pairs):
                cols = slice(pr * 128, pr * 128 + 128)
                qp = qr[0, :, cols]
                kp = kf[0, 0:keys, cols]
                vp = vf[0, 0:keys, cols]
                dop = do[:, cols]
                prod = dop.astype(F32) * orf[:, cols].astype(F32)
                dqs, dss, ps, qs, dos = [], [], [], [], []
                for hh in range(2):
                    hm = half_lane(hh)
                    qh = jnp.where(hm, qp, jnp.zeros_like(qp))
                    doh = jnp.where(hm, dop, jnp.zeros_like(dop))
                    delta = jnp.sum(jnp.where(hm, prod, 0.0), axis=-1, keepdims=True)
                    h = pr * 2 + hh
                    p = jnp.exp(mm_nt(qh, kp) + bias - lse[:, h : h + 1])
                    dp = mm_nt(doh, vp)
                    ds = (p * (dp - delta)).astype(BF)
                    dqs.append(mm(ds, kp))
                    dks[0:keys, cols] += mm_tn(ds, qh)
                    dvs[0:keys, cols] += mm_tn(p.astype(BF), doh)
                dq = jnp.where(half_lane(0), dqs[0], dqs[1]) * 0.125
                dqk_out[:, cols] = dq.astype(BF)
            dqk_out[:, pairs * 128 :] = dks[here, :].astype(BF)
            dv_out[...] = dvs[here, :].astype(BF)

    c = pairs * 128
    dn_out[...] = (
        mm_nt(dqk_out[:, :c], wqkv[0]) + mm_nt(dqk_out[:, c:], wqkv[1]) + mm_nt(dv_out[...], wqkv[2])
    ).astype(BF)


def dense_fwd_kernel(xr, pa, pb, g, up, down, x_out, n_out, act_out, gp_out, p_out):
    x = xr[...] + (pa[...].astype(F32) + pb[...].astype(F32))
    x_out[...] = x
    xh, _ = norm_stats(x)
    n = (xh * g[...]).astype(BF)
    n_out[...] = n
    act, gp = gelu_pair(mm(n, up[...]))
    act = act.astype(BF)
    act_out[...] = act
    gp_out[...] = gp.astype(BF)
    p_out[...] = mm(act, down[...]).astype(BF)


def dense_bwd_kernel(drr, dna, dnb, xn, gn, gp, up, down, dr_out, df_out, du_out, dn_out, dg_out):
    dx, dg = norm_back(xn[...], gn[...], dna[...].astype(F32) + dnb[...].astype(F32))
    dr = drr[...] + dx
    dr_out[...] = dr
    df = dr.astype(BF)
    df_out[...] = df

    @pl.when(pl.program_id(0) == 0)
    def _():
        dg_out[...] = jnp.zeros_like(dg_out)

    dg_out[...] += jnp.broadcast_to(dg, dg_out.shape)
    du = (mm_nt(df, down[...]) * gp[...].astype(F32)).astype(BF)
    du_out[...] = du
    dn_out[...] = mm_nt(du, up[...]).astype(BF)


def final_kernel(h_ref, drr, dna, dnb, xo, xp, gn, dr_out, dg_out):
    i = pl.program_id(0)
    mine = i >= 2
    x = jnp.where(mine, xo[...].astype(F32), xp[...].astype(F32))
    dx, dg = norm_back(x, gn[...], dna[...].astype(F32) + dnb[...].astype(F32))
    dr_out[...] = drr[...] + dx

    @pl.when(i == 0)
    def _():
        dg_out[...] = jnp.zeros_like(dg_out)

    dg_out[...] += jnp.broadcast_to(dg, dg_out.shape)


def spread_kernel(rows_ref, slot_ref, out_ref):
    count = out_ref.shape[0]
    place = lax.broadcasted_iota(jnp.int32, (count, rows_ref.shape[0]), 0)
    place = place + pl.program_id(0) * count
    hot = (place == slot_ref[...]).astype(F32).astype(BF)
    out_ref[...] = mm(hot, rows_ref[...]).astype(BF)


def route_kernel(h_ref, xr, pa, pb, g, slot_ref, x_out, send_out, ms):
    i = pl.program_id(0)
    x = xr[...] + (pa[...].astype(F32) + pb[...].astype(F32))
    x_out[...] = x

    @pl.when(i >= 2)
    def _():
        xh, _ = norm_stats(x)
        rows = pl.ds(pl.multiple_of((i - 2) * BLK, BLK), BLK)
        ms[rows, :] = (xh * g[...]).astype(BF)

    @pl.when(i == 3)
    def _():
        count = send_out.shape[0]
        place = lax.broadcasted_iota(jnp.int32, (count, ms.shape[0]), 0)
        hot = (place == slot_ref[...]).astype(F32).astype(BF)
        send_out[...] = mm(hot, ms[...]).astype(BF)


def collect_kernel(table, slot_ref, out_ref):
    count = table.shape[0]
    place = lax.broadcasted_iota(jnp.int32, (out_ref.shape[0], count), 1)
    hot = (place == slot_ref[...]).astype(F32).astype(BF)
    out_ref[...] = mm(hot, table[...]).astype(BF)


def collect_add_kernel(h_ref, table, slot_ref, x_ref, out_ref):
    count = table.shape[0]
    place = lax.broadcasted_iota(jnp.int32, (out_ref.shape[0], count), 1)
    hot = (place == slot_ref[...]).astype(F32).astype(BF)
    out_ref[...] = (x_ref[...] + mm(hot, table[...])).astype(BF)


def expert_kernel(
    half, mo, mp, go, gp_, cen, up, down,
    yo, yp, dmo, dmp, m_all, dy_all, ae_all, due_all, dc_out,
):
    i = pl.program_id(0)
    first = i < half
    m = jnp.where(first, mo[...], mp[...])
    gb = jnp.where(first, go[...], gp_[...]).astype(F32)
    mf = m.astype(F32)
    cf = cen[...].astype(F32)
    gate = jax.nn.sigmoid(jnp.sum(mf * cf, axis=-1, keepdims=True))
    act, gd = gelu_pair(mm(m, up[0]))
    act = act.astype(BF)
    y = mm(act, down[0])
    dscore = jnp.sum(gb * y, axis=-1, keepdims=True) * gate * (1.0 - gate)
    dy = (gate * gb).astype(BF)
    due = (mm_nt(dy, down[0]) * gd).astype(BF)
    dm = (mm_nt(due, up[0]) + dscore * cf).astype(BF)
    gy = (gate * y).astype(BF)
    m_all[...] = m
    dy_all[...] = dy
    ae_all[...] = act
    due_all[...] = due

    @pl.when(i == 0)
    def _():
        dc_out[...] = jnp.zeros_like(dc_out)

    dc_out[...] += jnp.broadcast_to(jnp.sum(dscore * mf, axis=0, keepdims=True), dc_out.shape)

    @pl.when(first)
    def _():
        yo[...] = gy
        dmo[...] = dm

    @pl.when(jnp.logical_not(first))
    def _():
        yp[...] = gy
        dmp[...] = dm


def shape(dims, kind):
    return jax.ShapeDtypeStruct(dims, kind)


def fixed(dims):
    zero = (0,) * len(dims)
    return pl.BlockSpec(dims, lambda *a: zero, pipeline_mode=pl.Buffered(1))


def rows_spec(width, index=lambda i: i):
    return pl.BlockSpec((BLK, width), lambda i, *a: (index(i), 0))


def call(
    kernel, grid, in_specs, out_specs, outs, scratch, flops, moved, args, prefetch=None, limit=VLIM
):
    params = pltpu.CompilerParams(
        vmem_limit_bytes=int(limit), dimension_semantics=("arbitrary",)
    )
    cost = pl.CostEstimate(flops=int(flops), bytes_accessed=int(moved), transcendentals=0)
    if prefetch is None:
        spec = pl.GridSpec(
            grid=grid, in_specs=in_specs, out_specs=out_specs, scratch_shapes=scratch
        )
    else:
        spec = pltpu.PrefetchScalarGridSpec(
            num_scalar_prefetch=1,
            grid=grid,
            in_specs=in_specs,
            out_specs=out_specs,
            scratch_shapes=scratch,
        )
        args = (prefetch,) + tuple(args)
    return pl.pallas_call(
        kernel, grid_spec=spec, out_shape=outs, compiler_params=params, cost_estimate=cost
    )(*args)


def attention_forward(h, inputs, split, gain, wqkv, wo, segc, segr):
    length, d = segc.shape[0], wqkv.shape[1]
    c = wqkv.shape[2]
    blocks = length // BLK
    if split:
        ins = [rows_spec(d, lambda i: i % (blocks // 2))] * 2
    else:
        ins = [rows_spec(d)] * 3
    ins += [
        fixed((1, d)),
        fixed((3, d, c)),
        fixed((c, d)),
        pl.BlockSpec((BLK, 1), lambda i, *a: (i, 0)),
        fixed((1, length)),
    ]
    outs = [
        (rows_spec(d), shape((length, d), F32)),
        (rows_spec(d), shape((length, d), BF)),
        (pl.BlockSpec((3, BLK, c), lambda i, *a: (0, i, 0)), shape((3, length, c), BF)),
        (rows_spec(c), shape((length, c), BF)),
        (rows_spec(128), shape((length, 128), F32)),
        (rows_spec(d), shape((length, d), BF)),
    ]
    scratch = [pltpu.VMEM((length, c), BF), pltpu.VMEM((length, c), BF)]
    flops = 2 * length * d * c * 4 + 4 * length * length * c
    return call(
        functools.partial(attn_fwd_kernel, blocks, split),
        (blocks,),
        ins,
        [o[0] for o in outs],
        [o[1] for o in outs],
        scratch,
        flops * 2,
        length * d * 20,
        (*inputs, gain, wqkv, wo, segc, segr),
        prefetch=h,
    )


def attention_backward(h, inputs, split, xn, gn, saved, wqkv, wo, segc, segr):
    qkv, o, lse = saved
    length, d = segc.shape[0], wqkv.shape[1]
    c = wqkv.shape[2]
    blocks = length // BLK
    back = lambda i: blocks - 1 - i
    if split:
        ins = [rows_spec(d, lambda i: back(i) % (blocks // 2))] * 4
    else:
        ins = [rows_spec(d, back)] * 3
    part = lambda n: pl.BlockSpec(
        (1, length, c), lambda i, *a: (n, 0, 0), pipeline_mode=pl.Buffered(1)
    )
    ins += [
        rows_spec(d, back),
        fixed((1, d)),
        pl.BlockSpec((1, BLK, c), lambda i, *a: (0, back(i), 0)),
        part(1),
        part(2),
        rows_spec(c, back),
        rows_spec(128, back),
        fixed((3, d, c)),
        fixed((c, d)),
        pl.BlockSpec((BLK, 1), lambda i, *a: (back(i), 0)),
        fixed((1, length)),
    ]
    outs = [
        (rows_spec(d, back), shape((length, d), F32)),
        (rows_spec(d, back), shape((length, d), BF)),
        (rows_spec(2 * c, back), shape((length, 2 * c), BF)),
        (rows_spec(c, back), shape((length, c), BF)),
        (rows_spec(d, back), shape((length, d), BF)),
        (fixed((8, d)), shape((8, d), F32)),
    ]
    scratch = [pltpu.VMEM((length, c), F32), pltpu.VMEM((length, c), F32)]
    flops = 2 * length * d * c * 4 + 10 * length * length * c
    return call(
        functools.partial(attn_bwd_kernel, blocks, split),
        (blocks,),
        ins,
        [s[0] for s in outs],
        [s[1] for s in outs],
        scratch,
        flops * 2,
        length * d * 20,
        (*inputs, xn, gn, qkv, qkv, qkv, o, lse, wqkv, wo, segc, segr),
        prefetch=h,
    )


def dense_forward(x, pa, pb, gain, up, down):
    length, d = x.shape
    f = up.shape[1]
    return call(
        dense_fwd_kernel,
        (length // BLK,),
        [rows_spec(d)] * 3 + [fixed((1, d)), fixed((d, f)), fixed((f, d))],
        [rows_spec(d), rows_spec(d), rows_spec(f), rows_spec(f), rows_spec(d)],
        [
            shape((length, d), F32),
            shape((length, d), BF),
            shape((length, f), BF),
            shape((length, f), BF),
            shape((length, d), BF),
        ],
        [],
        4 * length * d * f,
        length * d * 20 + 4 * d * f,
        (x, pa, pb, gain, up, down),
    )


def dense_backward(dr, dna, dnb, xn, gn, gp, up, down):
    length, d = dr.shape
    f = up.shape[1]
    return call(
        dense_bwd_kernel,
        (length // BLK,),
        [rows_spec(d)] * 4
        + [fixed((1, d)), rows_spec(f), fixed((d, f)), fixed((f, d))],
        [rows_spec(d), rows_spec(d), rows_spec(f), rows_spec(d), fixed((8, d))],
        [
            shape((length, d), F32),
            shape((length, d), BF),
            shape((length, f), BF),
            shape((length, d), BF),
            shape((8, d), F32),
        ],
        [],
        4 * length * d * f,
        length * d * 20 + 4 * d * f,
        (dr, dna, dnb, xn, gn, gp, up, down),
    )


def own_last(blocks):
    return lambda i, h: lax.rem(i + (blocks // 2) * (1 - h[0]), blocks)


def final_step(h, dr, dna, dnb, xo, xp, gn):
    length, d = dr.shape
    blocks = length // BLK
    place = own_last(blocks)
    spec = pl.BlockSpec((BLK, d), lambda i, h: (place(i, h), 0))
    late = lambda i, h: (jnp.maximum(i - blocks // 2, 0), 0)
    return call(
        final_kernel,
        (blocks,),
        [spec] * 3
        + [pl.BlockSpec((BLK, d), late)]
        + [pl.BlockSpec((BLK, d), lambda i, h: (lax.rem(i, blocks // 2), 0)), fixed((1, d))],
        [pl.BlockSpec((BLK, d), late), fixed((8, d))],
        [shape((length // 2, d), F32), shape((8, d), F32)],
        [],
        length * d * 40,
        length * d * 14,
        (dr, dna, dnb, xo, xp, gn),
        prefetch=h,
    )


def route_step(h, x, pa, pb, gain, slot_row, slots):
    length, d = x.shape
    blocks = length // BLK
    place = own_last(blocks)
    spec = pl.BlockSpec((BLK, d), lambda i, h: (place(i, h), 0))
    return call(
        route_kernel,
        (blocks,),
        [spec] * 3 + [fixed((1, d)), fixed((1, length // 2))],
        [spec, fixed((slots, d))],
        [shape((length, d), F32), shape((slots, d), BF)],
        [pltpu.VMEM((length // 2, d), BF)],
        length * slots * d,
        length * d * 14,
        (x, pa, pb, gain, slot_row),
        prefetch=h,
    )


def spread(rows, slot_row, slots):
    count, d = rows.shape
    return call(
        spread_kernel,
        (slots // BLK,),
        [fixed((count, d)), fixed((1, count))],
        [rows_spec(d)],
        [shape((slots, d), BF)],
        [],
        2 * count * slots * d,
        4 * slots * d,
        (rows, slot_row),
    )[0]


def collect(table, slot_col):
    slots, d = table.shape
    count = slot_col.shape[0]
    return call(
        collect_kernel,
        (count // BLK,),
        [fixed((slots, d)), pl.BlockSpec((BLK, 1), lambda i, *a: (i, 0))],
        [rows_spec(d)],
        [shape((count, d), BF)],
        [],
        2 * count * slots * d,
        4 * slots * d,
        (table, slot_col),
    )[0]


def collect_add(h, table, slot_col, x):
    slots, d = table.shape
    count = slot_col.shape[0]
    per = count // BLK
    return call(
        collect_add_kernel,
        (per,),
        [
            fixed((slots, d)),
            pl.BlockSpec((BLK, 1), lambda i, *a: (i, 0)),
            pl.BlockSpec((BLK, d), lambda i, h: (h[0] * per + i, 0)),
        ],
        [rows_spec(d)],
        [shape((count, d), BF)],
        [],
        2 * count * slots * d,
        8 * slots * d,
        (table, slot_col, x),
        prefetch=h,
    )[0]


def expert_step(mo, mp, go, gp, cen, up, down):
    rows, d = mo.shape
    f = up.shape[2]
    half = rows // BLK
    lo = lambda i: jnp.minimum(i, half - 1)
    hi = lambda i: jnp.maximum(i - half, 0)
    return call(
        functools.partial(expert_kernel, half),
        (2 * half,),
        [rows_spec(d, lo), rows_spec(d, hi), rows_spec(d, lo), rows_spec(d, hi)]
        + [fixed((1, d)), fixed((1, d, f)), fixed((1, f, d))],
        [rows_spec(d, lo), rows_spec(d, hi), rows_spec(d, lo), rows_spec(d, hi)]
        + [rows_spec(d), rows_spec(d), rows_spec(f), rows_spec(f), fixed((8, d))],
        [shape((rows, d), BF)] * 4
        + [shape((2 * rows, d), BF)] * 2
        + [shape((2 * rows, f), BF)] * 2
        + [shape((8, d), F32)],
        [],
        16 * rows * d * f,
        rows * d * 24 + rows * f * 8,
        (mo, mp, go, gp, cen, up, down),
    )


def slot_index(chosen, capacity, experts):
    rows = chosen.shape[0]
    matches = chosen[:, None] == jnp.arange(experts, dtype=jnp.int32)[None, :]
    position = jnp.arange(rows, dtype=jnp.int32)
    earlier = (position[None, :] < position[:, None]).astype(BF)
    before = jnp.dot(earlier, matches.astype(BF), preferred_element_type=F32)
    rank = jnp.sum(jnp.where(matches, before, 0.0), axis=1).astype(jnp.int32)
    return chosen * capacity + rank


def swap(v):
    return lax.ppermute(v, "head", SWAP)


def pick(bit, a, b):
    return jnp.where(bit == 1, a, b)


def total_of(a, b):
    return (a.astype(F32) + b.astype(F32)).astype(BF)


def whole(arrays):
    return [pl.BlockSpec(a.shape, lambda i, *r, n=len(a.shape): (0,) * n) for a in arrays]


def one_step(kernel, bits, args, outs):
    moved = sum(a.size * a.dtype.itemsize for a in (*args, *outs))
    return call(
        kernel,
        (1,),
        whole(args),
        whole(outs),
        outs,
        [],
        moved,
        moved,
        args,
        prefetch=bits,
        limit=2 * moved + 8 * 1024 * 1024,
    )


PLACE = {1: 0, 2: 1, 4: 2, 8: 3}


def fold_kernel(plan, n_in, bits, *refs):
    def get(piece):
        at, lo, n = piece
        return refs[at][lo : lo + n, :]

    def put(piece, value):
        at, lo, n = piece
        refs[n_in + at][lo : lo + n, :] = value

    for kind, ins, outs, place in plan:
        if kind == "copy":
            put(outs[0], get(ins[0]))
        elif kind == "sum":
            put(outs[0], total_of(get(ins[0]), get(ins[1])))
        elif kind == "split":
            (ka, kl, n), (ga, gl, _) = ins
            q = n // 2
            lo = total_of(get((ka, kl, q)), get((ga, gl, q)))
            hi = total_of(get((ka, kl + q, q)), get((ga, gl + q, q)))
            put(outs[0], pick(bits[place], lo, hi))
            put(outs[1], pick(bits[place], hi, lo))
        else:
            p, g = get(ins[0]), get(ins[1])
            at, lo, n = outs[0]
            put((at, lo, n // 2), pick(bits[place], g, p))
            put((at, lo + n // 2, n // 2), pick(bits[place], p, g))


class Part:
    def __init__(self, order, send, keep=None):
        self.order, self.phase = order, 0
        self.sent = (send, 0, send.shape[0])
        self.kept = None if keep is None else (keep, 0, keep.shape[0])
        self.got = None
        self.fresh = True

    @property
    def live(self):
        return self.phase < len(self.order)


def halving(order):
    return order + order[::-1]


def advance(bits, parts, during=None, inputs=()):
    parts = [p for p in parts if p.live]
    width = parts[0].sent[0].shape[1]
    buffers = {}
    for p in parts:
        buffers.setdefault(p.order[p.phase], p.sent[0])
    steps = sorted(buffers)
    flat, inputs = lax.optimization_barrier(([buffers[s] for s in steps], inputs))
    got = [lax.ppermute(v, "dp", [(i, i ^ s) for i in range(16)]) for v, s in zip(flat, steps)]
    result = during(*inputs) if during else inputs
    (flat, got), result = lax.optimization_barrier(((flat, got), result))
    for p in parts:
        at = steps.index(p.order[p.phase])
        p.sent = (flat[at],) + p.sent[1:]
        p.got = (got[at],) + p.sent[1:]
        p.phase += 1
    return result


def fold(bits, parts):
    args, plan, rows, moved = [], [], {}, []

    def source(piece):
        for j, a in enumerate(args):
            if a is piece[0]:
                return (j,) + piece[1:]
        args.append(piece[0])
        return (len(args) - 1,) + piece[1:]

    def room(name, n):
        lo = rows.get(name, 0)
        rows[name] = lo + n
        return (name, lo, n)

    for p in parts:
        if not p.live:
            continue
        step = p.order[p.phase]
        half = len(p.order) // 2
        if p.phase == 0:
            ins, kind, place = [source(p.sent)], "copy", 0
            outs = [room(step, p.sent[2])]
        elif p.kept is not None and p.kept[0] is None:
            ins, kind, place = [source(p.sent), source(p.got)], "sum", 0
            outs = [room(step, p.sent[2])]
        elif p.phase < half:
            ins, kind, place = [source(p.kept), source(p.got)], "split", PLACE[step]
            n = p.kept[2] // 2
            outs = [room(step, n), room("keep", n)]
        elif p.phase == half:
            ins, kind, place = [source(p.kept), source(p.got)], "sum", 0
            outs = [room(step, p.kept[2])]
        else:
            ins, kind, place = [source(p.sent), source(p.got)], "raise", PLACE[p.order[p.phase - 1]]
            outs = [room(step, 2 * p.sent[2])]
        plan.append((kind, ins, outs, place))
        moved.append(p)
    names = list(rows)
    width = args[0].shape[1]
    shapes = [shape((rows[n], width), BF) for n in names]
    fixed_plan = tuple(
        (kind, tuple(ins), tuple((names.index(o[0]),) + o[1:] for o in outs), place)
        for kind, ins, outs, place in plan
    )
    made = one_step(functools.partial(fold_kernel, fixed_plan, len(args)), bits, args, shapes)
    for p, (_, _, outs, _) in zip(moved, plan):
        p.sent = (made[names.index(outs[0][0])],) + outs[0][1:]
        if len(outs) > 1:
            p.kept = (made[names.index(outs[1][0])],) + outs[1][1:]


def ends(bits, ref_s, ref_g, piece, place):
    lo, n = piece
    a, b = ref_s[lo : lo + n, :].astype(F32), ref_g[lo : lo + n, :].astype(F32)
    return pick(bits[place], b, a), pick(bits[place], a, b)


def put_query_key(qkv, blocks):
    c = qkv.shape[2]
    n = blocks[0].shape[0]
    for j, block in enumerate(blocks):
        qkv[0, j * n : j * n + n, :] = block[:, :c]
        qkv[1, j * n : j * n + n, :] = block[:, c:]


def put_value_out(qkv, out, v, o):
    c = qkv.shape[2]
    n = v.shape[0]
    qkv[2, :n, :] = v[:, :c]
    qkv[2, n:, :] = v[:, c:]
    out[...] = o


def finish_wide_kernel(at, bits, xp, xg, yp, yg, ap, ag, bp, bg, up, down, qkv, out):
    lo, hi = ends(bits, xp, xg, at[0], 0)
    f = lo.shape[1]
    up[:, :f] = lo
    up[:, f:] = hi
    lo, hi = ends(bits, yp, yg, at[1], 1)
    f = lo.shape[0]
    down[:f, :] = lo
    down[f:, :] = hi
    put_query_key(qkv, ends(bits, ap, ag, at[2], 2))
    put_value_out(qkv, out, *ends(bits, bp, bg, at[3], 3))


def finish_narrow_kernel(at, bits, xp, xg, yp, yg, qkv, out):
    put_query_key(qkv, ends(bits, xp, xg, at[0], 0))
    put_value_out(qkv, out, *ends(bits, yp, yg, at[1], 1))


def stack_kernel(bits, *refs):
    out = refs[-1]
    row = lax.broadcasted_iota(jnp.int32, out.shape, 0)
    total = jnp.zeros(out.shape, F32)
    for j, ref in enumerate(refs[:-1]):
        total = jnp.where(row == j, ref[0:1, :], total)
    out[...] = total.astype(BF)


def finish(kernel, bits, parts, arrays, outs):
    at = tuple((p.sent[1], p.sent[2]) for p in parts)
    return one_step(functools.partial(kernel, at), bits, arrays, outs)


def body(
    steps,
    tokens,
    segment_ids,
    routes,
    norm_gains,
    qkv_one,
    out_one,
    up_one,
    down_one,
    qkv_two,
    out_two,
    expert_up,
    expert_down,
    centroids,
    cotangent,
):
    count, d = tokens.shape
    side = lax.axis_index("head")
    h = side.astype(jnp.int32).reshape(1)
    experts = lax.axis_size("dp") * expert_up.shape[0]
    capacity = 2 * count // experts
    slots = experts * capacity
    gains = norm_gains.astype(F32)
    gain = [gains[j : j + 1] for j in range(4)]
    segc, segr = segment_ids[:, None], segment_ids[None, :]

    chosen = lax.dynamic_slice_in_dim(routes[:, 0], side * count, count, 0)
    flat = slot_index(chosen, capacity, experts)
    slot_row, slot_col = flat[None, :], flat[:, None]

    def travel(v):
        box = v.reshape(experts, capacity, d)
        return lax.all_to_all(box, "dp", 0, 0, tiled=True).reshape(slots, d)

    tokens_peer = swap(tokens)
    x0, n1, qkv1, o1, lse1, p1 = attention_forward(
        h, (tokens, tokens_peer), True, gain[0], qkv_one, out_one, segc, segr
    )
    p1r = swap(p1)
    cot_peer = swap(cotangent)
    grad_own = travel(spread(cotangent, slot_row, slots))
    grad_peer = swap(grad_own)
    x1, n2, act, gp, p2 = dense_forward(x0, p1, p1r, gain[1], up_one, down_one)
    p2r = swap(p2)
    first, n3, qkv2, o2, lse2, p3 = attention_forward(
        h, (x1, p2, p2r), False, gain[2], qkv_two, out_two, segc, segr
    )
    p3r = swap(p3)
    x2, sent = route_step(h, first, p3, p3r, gain[3], slot_row, slots)
    m_own = travel(sent)
    m_peer = swap(m_own)
    yo, yp, dmo, dmp, m_all, dy_all, ae_all, due_all, dc = expert_step(
        m_own, m_peer, grad_own, grad_peer, centroids, expert_up, expert_down
    )
    dm_sum = (dmo.astype(F32) + swap(dmp).astype(F32)).astype(BF)
    up_grad = mm_tn(m_all, due_all)[None]
    down_grad = mm_tn(ae_all, dy_all)[None]
    dm_back, up_grad, down_grad = lax.optimization_barrier((travel(dm_sum), up_grad, down_grad))
    dm_own = collect(dm_back, slot_col)
    dm_peer = swap(dm_own)
    y_sum = (yo.astype(F32) + swap(yp).astype(F32)).astype(BF)
    y_back = travel(y_sum)
    dc = dc[:1]
    cen_grad = dc + swap(dc)

    dr2, da2, dqk2, dv2, dn2, dg3 = attention_backward(
        h,
        (cotangent, cot_peer, dm_own, dm_peer),
        True,
        x2,
        gain[3],
        (qkv2, o2, lse2),
        qkv_two,
        out_two,
        segc,
        segr,
    )
    dn2r = swap(dn2)
    f = up_one.shape[1]
    c = qkv_one.shape[2]

    def grad(a, b):
        return mm_tn(a, b).astype(BF)

    def value_sides(n, dv):
        w = grad(n, dv)
        return jnp.concatenate([w[: d // 2], w[d // 2 :]], axis=1)

    def last_step(dr, dna, dnb):
        return final_step(h, dr, dna, dnb, tokens, tokens_peer, gain[0])

    def gather_y(y):
        return collect_add(h, y, slot_col, x2)

    def stack_gains(dg0):
        return jnp.concatenate([dg0[:1], dg1[:1], dg2[:1], dg3[:1]], axis=0)

    def last_attention(dr, dna, dnb):
        return attention_backward(
            h, (dr, dna, dnb), False, x1, gain[1], (qkv1, o1, lse1), qkv_one, out_one, segc, segr
        )

    if steps is None:
        dr1, df, du, dnd, dg2 = dense_backward(
            dr2, dn2, dn2r, first, gain[2], gp, up_one, down_one
        )
        dr0, da1, dqk1, dv1, dn1, dg1 = last_attention(dr1, dnd, swap(dnd))
        input_grad, dg0 = last_step(dr0, dn1, swap(dn1))
        second = gather_y(y_back)
        up_first, down_first, qk_two, v_two, wo_two, qk_one, v_one, wo_one, gain_grads = lax.psum(
            (
                grad(n2, du),
                grad(act, df),
                grad(n3, dqk2),
                grad(n3, dv2),
                grad(o2, da2),
                grad(n1, dqk1),
                grad(n1, dv1),
                grad(o1, da1),
                stack_gains(dg0),
            ),
            "dp",
        )

        def unpack(qk, v):
            return jnp.stack([qk[:, :c], qk[:, c:], v]).astype(F32)

        up_first, down_first = up_first.astype(F32), down_first.astype(F32)
        qkv_second, out_second = unpack(qk_two, v_two), wo_two.astype(F32)
        qkv_first, out_first = unpack(qk_one, v_one), wo_one.astype(F32)
    else:
        me = lax.axis_index("dp")
        bits = jnp.stack([(me // s) % 2 for s in (1, 2, 4, 8)]).astype(jnp.int32)

        def columns(v, bit):
            half = v.shape[1] // 2
            return lax.dynamic_slice_in_dim(v, bit * half, half, 1)

        def query_key(n, dqk, bit):
            return grad(columns(n, bit), dqk)

        def value_out(n, dv, o, da, bit):
            v, wo = value_sides(n, dv), grad(o, da)
            return jnp.where(bit == 1, v, wo), jnp.where(bit == 1, wo, v)

        qk_send = query_key(n3, dqk2, 1 - bits[2])
        qk_keep = query_key(n3, dqk2, bits[2])
        vo_send, vo_keep = value_out(n3, dv2, o2, da2, bits[3])
        (qk_send, qk_keep, vo_send, vo_keep), dr2, dn2, dn2r, y_back = lax.optimization_barrier(
            ((qk_send, qk_keep, vo_send, vo_keep), dr2, dn2, dn2r, y_back)
        )
        dr1, df, du, dnd, dg2 = dense_backward(
            dr2, dn2, dn2r, first, gain[2], gp, up_one, down_one
        )
        dndr = swap(dnd)

        def gather_all(y, *dgs):
            stacked = one_step(stack_kernel, bits, dgs, [shape((16, d), BF)])[0]
            return gather_y(y), stacked

        def heavy(dr, dna, dnb, n, g, a, b):
            kept = grad(n, columns(g, bits[0])), grad(columns(a, bits[1]), b)
            kept, dr, dna, dnb = lax.optimization_barrier((kept, dr, dna, dnb))
            return last_attention(dr, dna, dnb), *kept

        orders = [halving(o) for o in ((1, 2, 4, 8), (2, 1, 8, 4), (4, 8, 1, 2), (8, 4, 2, 1))]
        big = [
            Part(orders[0], grad(n2, columns(du, 1 - bits[0]))),
            Part(orders[1], grad(columns(act, 1 - bits[1]), df)),
            Part(orders[2], qk_send, qk_keep),
            Part(orders[3], vo_send, vo_keep),
        ]
        last, up_keep, down_keep = advance(bits, big, heavy, (dr1, dnd, dndr, n2, du, act, df))
        dr0, da1, dqk1, dv1, dn1, dg1 = last
        dn1r = swap(dn1)
        big[0].kept, big[1].kept = (up_keep, 0, up_keep.shape[0]), (down_keep, 0, down_keep.shape[0])
        fold(bits, big)

        def narrow_grads(n, dqk, dv, o, da):
            return (
                query_key(n, dqk, 1 - bits[0]),
                query_key(n, dqk, bits[0]),
                value_out(n, dv, o, da, bits[1]),
            )

        qk_send, qk_keep, (vo_send, vo_keep) = advance(
            bits, big, narrow_grads, (n1, dqk1, dv1, o1, da1)
        )
        small = [Part(orders[0], qk_send, qk_keep), Part(orders[1], vo_send, vo_keep)]
        parts = big + small
        fold(bits, parts)
        input_grad, dg0 = advance(bits, parts, last_step, (dr0, dn1, dn1r))
        fold(bits, parts)
        second, gains_own = advance(bits, parts, gather_all, (y_back, dg0, dg1, dg2, dg3))
        tail = Part((1, 2, 4, 8), gains_own)
        tail.kept = (None, 0, 0)
        parts.append(tail)
        while big[0].live:
            fold(bits, parts)
            advance(bits, parts)
        fold(bits, parts)
        arrays = [x for p in big for x in (p.sent[0], p.got[0])]

        def finish_wide(*arrays):
            return finish(
                finish_wide_kernel,
                bits,
                big,
                arrays,
                [
                    shape((d, f), F32),
                    shape((f, d), F32),
                    shape((3, d, c), F32),
                    shape((c, d), F32),
                ],
            )

        up_first, down_first, qkv_second, out_second = advance(bits, small, finish_wide, arrays)
        while small[0].live:
            fold(bits, small)
            advance(bits, small)
        gain_grads = (tail.sent[0], tail.got[0])
        lo = tail.sent[1]
        gain_grads = sum(v[lo : lo + 4].astype(F32) for v in gain_grads)
        qkv_first, out_first = finish(
            finish_narrow_kernel,
            bits,
            small,
            [x for p in small for x in (p.sent[0], p.got[0])],
            [shape((3, d, c), F32), shape((c, d), F32)],
        )
    first_own = lax.dynamic_slice_in_dim(first, side * count, count, 0).astype(BF)
    return (
        first_own,
        second,
        input_grad,
        gain_grads,
        qkv_first,
        out_first,
        up_first,
        down_first,
        qkv_second,
        out_second,
        up_grad,
        down_grad,
        cen_grad,
    )


def solution(mesh):
    rows = P(("dp", "head"), None)
    shared = (
        P(None, None, "head"),
        P("head", None),
        P(None, "head"),
        P("head", None),
        P(None, None, "head"),
        P("head", None),
        P("dp", None, "head"),
        P("dp", "head", None),
        P("dp", None),
    )
    steps = 16 if mesh.shape["dp"] == 16 else None
    return jax.shard_map(
        functools.partial(body, steps),
        mesh=mesh,
        in_specs=(rows, P("dp"), P("dp", None), P(), *shared, rows),
        out_specs=(rows, rows, rows, P(), *shared),
        check_vma=False,
    )
```

```python
import functools

import jax
import jax.numpy as jnp
from jax import lax
from jax.experimental import pallas as pl
from jax.experimental.pallas import tpu as pltpu
from jax.sharding import PartitionSpec as P

BF = jnp.bfloat16
F32 = jnp.float32
EPS = 1e-05
MASKED = -1e30
BLK = 256
HEAD_DIM = 64
SWAP = [(0, 1), (1, 0)]
VLIM = 56 * 1024 * 1024
SMALL = 16 * 1024 * 1024


def mm(a, b):
    return lax.dot_general(a, b, (((1,), (0,)), ((), ())), preferred_element_type=F32)


def mm_nt(a, b):
    return lax.dot_general(a, b, (((1,), (1,)), ((), ())), preferred_element_type=F32)


def mm_tn(a, b):
    return lax.dot_general(a, b, (((0,), (0,)), ((), ())), preferred_element_type=F32)


def norm_stats(x):
    c = x - jnp.mean(x, axis=-1, keepdims=True)
    r = lax.rsqrt(jnp.mean(c * c, axis=-1, keepdims=True) + EPS)
    return c * r, r


def norm_back(x, gain, dn):
    xh, r = norm_stats(x)
    dxh = dn * gain
    a = jnp.mean(dxh, axis=-1, keepdims=True)
    b = jnp.mean(dxh * xh, axis=-1, keepdims=True)
    return r * (dxh - a - xh * b), jnp.sum(dn * xh, axis=0, keepdims=True)


def gelu_pair(u):
    z = jnp.abs(u) * 0.7071067811865476
    t = 1.0 / (1.0 + 0.3275911 * z)
    ex = jnp.exp(-(z * z))
    poly = t * (
        0.254829592
        + t * (-0.284496736 + t * (1.421413741 + t * (-1.453152027 + t * 1.061405429)))
    )
    tail = 0.5 * poly * ex
    phi = jnp.where(u >= 0.0, 1.0 - tail, tail)
    return u * phi, phi + u * (ex * 0.3989422804014327)


def mask_bias(segc, segr, b, keys):
    row = lax.broadcasted_iota(jnp.int32, (BLK, keys), 0) + b * BLK
    col = lax.broadcasted_iota(jnp.int32, (BLK, keys), 1)
    return jnp.where((segc == segr[:, :keys]) & (col <= row), 0.0, MASKED)


def half_lane(hh):
    lane = lax.broadcasted_iota(jnp.int32, (BLK, 128), 1)
    return (lane >= 64) if hh else (lane < 64)


def residual_of(xr, pa, pb):
    return xr[...].astype(F32) + (pa[...].astype(F32) + pb[...].astype(F32))


def attn_fwd_kernel(blocks, split, h_ref, *refs):
    if split:
        own, peer, g, wqkv, wo, segc, segr = refs[:7]
        outs = refs[7:]
    else:
        xr, pa, pb, g, wqkv, wo, segc, segr = refs[:8]
        outs = refs[8:]
    x_out = None
    if not split:
        x_out, *outs = outs
    n_out, qkv_out, o_out, lse_out, p_out, ks, vs = outs
    i = pl.program_id(0)
    if split:
        mine = (i // (blocks // 2)) == h_ref[0]
        x = jnp.where(mine, own[...].astype(F32), peer[...].astype(F32))
    else:
        x = residual_of(xr, pa, pb)
        x_out[...] = x.astype(BF)
    xh, _ = norm_stats(x)
    n = (xh * g[...]).astype(BF)
    n_out[...] = n
    q = (mm(n, wqkv[0]).astype(BF).astype(F32) * 0.125).astype(BF)
    k = mm(n, wqkv[1]).astype(BF)
    v = mm(n, wqkv[2]).astype(BF)
    qkv_out[0] = q
    qkv_out[1] = k
    qkv_out[2] = v
    rows = pl.ds(pl.multiple_of(i * BLK, BLK), BLK)
    ks[rows, :] = k
    vs[rows, :] = v
    pairs = q.shape[1] // 128
    for b in range(blocks):

        @pl.when(i == b)
        def _(b=b):
            keys = BLK * (b + 1)
            bias = mask_bias(segc[...], segr[...], b, keys)
            lse = jnp.zeros((BLK, 128), F32)
            lanes = lax.broadcasted_iota(jnp.int32, (BLK, 128), 1)
            total = jnp.zeros((BLK, wo.shape[1]), F32)
            for pr in range(pairs):
                cols = slice(pr * 128, pr * 128 + 128)
                qp = qkv_out[0, :, cols]
                kp = ks[0:keys, cols]
                vp = vs[0:keys, cols]
                res = []
                for hh in range(2):
                    qh = jnp.where(half_lane(hh), qp, jnp.zeros_like(qp))
                    s = mm_nt(qh, kp) + bias
                    m = jnp.max(s, axis=-1, keepdims=True)
                    e = jnp.exp(s - m)
                    l = jnp.sum(e, axis=-1, keepdims=True)
                    res.append(mm(e.astype(BF), vp) * (1.0 / l))
                    lse = jnp.where(lanes == pr * 2 + hh, m + jnp.log(l), lse)
                ob = jnp.where(half_lane(0), res[0], res[1]).astype(BF)
                o_out[:, cols] = ob
                total = total + mm(ob, wo[cols, :])
            lse_out[...] = lse
            p_out[...] = total.astype(BF)


def attn_bwd_kernel(blocks, split, h_ref, *refs):
    if split:
        dro, drp, dno, dnp_ = refs[:4]
    else:
        drr, dna, dnb = refs[:3]
    if split:
        xr, pa, pb = refs[4:7]
        xn = residual_of(xr, pa, pb)
        rest = refs[7:]
    else:
        xn = refs[3][...].astype(F32)
        rest = refs[4:]
    gn, qr, kf, vf, orf, lser, wqkv, wo, segc, segr = rest[:10]
    da_out, dqk_out, dv_out, dn_out, dg_out, dks, dvs = rest[10:]
    i = pl.program_id(0)
    blk = blocks - 1 - i
    if split:
        mine = (blk // (blocks // 2)) == h_ref[0]
        dr = jnp.where(mine, dro[...].astype(F32), drp[...].astype(F32))
        dn = jnp.where(mine, dno[...].astype(F32), dnp_[...].astype(F32))
    else:
        dr = drr[...].astype(F32)
        dn = dna[...].astype(F32) + dnb[...].astype(F32)
    dx, dg = norm_back(xn, gn[...], dn)
    da = (dr + dx).astype(BF)
    da_out[...] = da

    @pl.when(i == 0)
    def _():
        dks[...] = jnp.zeros_like(dks)
        dvs[...] = jnp.zeros_like(dvs)
        dg_out[...] = jnp.zeros_like(dg_out)

    dg_out[...] += jnp.broadcast_to(dg, dg_out.shape)
    do = mm_nt(da, wo[...]).astype(BF)
    pairs = wo.shape[0] // 128
    for b in range(blocks):

        @pl.when(blk == b)
        def _(b=b):
            keys = BLK * (b + 1)
            here = slice(b * BLK, b * BLK + BLK)
            bias = mask_bias(segc[...], segr[...], b, keys)
            lse = lser[...]
            for pr in range(pairs):
                cols = slice(pr * 128, pr * 128 + 128)
                qp = qr[0, :, cols]
                kp = kf[0, 0:keys, cols]
                vp = vf[0, 0:keys, cols]
                dop = do[:, cols]
                prod = dop.astype(F32) * orf[:, cols].astype(F32)
                dqs, dss, ps, qs, dos = [], [], [], [], []
                for hh in range(2):
                    hm = half_lane(hh)
                    qh = jnp.where(hm, qp, jnp.zeros_like(qp))
                    doh = jnp.where(hm, dop, jnp.zeros_like(dop))
                    delta = jnp.sum(jnp.where(hm, prod, 0.0), axis=-1, keepdims=True)
                    h = pr * 2 + hh
                    p = jnp.exp(mm_nt(qh, kp) + bias - lse[:, h : h + 1])
                    dp = mm_nt(doh, vp)
                    ds = (p * (dp - delta)).astype(BF)
                    dqs.append(mm(ds, kp))
                    dks[0:keys, cols] += mm_tn(ds, qh)
                    dvs[0:keys, cols] += mm_tn(p.astype(BF), doh)
                dq = jnp.where(half_lane(0), dqs[0], dqs[1]) * 0.125
                dqk_out[:, cols] = dq.astype(BF)
            dqk_out[:, pairs * 128 :] = dks[here, :].astype(BF)
            dv_out[...] = dvs[here, :].astype(BF)

    c = pairs * 128
    dn_out[...] = (
        mm_nt(dqk_out[:, :c], wqkv[0]) + mm_nt(dqk_out[:, c:], wqkv[1]) + mm_nt(dv_out[...], wqkv[2])
    ).astype(BF)


def dense_fwd_kernel(
    blocks, h_ref, own, peer, pa, pb, g, up, down, x_out, n_out, act_out, gp_out, p_out
):
    mine = (pl.program_id(0) // (blocks // 2)) == h_ref[0]
    x = jnp.where(mine, own[...].astype(F32), peer[...].astype(F32))
    x = x + (pa[...].astype(F32) + pb[...].astype(F32))
    x_out[...] = x.astype(BF)
    xh, _ = norm_stats(x)
    n = (xh * g[...]).astype(BF)
    n_out[...] = n
    act, gp = gelu_pair(mm(n, up[...]))
    act = act.astype(BF)
    act_out[...] = act
    gp_out[...] = gp.astype(BF)
    p_out[...] = mm(act, down[...]).astype(BF)


def dense_bwd_kernel(drr, dna, dnb, xn, gn, gp, up, down, df_out, du_out, dn_out, dg_out):
    dx, dg = norm_back(xn[...].astype(F32), gn[...], dna[...].astype(F32) + dnb[...].astype(F32))
    df = (drr[...].astype(F32) + dx).astype(BF)
    df_out[...] = df

    @pl.when(pl.program_id(0) == 0)
    def _():
        dg_out[...] = jnp.zeros_like(dg_out)

    dg_out[...] += jnp.broadcast_to(dg, dg_out.shape)
    du = (mm_nt(df, down[...]) * gp[...].astype(F32)).astype(BF)
    du_out[...] = du
    dn_out[...] = mm_nt(du, up[...]).astype(BF)


def final_kernel(h_ref, drr, dna, dnb, xo, xp, gn, dr_out, dg_out):
    i = pl.program_id(0)
    mine = i >= 2
    x = jnp.where(mine, xo[...].astype(F32), xp[...].astype(F32))
    dx, dg = norm_back(x, gn[...], dna[...].astype(F32) + dnb[...].astype(F32))
    dr_out[...] = drr[...].astype(F32) + dx

    @pl.when(i == 0)
    def _():
        dg_out[...] = jnp.zeros_like(dg_out)

    dg_out[...] += jnp.broadcast_to(dg, dg_out.shape)


def spread_kernel(rows_ref, slot_ref, out_ref):
    count = out_ref.shape[0]
    place = lax.broadcasted_iota(jnp.int32, (count, rows_ref.shape[0]), 0)
    place = place + pl.program_id(0) * count
    hot = (place == slot_ref[...]).astype(F32).astype(BF)
    out_ref[...] = mm(hot, rows_ref[...]).astype(BF)


def route_kernel(h_ref, xr, pa, pb, g, slot_ref, x_out, send_out, ms):
    i = pl.program_id(0)
    x = residual_of(xr, pa, pb)
    x_out[...] = x
    xh, _ = norm_stats(x)
    rows = pl.ds(pl.multiple_of(i * BLK, BLK), BLK)
    ms[rows, :] = (xh * g[...]).astype(BF)

    @pl.when(i == pl.num_programs(0) - 1)
    def _():
        count = send_out.shape[0]
        place = lax.broadcasted_iota(jnp.int32, (count, ms.shape[0]), 0)
        hot = (place == slot_ref[...]).astype(F32).astype(BF)
        send_out[...] = mm(hot, ms[...]).astype(BF)


def collect_kernel(table, slot_ref, out_ref):
    count = table.shape[0]
    place = lax.broadcasted_iota(jnp.int32, (out_ref.shape[0], count), 1)
    hot = (place == slot_ref[...]).astype(F32).astype(BF)
    out_ref[...] = mm(hot, table[...]).astype(BF)


def collect_add_kernel(h_ref, table, slot_ref, x_ref, out_ref):
    count = table.shape[0]
    place = lax.broadcasted_iota(jnp.int32, (out_ref.shape[0], count), 1)
    hot = (place == slot_ref[...]).astype(F32).astype(BF)
    out_ref[...] = (x_ref[...] + mm(hot, table[...])).astype(BF)


def expert_kernel(
    half, mo, mp, go, gp_, cen, up, down,
    yo, yp, dmo, dmp, m_all, dy_all, ae_all, due_all, dc_out,
):
    i = pl.program_id(0)
    first = i < half
    m = jnp.where(first, mo[...], mp[...])
    gb = jnp.where(first, go[...], gp_[...]).astype(F32)
    mf = m.astype(F32)
    cf = cen[...].astype(F32)
    gate = jax.nn.sigmoid(jnp.sum(mf * cf, axis=-1, keepdims=True))
    dy = (gate * gb).astype(BF)
    u = mm(m, up[0])
    dact = mm_nt(dy, down[0])
    act, gd = gelu_pair(u)
    act = act.astype(BF)
    y = mm(act, down[0])
    dscore = jnp.sum(gb * y, axis=-1, keepdims=True) * gate * (1.0 - gate)
    due = (dact * gd).astype(BF)
    dm = (mm_nt(due, up[0]) + dscore * cf).astype(BF)
    gy = (gate * y).astype(BF)
    m_all[...] = m
    dy_all[...] = dy
    ae_all[...] = act
    due_all[...] = due

    @pl.when(i == 0)
    def _():
        dc_out[...] = jnp.zeros_like(dc_out)

    dc_out[...] += jnp.broadcast_to(jnp.sum(dscore * mf, axis=0, keepdims=True), dc_out.shape)

    @pl.when(first)
    def _():
        yo[...] = gy
        dmo[...] = dm

    @pl.when(jnp.logical_not(first))
    def _():
        yp[...] = gy
        dmp[...] = dm


def shape(dims, kind):
    return jax.ShapeDtypeStruct(dims, kind)


def fixed(dims):
    zero = (0,) * len(dims)
    return pl.BlockSpec(dims, lambda *a: zero, pipeline_mode=pl.Buffered(1))


def rows_spec(width, index=lambda i: i):
    return pl.BlockSpec((BLK, width), lambda i, *a: (index(i), 0))


def call(
    kernel, grid, in_specs, out_specs, outs, scratch, flops, moved, args, prefetch=None, limit=VLIM
):
    params = pltpu.CompilerParams(
        vmem_limit_bytes=int(limit), dimension_semantics=("arbitrary",)
    )
    cost = pl.CostEstimate(flops=int(flops), bytes_accessed=int(moved), transcendentals=0)
    if prefetch is None:
        spec = pl.GridSpec(
            grid=grid, in_specs=in_specs, out_specs=out_specs, scratch_shapes=scratch
        )
    else:
        spec = pltpu.PrefetchScalarGridSpec(
            num_scalar_prefetch=1,
            grid=grid,
            in_specs=in_specs,
            out_specs=out_specs,
            scratch_shapes=scratch,
        )
        args = (prefetch,) + tuple(args)
    return pl.pallas_call(
        kernel, grid_spec=spec, out_shape=outs, compiler_params=params, cost_estimate=cost
    )(*args)


def attention_forward(h, inputs, split, gain, wqkv, wo, segc, segr):
    length, d = segc.shape[0], wqkv.shape[1]
    c = wqkv.shape[2]
    blocks = length // BLK
    if split:
        ins = [rows_spec(d, lambda i: i % (blocks // 2))] * 2
    else:
        ins = [rows_spec(d)] * 3
    ins += [
        fixed((1, d)),
        fixed((3, d, c)),
        fixed((c, d)),
        pl.BlockSpec((BLK, 1), lambda i, *a: (i, 0)),
        fixed((1, length)),
    ]
    outs = [] if split else [(rows_spec(d), shape((length, d), BF))]
    outs += [
        (rows_spec(d), shape((length, d), BF)),
        (pl.BlockSpec((3, BLK, c), lambda i, *a: (0, i, 0)), shape((3, length, c), BF)),
        (rows_spec(c), shape((length, c), BF)),
        (rows_spec(128), shape((length, 128), F32)),
        (rows_spec(d), shape((length, d), BF)),
    ]
    scratch = [pltpu.VMEM((length, c), BF), pltpu.VMEM((length, c), BF)]
    flops = 2 * length * d * c * 4 + 4 * length * length * c
    return call(
        functools.partial(attn_fwd_kernel, blocks, split),
        (blocks,),
        ins,
        [o[0] for o in outs],
        [o[1] for o in outs],
        scratch,
        flops * 2,
        length * d * 20,
        (*inputs, gain, wqkv, wo, segc, segr),
        prefetch=h,
    )


def attention_backward(h, inputs, split, gn, saved, wqkv, wo, segc, segr):
    qkv, o, lse = saved
    length, d = segc.shape[0], wqkv.shape[1]
    c = wqkv.shape[2]
    blocks = length // BLK
    back = lambda i: blocks - 1 - i
    if split:
        ins = [rows_spec(d, lambda i: back(i) % (blocks // 2))] * 4 + [rows_spec(d, back)] * 3
    else:
        ins = [rows_spec(d, back)] * 4
    part = lambda n: pl.BlockSpec(
        (1, length, c), lambda i, *a: (n, 0, 0), pipeline_mode=pl.Buffered(1)
    )
    ins += [
        fixed((1, d)),
        pl.BlockSpec((1, BLK, c), lambda i, *a: (0, back(i), 0)),
        part(1),
        part(2),
        rows_spec(c, back),
        rows_spec(128, back),
        fixed((3, d, c)),
        fixed((c, d)),
        pl.BlockSpec((BLK, 1), lambda i, *a: (back(i), 0)),
        fixed((1, length)),
    ]
    outs = [
        (rows_spec(d, back), shape((length, d), BF)),
        (rows_spec(2 * c, back), shape((length, 2 * c), BF)),
        (rows_spec(c, back), shape((length, c), BF)),
        (rows_spec(d, back), shape((length, d), BF)),
        (fixed((8, d)), shape((8, d), F32)),
    ]
    scratch = [pltpu.VMEM((length, c), F32), pltpu.VMEM((length, c), F32)]
    flops = 2 * length * d * c * 4 + 10 * length * length * c
    return call(
        functools.partial(attn_bwd_kernel, blocks, split),
        (blocks,),
        ins,
        [s[0] for s in outs],
        [s[1] for s in outs],
        scratch,
        flops * 2,
        length * d * 20,
        (*inputs, gn, qkv, qkv, qkv, o, lse, wqkv, wo, segc, segr),
        prefetch=h,
    )


def dense_forward(h, own, peer, pa, pb, gain, up, down):
    length, d = pa.shape
    f = up.shape[1]
    blocks = length // BLK
    half = rows_spec(d, lambda i: lax.rem(i, blocks // 2))
    return call(
        functools.partial(dense_fwd_kernel, blocks),
        (blocks,),
        [half] * 2 + [rows_spec(d)] * 2 + [fixed((1, d)), fixed((d, f)), fixed((f, d))],
        [rows_spec(d), rows_spec(d), rows_spec(f), rows_spec(f), rows_spec(d)],
        [
            shape((length, d), BF),
            shape((length, d), BF),
            shape((length, f), BF),
            shape((length, f), BF),
            shape((length, d), BF),
        ],
        [],
        4 * length * d * f,
        length * d * 20 + 4 * d * f,
        (own, peer, pa, pb, gain, up, down),
        prefetch=h,
    )


def dense_backward(dr, dna, dnb, xn, gn, gp, up, down):
    length, d = dr.shape
    f = up.shape[1]
    return call(
        dense_bwd_kernel,
        (length // BLK,),
        [rows_spec(d)] * 4
        + [fixed((1, d)), rows_spec(f), fixed((d, f)), fixed((f, d))],
        [rows_spec(d), rows_spec(f), rows_spec(d), fixed((8, d))],
        [
            shape((length, d), BF),
            shape((length, f), BF),
            shape((length, d), BF),
            shape((8, d), F32),
        ],
        [],
        4 * length * d * f,
        length * d * 20 + 4 * d * f,
        (dr, dna, dnb, xn, gn, gp, up, down),
    )


def own_last(blocks):
    return lambda i, h: lax.rem(i + (blocks // 2) * (1 - h[0]), blocks)


def final_step(h, dr, dna, dnb, xo, xp, gn):
    length, d = dr.shape
    blocks = length // BLK
    place = own_last(blocks)
    spec = pl.BlockSpec((BLK, d), lambda i, h: (place(i, h), 0))
    late = lambda i, h: (jnp.maximum(i - blocks // 2, 0), 0)
    return call(
        final_kernel,
        (blocks,),
        [spec] * 3
        + [pl.BlockSpec((BLK, d), late)]
        + [pl.BlockSpec((BLK, d), lambda i, h: (lax.rem(i, blocks // 2), 0)), fixed((1, d))],
        [pl.BlockSpec((BLK, d), late), fixed((8, d))],
        [shape((length // 2, d), F32), shape((8, d), F32)],
        [],
        length * d * 40,
        length * d * 14,
        (dr, dna, dnb, xo, xp, gn),
        prefetch=h,
        limit=SMALL,
    )


def route_step(h, x, pa, pb, gain, slot_row, slots):
    length, d = x.shape
    per = length // 2 // BLK
    spec = pl.BlockSpec((BLK, d), lambda i, h: (h[0] * per + i, 0))
    return call(
        route_kernel,
        (per,),
        [spec] * 3 + [fixed((1, d)), fixed((1, length // 2))],
        [rows_spec(d), fixed((slots, d))],
        [shape((length // 2, d), F32), shape((slots, d), BF)],
        [pltpu.VMEM((length // 2, d), BF)],
        length * slots * d,
        length * d * 14,
        (x, pa, pb, gain, slot_row),
        prefetch=h,
        limit=SMALL,
    )


def spread(rows, slot_row, slots):
    count, d = rows.shape
    return call(
        spread_kernel,
        (slots // BLK,),
        [fixed((count, d)), fixed((1, count))],
        [rows_spec(d)],
        [shape((slots, d), BF)],
        [],
        2 * count * slots * d,
        4 * slots * d,
        (rows, slot_row),
        limit=SMALL,
    )[0]


def collect(table, slot_col):
    slots, d = table.shape
    count = slot_col.shape[0]
    return call(
        collect_kernel,
        (count // BLK,),
        [fixed((slots, d)), pl.BlockSpec((BLK, 1), lambda i, *a: (i, 0))],
        [rows_spec(d)],
        [shape((count, d), BF)],
        [],
        2 * count * slots * d,
        4 * slots * d,
        (table, slot_col),
        limit=SMALL,
    )[0]


def collect_add(h, table, slot_col, x):
    slots, d = table.shape
    count = slot_col.shape[0]
    per = count // BLK
    return call(
        collect_add_kernel,
        (per,),
        [
            fixed((slots, d)),
            pl.BlockSpec((BLK, 1), lambda i, *a: (i, 0)),
            rows_spec(d),
        ],
        [rows_spec(d)],
        [shape((count, d), BF)],
        [],
        2 * count * slots * d,
        8 * slots * d,
        (table, slot_col, x),
        prefetch=h,
        limit=SMALL,
    )[0]


def expert_step(mo, mp, go, gp, cen, up, down):
    rows, d = mo.shape
    f = up.shape[2]
    half = rows // BLK
    lo = lambda i: jnp.minimum(i, half - 1)
    hi = lambda i: jnp.maximum(i - half, 0)
    return call(
        functools.partial(expert_kernel, half),
        (2 * half,),
        [rows_spec(d, lo), rows_spec(d, hi), rows_spec(d, lo), rows_spec(d, hi)]
        + [fixed((1, d)), fixed((1, d, f)), fixed((1, f, d))],
        [rows_spec(d, lo), rows_spec(d, hi), rows_spec(d, lo), rows_spec(d, hi)]
        + [rows_spec(d), rows_spec(d), rows_spec(f), rows_spec(f), fixed((8, d))],
        [shape((rows, d), BF)] * 4
        + [shape((2 * rows, d), BF)] * 2
        + [shape((2 * rows, f), BF)] * 2
        + [shape((8, d), F32)],
        [],
        16 * rows * d * f,
        rows * d * 24 + rows * f * 8,
        (mo, mp, go, gp, cen, up, down),
    )


def slot_index(chosen, capacity, experts):
    rows = chosen.shape[0]
    matches = chosen[:, None] == jnp.arange(experts, dtype=jnp.int32)[None, :]
    position = jnp.arange(rows, dtype=jnp.int32)
    earlier = (position[None, :] < position[:, None]).astype(BF)
    before = jnp.dot(earlier, matches.astype(BF), preferred_element_type=F32)
    rank = jnp.sum(jnp.where(matches, before, 0.0), axis=1).astype(jnp.int32)
    return chosen * capacity + rank


def swap(v):
    return lax.ppermute(v, "head", SWAP)


def pick(bit, a, b):
    return jnp.where(bit == 1, a, b)


def total_of(a, b):
    return (a.astype(F32) + b.astype(F32)).astype(BF)


def whole(arrays):
    return [pl.BlockSpec(a.shape, lambda i, *r, n=len(a.shape): (0,) * n) for a in arrays]


def one_step(kernel, bits, args, outs):
    moved = sum(a.size * a.dtype.itemsize for a in (*args, *outs))
    return call(
        kernel,
        (1,),
        whole(args),
        whole(outs),
        outs,
        [],
        moved,
        moved,
        args,
        prefetch=bits,
        limit=2 * moved + 8 * 1024 * 1024,
    )


def sum_kernel(h_ref, a, b, out):
    out[...] = total_of(a[...], b[...])


PLACE = {1: 0, 2: 1, 4: 2, 8: 3}


def fold_kernel(plan, n_in, bits, *refs):
    def get(piece):
        at, lo, n = piece
        return refs[at][lo : lo + n, :]

    def put(piece, value):
        at, lo, n = piece
        refs[n_in + at][lo : lo + n, :] = value

    for kind, ins, outs, place in plan:
        if kind == "copy":
            put(outs[0], get(ins[0]))
        elif kind == "sum":
            put(outs[0], total_of(get(ins[0]), get(ins[1])))
        elif kind == "split":
            (ka, kl, n), (ga, gl, _) = ins
            q = n // 2
            lo = total_of(get((ka, kl, q)), get((ga, gl, q)))
            hi = total_of(get((ka, kl + q, q)), get((ga, gl + q, q)))
            put(outs[0], pick(bits[place], lo, hi))
            put(outs[1], pick(bits[place], hi, lo))
        else:
            p, g = get(ins[0]), get(ins[1])
            at, lo, n = outs[0]
            put((at, lo, n // 2), pick(bits[place], g, p))
            put((at, lo + n // 2, n // 2), pick(bits[place], p, g))


class Part:
    def __init__(self, order, send, keep=None):
        self.order, self.phase = order, 0
        self.sent = (send, 0, send.shape[0])
        self.kept = None if keep is None else (keep, 0, keep.shape[0])
        self.got = None
        self.fresh = True

    @property
    def live(self):
        return self.phase < len(self.order)


def halving(order):
    return order + order[::-1]


def advance(bits, parts, during=None, inputs=()):
    parts = [p for p in parts if p.live]
    width = parts[0].sent[0].shape[1]
    buffers = {}
    for p in parts:
        buffers.setdefault(p.order[p.phase], p.sent[0])
    steps = sorted(buffers)
    flat, inputs = lax.optimization_barrier(([buffers[s] for s in steps], inputs))
    got = [lax.ppermute(v, "dp", [(i, i ^ s) for i in range(16)]) for v, s in zip(flat, steps)]
    result = during(*inputs) if during else inputs
    (flat, got), result = lax.optimization_barrier(((flat, got), result))
    for p in parts:
        at = steps.index(p.order[p.phase])
        p.sent = (flat[at],) + p.sent[1:]
        p.got = (got[at],) + p.sent[1:]
        p.phase += 1
    return result


def fold(bits, parts):
    args, plan, rows, moved = [], [], {}, []

    def source(piece):
        for j, a in enumerate(args):
            if a is piece[0]:
                return (j,) + piece[1:]
        args.append(piece[0])
        return (len(args) - 1,) + piece[1:]

    def room(name, n):
        lo = rows.get(name, 0)
        rows[name] = lo + n
        return (name, lo, n)

    for p in parts:
        if not p.live:
            continue
        step = p.order[p.phase]
        half = len(p.order) // 2
        if p.phase == 0:
            ins, kind, place = [source(p.sent)], "copy", 0
            outs = [room(step, p.sent[2])]
        elif p.kept is not None and p.kept[0] is None:
            ins, kind, place = [source(p.sent), source(p.got)], "sum", 0
            outs = [room(step, p.sent[2])]
        elif p.phase < half:
            ins, kind, place = [source(p.kept), source(p.got)], "split", PLACE[step]
            n = p.kept[2] // 2
            outs = [room(step, n), room("keep", n)]
        elif p.phase == half:
            ins, kind, place = [source(p.kept), source(p.got)], "sum", 0
            outs = [room(step, p.kept[2])]
        else:
            ins, kind, place = [source(p.sent), source(p.got)], "raise", PLACE[p.order[p.phase - 1]]
            outs = [room(step, 2 * p.sent[2])]
        plan.append((kind, ins, outs, place))
        moved.append(p)
    names = list(rows)
    width = args[0].shape[1]
    shapes = [shape((rows[n], width), BF) for n in names]
    fixed_plan = tuple(
        (kind, tuple(ins), tuple((names.index(o[0]),) + o[1:] for o in outs), place)
        for kind, ins, outs, place in plan
    )
    made = one_step(functools.partial(fold_kernel, fixed_plan, len(args)), bits, args, shapes)
    for p, (_, _, outs, _) in zip(moved, plan):
        p.sent = (made[names.index(outs[0][0])],) + outs[0][1:]
        if len(outs) > 1:
            p.kept = (made[names.index(outs[1][0])],) + outs[1][1:]


def ends(bits, ref_s, ref_g, piece, place):
    lo, n = piece
    a, b = ref_s[lo : lo + n, :].astype(F32), ref_g[lo : lo + n, :].astype(F32)
    return pick(bits[place], b, a), pick(bits[place], a, b)


def put_query_key(qkv, blocks):
    c = qkv.shape[2]
    n = blocks[0].shape[0]
    for j, block in enumerate(blocks):
        qkv[0, j * n : j * n + n, :] = block[:, :c]
        qkv[1, j * n : j * n + n, :] = block[:, c:]


def put_value_out(qkv, out, v, o):
    c = qkv.shape[2]
    n = v.shape[0]
    qkv[2, :n, :] = v[:, :c]
    qkv[2, n:, :] = v[:, c:]
    out[...] = o


def finish_wide_kernel(at, bits, xp, xg, yp, yg, ap, ag, bp, bg, up, down, qkv, out):
    lo, hi = ends(bits, xp, xg, at[0], 0)
    f = lo.shape[1]
    up[:, :f] = lo
    up[:, f:] = hi
    lo, hi = ends(bits, yp, yg, at[1], 1)
    f = lo.shape[0]
    down[:f, :] = lo
    down[f:, :] = hi
    put_query_key(qkv, ends(bits, ap, ag, at[2], 2))
    put_value_out(qkv, out, *ends(bits, bp, bg, at[3], 3))


def finish_narrow_kernel(at, bits, xp, xg, yp, yg, qkv, out):
    put_query_key(qkv, ends(bits, xp, xg, at[0], 0))
    put_value_out(qkv, out, *ends(bits, yp, yg, at[1], 1))


def stack_kernel(bits, *refs):
    out = refs[-1]
    row = lax.broadcasted_iota(jnp.int32, out.shape, 0)
    total = jnp.zeros(out.shape, F32)
    for j, ref in enumerate(refs[:-1]):
        total = jnp.where(row == j, ref[0:1, :], total)
    out[...] = total.astype(BF)


def finish(kernel, bits, parts, arrays, outs):
    at = tuple((p.sent[1], p.sent[2]) for p in parts)
    return one_step(functools.partial(kernel, at), bits, arrays, outs)


def body(
    steps,
    tokens,
    segment_ids,
    routes,
    norm_gains,
    qkv_one,
    out_one,
    up_one,
    down_one,
    qkv_two,
    out_two,
    expert_up,
    expert_down,
    centroids,
    cotangent,
):
    count, d = tokens.shape
    side = lax.axis_index("head")
    h = side.astype(jnp.int32).reshape(1)
    experts = lax.axis_size("dp") * expert_up.shape[0]
    capacity = 2 * count // experts
    slots = experts * capacity
    gains = norm_gains.astype(F32)
    gain = [gains[j : j + 1] for j in range(4)]
    segc, segr = segment_ids[:, None], segment_ids[None, :]

    chosen = lax.dynamic_slice_in_dim(routes[:, 0], side * count, count, 0)
    flat = slot_index(chosen, capacity, experts)
    slot_row, slot_col = flat[None, :], flat[:, None]

    def travel(v):
        box = v.reshape(experts, capacity, d)
        return lax.all_to_all(box, "dp", 0, 0, tiled=True).reshape(slots, d)

    def add(a, b):
        return one_step(sum_kernel, h, (a, b), [shape(a.shape, BF)])[0]

    tokens_peer = swap(tokens)
    n1, qkv1, o1, lse1, p1 = attention_forward(
        h, (tokens, tokens_peer), True, gain[0], qkv_one, out_one, segc, segr
    )
    p1r = swap(p1)
    cot_peer = swap(cotangent)
    p1r, cot_table = lax.optimization_barrier((p1r, spread(cotangent, slot_row, slots)))
    grad_own = travel(cot_table)
    grad_peer = swap(grad_own)
    x1, n2, act, gp, p2 = dense_forward(
        h, tokens, tokens_peer, p1, p1r, gain[1], up_one, down_one
    )
    p2r = swap(p2)
    first, n3, qkv2, o2, lse2, p3 = attention_forward(
        h, (x1, p2, p2r), False, gain[2], qkv_two, out_two, segc, segr
    )
    p3r = swap(p3)
    x2, sent = route_step(h, first, p3, p3r, gain[3], slot_row, slots)
    m_own = travel(sent)
    m_peer = swap(m_own)
    yo, yp, dmo, dmp, m_all, dy_all, ae_all, due_all, dc = expert_step(
        m_own, m_peer, grad_own, grad_peer, centroids, expert_up, expert_down
    )
    dm_sum = add(dmo, swap(dmp))
    y_sum = add(yo, swap(yp))
    up_grad = mm_tn(m_all, due_all)[None]
    down_grad = mm_tn(ae_all, dy_all)[None]
    dm_back, up_grad, down_grad, y_sum = lax.optimization_barrier(
        (travel(dm_sum), up_grad, down_grad, y_sum)
    )
    y_back = travel(y_sum)
    dm_own = collect(dm_back, slot_col)
    dm_peer = swap(dm_own)
    dc = dc[:1]
    cen_grad = dc + swap(dc)

    da2, dqk2, dv2, dn2, dg3 = attention_backward(
        h,
        (cotangent, cot_peer, dm_own, dm_peer, first, p3, p3r),
        True,
        gain[3],
        (qkv2, o2, lse2),
        qkv_two,
        out_two,
        segc,
        segr,
    )
    dn2r = swap(dn2)
    f = up_one.shape[1]
    c = qkv_one.shape[2]

    def grad(a, b):
        return mm_tn(a, b).astype(BF)

    def value_sides(n, dv):
        w = grad(n, dv)
        return jnp.concatenate([w[: d // 2], w[d // 2 :]], axis=1)

    def last_step(dr, dna, dnb):
        return final_step(h, dr, dna, dnb, tokens, tokens_peer, gain[0])

    def gather_y(y):
        return collect_add(h, y, slot_col, x2)

    def stack_gains(dg0):
        return jnp.concatenate([dg0[:1], dg1[:1], dg2[:1], dg3[:1]], axis=0)

    def last_attention(dr, dna, dnb):
        return attention_backward(
            h, (dr, dna, dnb, x1), False, gain[1], (qkv1, o1, lse1), qkv_one, out_one, segc, segr
        )

    if steps is None:
        df, du, dnd, dg2 = dense_backward(
            da2, dn2, dn2r, first, gain[2], gp, up_one, down_one
        )
        da1, dqk1, dv1, dn1, dg1 = last_attention(df, dnd, swap(dnd))
        input_grad, dg0 = last_step(da1, dn1, swap(dn1))
        second = gather_y(y_back)
        up_first, down_first, qk_two, v_two, wo_two, qk_one, v_one, wo_one, gain_grads = lax.psum(
            (
                grad(n2, du),
                grad(act, df),
                grad(n3, dqk2),
                grad(n3, dv2),
                grad(o2, da2),
                grad(n1, dqk1),
                grad(n1, dv1),
                grad(o1, da1),
                stack_gains(dg0),
            ),
            "dp",
        )

        def unpack(qk, v):
            return jnp.stack([qk[:, :c], qk[:, c:], v]).astype(F32)

        up_first, down_first = up_first.astype(F32), down_first.astype(F32)
        qkv_second, out_second = unpack(qk_two, v_two), wo_two.astype(F32)
        qkv_first, out_first = unpack(qk_one, v_one), wo_one.astype(F32)
    else:
        me = lax.axis_index("dp")
        bits = jnp.stack([(me // s) % 2 for s in (1, 2, 4, 8)]).astype(jnp.int32)

        def columns(v, bit):
            half = v.shape[1] // 2
            return lax.dynamic_slice_in_dim(v, bit * half, half, 1)

        def query_key(n, dqk, bit):
            return grad(columns(n, bit), dqk)

        def value_out(n, dv, o, da, bit):
            v, wo = value_sides(n, dv), grad(o, da)
            return jnp.where(bit == 1, v, wo), jnp.where(bit == 1, wo, v)

        qk_send = query_key(n3, dqk2, 1 - bits[2])
        qk_keep = query_key(n3, dqk2, bits[2])
        vo_send, vo_keep = value_out(n3, dv2, o2, da2, bits[3])
        (qk_send, qk_keep, vo_send, vo_keep), da2, dn2, dn2r, y_back = lax.optimization_barrier(
            ((qk_send, qk_keep, vo_send, vo_keep), da2, dn2, dn2r, y_back)
        )
        df, du, dnd, dg2 = dense_backward(
            da2, dn2, dn2r, first, gain[2], gp, up_one, down_one
        )
        dndr = swap(dnd)

        def gather_all(y, *dgs):
            stacked = one_step(stack_kernel, bits, dgs, [shape((16, d), BF)])[0]
            return gather_y(y), stacked

        def heavy(dr, dna, dnb, n, g, a, b):
            kept = grad(n, columns(g, bits[0])), grad(columns(a, bits[1]), b)
            kept, dr, dna, dnb = lax.optimization_barrier((kept, dr, dna, dnb))
            return last_attention(dr, dna, dnb), *kept

        orders = [halving(o) for o in ((1, 2, 4, 8), (2, 1, 8, 4), (4, 8, 1, 2), (8, 4, 2, 1))]
        big = [
            Part(orders[0], grad(n2, columns(du, 1 - bits[0]))),
            Part(orders[1], grad(columns(act, 1 - bits[1]), df)),
            Part(orders[2], qk_send, qk_keep),
            Part(orders[3], vo_send, vo_keep),
        ]
        last, up_keep, down_keep = advance(bits, big, heavy, (df, dnd, dndr, n2, du, act, df))
        da1, dqk1, dv1, dn1, dg1 = last
        dn1r = swap(dn1)
        big[0].kept = (up_keep, 0, up_keep.shape[0])
        big[1].kept = (down_keep, 0, down_keep.shape[0])
        fold(bits, big)

        def narrow_grads(n, dqk, dv, o, da):
            return (
                query_key(n, dqk, 1 - bits[0]),
                query_key(n, dqk, bits[0]),
                value_out(n, dv, o, da, bits[1]),
            )

        qk_send, qk_keep, (vo_send, vo_keep) = advance(
            bits, big, narrow_grads, (n1, dqk1, dv1, o1, da1)
        )
        small = [Part(orders[0], qk_send, qk_keep), Part(orders[1], vo_send, vo_keep)]
        parts = big + small
        fold(bits, parts)
        input_grad, dg0 = advance(bits, parts, last_step, (da1, dn1, dn1r))
        fold(bits, parts)
        second, gains_own = advance(bits, parts, gather_all, (y_back, dg0, dg1, dg2, dg3))
        tail = Part((1, 2, 4, 8), gains_own)
        tail.kept = (None, 0, 0)
        parts.append(tail)
        while big[0].live:
            fold(bits, parts)
            advance(bits, parts)
        fold(bits, parts)
        arrays = [x for p in big for x in (p.sent[0], p.got[0])]

        def finish_wide(*arrays):
            return finish(
                finish_wide_kernel,
                bits,
                big,
                arrays,
                [
                    shape((d, f), F32),
                    shape((f, d), F32),
                    shape((3, d, c), F32),
                    shape((c, d), F32),
                ],
            )

        up_first, down_first, qkv_second, out_second = advance(bits, small, finish_wide, arrays)
        while small[0].live:
            fold(bits, small)
            advance(bits, small)
        gain_grads = (tail.sent[0], tail.got[0])
        lo = tail.sent[1]
        gain_grads = sum(v[lo : lo + 4].astype(F32) for v in gain_grads)
        qkv_first, out_first = finish(
            finish_narrow_kernel,
            bits,
            small,
            [x for p in small for x in (p.sent[0], p.got[0])],
            [shape((3, d, c), F32), shape((c, d), F32)],
        )
    first_own = lax.dynamic_slice_in_dim(first, side * count, count, 0)
    return (
        first_own,
        second,
        input_grad,
        gain_grads,
        qkv_first,
        out_first,
        up_first,
        down_first,
        qkv_second,
        out_second,
        up_grad,
        down_grad,
        cen_grad,
    )


def solution(mesh):
    rows = P(("dp", "head"), None)
    shared = (
        P(None, None, "head"),
        P("head", None),
        P(None, "head"),
        P("head", None),
        P(None, None, "head"),
        P("head", None),
        P("dp", None, "head"),
        P("dp", "head", None),
        P("dp", None),
    )
    steps = 16 if mesh.shape["dp"] == 16 else None
    return jax.shard_map(
        functools.partial(body, steps),
        mesh=mesh,
        in_specs=(rows, P("dp"), P("dp", None), P(), *shared, rows),
        out_specs=(rows, rows, rows, P(), *shared),
        check_vma=False,
    )
```

```python
import functools

import jax
import jax.numpy as jnp
from jax import lax
from jax.experimental import pallas as pl
from jax.experimental.pallas import tpu as pltpu
from jax.sharding import PartitionSpec as P

BF = jnp.bfloat16
F32 = jnp.float32
EPS = 1e-05
MASKED = -1e30
BLK = 256
HEAD_DIM = 64
SWAP = [(0, 1), (1, 0)]
VLIM = 56 * 1024 * 1024
SMALL = 16 * 1024 * 1024


def mm(a, b):
    return lax.dot_general(a, b, (((1,), (0,)), ((), ())), preferred_element_type=F32)


def mm_nt(a, b):
    return lax.dot_general(a, b, (((1,), (1,)), ((), ())), preferred_element_type=F32)


def mm_tn(a, b):
    return lax.dot_general(a, b, (((0,), (0,)), ((), ())), preferred_element_type=F32)


def norm_stats(x):
    c = x - jnp.mean(x, axis=-1, keepdims=True)
    r = lax.rsqrt(jnp.mean(c * c, axis=-1, keepdims=True) + EPS)
    return c * r, r


def norm_back(x, gain, dn):
    xh, r = norm_stats(x)
    dxh = dn * gain
    a = jnp.mean(dxh, axis=-1, keepdims=True)
    b = jnp.mean(dxh * xh, axis=-1, keepdims=True)
    return r * (dxh - a - xh * b), jnp.sum(dn * xh, axis=0, keepdims=True)


def gelu_pair(u):
    z = jnp.abs(u) * 0.7071067811865476
    t = 1.0 / (1.0 + 0.3275911 * z)
    ex = jnp.exp(-(z * z))
    poly = t * (
        0.254829592
        + t * (-0.284496736 + t * (1.421413741 + t * (-1.453152027 + t * 1.061405429)))
    )
    tail = 0.5 * poly * ex
    phi = jnp.where(u >= 0.0, 1.0 - tail, tail)
    return u * phi, phi + u * (ex * 0.3989422804014327)


def mask_bias(segc, segr, b, keys):
    row = lax.broadcasted_iota(jnp.int32, (BLK, keys), 0) + b * BLK
    col = lax.broadcasted_iota(jnp.int32, (BLK, keys), 1)
    return jnp.where((segc == segr[:, :keys]) & (col <= row), 0.0, MASKED)


def half_lane(hh):
    lane = lax.broadcasted_iota(jnp.int32, (BLK, 128), 1)
    return (lane >= 64) if hh else (lane < 64)


def residual_of(xr, pa, pb):
    return xr[...].astype(F32) + (pa[...].astype(F32) + pb[...].astype(F32))


def attn_fwd_kernel(blocks, split, h_ref, *refs):
    if split:
        own, peer, g, wqkv, wo, segc, segr = refs[:7]
        outs = refs[7:]
    else:
        xr, pa, pb, g, wqkv, wo, segc, segr = refs[:8]
        outs = refs[8:]
    x_out = None
    if not split:
        x_out, *outs = outs
    n_out, qkv_out, o_out, lse_out, p_out, ks, vs = outs
    i = pl.program_id(0)
    if split:
        mine = (i // (blocks // 2)) == h_ref[0]
        x = jnp.where(mine, own[...].astype(F32), peer[...].astype(F32))
    else:
        x = residual_of(xr, pa, pb)
        x_out[...] = x.astype(BF)
    xh, _ = norm_stats(x)
    n = (xh * g[...]).astype(BF)
    n_out[...] = n
    q = (mm(n, wqkv[0]).astype(BF).astype(F32) * 0.125).astype(BF)
    k = mm(n, wqkv[1]).astype(BF)
    v = mm(n, wqkv[2]).astype(BF)
    qkv_out[0] = q
    qkv_out[1] = k
    qkv_out[2] = v
    rows = pl.ds(pl.multiple_of(i * BLK, BLK), BLK)
    ks[rows, :] = k
    vs[rows, :] = v
    pairs = q.shape[1] // 128
    for b in range(blocks):

        @pl.when(i == b)
        def _(b=b):
            keys = BLK * (b + 1)
            bias = mask_bias(segc[...], segr[...], b, keys)
            lse = jnp.zeros((BLK, 128), F32)
            lanes = lax.broadcasted_iota(jnp.int32, (BLK, 128), 1)
            total = jnp.zeros((BLK, wo.shape[1]), F32)
            for pr in range(pairs):
                cols = slice(pr * 128, pr * 128 + 128)
                qp = qkv_out[0, :, cols]
                kp = ks[0:keys, cols]
                vp = vs[0:keys, cols]
                res = []
                for hh in range(2):
                    qh = jnp.where(half_lane(hh), qp, jnp.zeros_like(qp))
                    s = mm_nt(qh, kp) + bias
                    m = jnp.max(s, axis=-1, keepdims=True)
                    e = jnp.exp(s - m)
                    l = jnp.sum(e, axis=-1, keepdims=True)
                    res.append(mm(e.astype(BF), vp) * (1.0 / l))
                    lse = jnp.where(lanes == pr * 2 + hh, m + jnp.log(l), lse)
                ob = jnp.where(half_lane(0), res[0], res[1]).astype(BF)
                o_out[:, cols] = ob
                total = total + mm(ob, wo[cols, :])
            lse_out[...] = lse
            p_out[...] = total.astype(BF)


def probs_kernel(blocks, qr, kf, lser, segc, segr, p_out):
    i = pl.program_id(0)
    pairs = kf.shape[2] // 128
    for b in range(blocks):

        @pl.when(i == b)
        def _(b=b):
            keys = BLK * (b + 1)
            bias = mask_bias(segc[...], segr[...], b, keys)
            lse = lser[...]
            for pr in range(pairs):
                cols = slice(pr * 128, pr * 128 + 128)
                qp = qr[0, :, cols]
                kp = kf[0, 0:keys, cols]
                for hh in range(2):
                    h = pr * 2 + hh
                    qh = jnp.where(half_lane(hh), qp, jnp.zeros_like(qp))
                    p = jnp.exp(mm_nt(qh, kp) + bias - lse[:, h : h + 1])
                    p_out[h, :, 0:keys] = p.astype(BF)


def attn_bwd_kernel(blocks, split, h_ref, *refs):
    if split:
        dro, drp, dno, dnp_ = refs[:4]
    else:
        drr, dna, dnb = refs[:3]
    if split:
        xr, pa, pb = refs[4:7]
        xn = residual_of(xr, pa, pb)
        rest = refs[7:]
    else:
        xn = refs[3][...].astype(F32)
        rest = refs[4:]
    gn, qr, kf, vf, orf, pr_in, wqkv, wo = rest[:8]
    da_out, dqk_out, dv_out, dn_out, dg_out, dks, dvs = rest[8:]
    i = pl.program_id(0)
    blk = blocks - 1 - i
    if split:
        mine = (blk // (blocks // 2)) == h_ref[0]
        dr = jnp.where(mine, dro[...].astype(F32), drp[...].astype(F32))
        dn = jnp.where(mine, dno[...].astype(F32), dnp_[...].astype(F32))
    else:
        dr = drr[...].astype(F32)
        dn = dna[...].astype(F32) + dnb[...].astype(F32)
    dx, dg = norm_back(xn, gn[...], dn)
    da = (dr + dx).astype(BF)
    da_out[...] = da

    @pl.when(i == 0)
    def _():
        dks[...] = jnp.zeros_like(dks)
        dvs[...] = jnp.zeros_like(dvs)
        dg_out[...] = jnp.zeros_like(dg_out)

    dg_out[...] += jnp.broadcast_to(dg, dg_out.shape)
    do = mm_nt(da, wo[...]).astype(BF)
    pairs = wo.shape[0] // 128
    for b in range(blocks):

        @pl.when(blk == b)
        def _(b=b):
            keys = BLK * (b + 1)
            here = slice(b * BLK, b * BLK + BLK)
            for pr in range(pairs):
                cols = slice(pr * 128, pr * 128 + 128)
                qp = qr[0, :, cols]
                kp = kf[0, 0:keys, cols]
                vp = vf[0, 0:keys, cols]
                dop = do[:, cols]
                prod = dop.astype(F32) * orf[:, cols].astype(F32)
                dqs, dss, ps, qs, dos = [], [], [], [], []
                for hh in range(2):
                    hm = half_lane(hh)
                    qh = jnp.where(hm, qp, jnp.zeros_like(qp))
                    doh = jnp.where(hm, dop, jnp.zeros_like(dop))
                    delta = jnp.sum(jnp.where(hm, prod, 0.0), axis=-1, keepdims=True)
                    h = pr * 2 + hh
                    p = pr_in[h, :, 0:keys]
                    dp = mm_nt(doh, vp)
                    ds = (p.astype(F32) * (dp - delta)).astype(BF)
                    dqs.append(mm(ds, kp))
                    dks[0:keys, cols] += mm_tn(ds, qh)
                    dvs[0:keys, cols] += mm_tn(p, doh)
                dq = jnp.where(half_lane(0), dqs[0], dqs[1]) * 0.125
                dqk_out[:, cols] = dq.astype(BF)
            dqk_out[:, pairs * 128 :] = dks[here, :].astype(BF)
            dv_out[...] = dvs[here, :].astype(BF)

    c = pairs * 128
    dn_out[...] = (
        mm_nt(dqk_out[:, :c], wqkv[0]) + mm_nt(dqk_out[:, c:], wqkv[1]) + mm_nt(dv_out[...], wqkv[2])
    ).astype(BF)


def dense_fwd_kernel(
    blocks, h_ref, own, peer, pa, pb, g, up, down, x_out, n_out, act_out, gp_out, p_out
):
    mine = (pl.program_id(0) // (blocks // 2)) == h_ref[0]
    x = jnp.where(mine, own[...].astype(F32), peer[...].astype(F32))
    x = x + (pa[...].astype(F32) + pb[...].astype(F32))
    x_out[...] = x.astype(BF)
    xh, _ = norm_stats(x)
    n = (xh * g[...]).astype(BF)
    n_out[...] = n
    act, gp = gelu_pair(mm(n, up[...]))
    act = act.astype(BF)
    act_out[...] = act
    gp_out[...] = gp.astype(BF)
    p_out[...] = mm(act, down[...]).astype(BF)


def dense_bwd_kernel(drr, dna, dnb, xn, gn, gp, up, down, df_out, du_out, dn_out, dg_out):
    dx, dg = norm_back(xn[...].astype(F32), gn[...], dna[...].astype(F32) + dnb[...].astype(F32))
    df = (drr[...].astype(F32) + dx).astype(BF)
    df_out[...] = df

    @pl.when(pl.program_id(0) == 0)
    def _():
        dg_out[...] = jnp.zeros_like(dg_out)

    dg_out[...] += jnp.broadcast_to(dg, dg_out.shape)
    du = (mm_nt(df, down[...]) * gp[...].astype(F32)).astype(BF)
    du_out[...] = du
    dn_out[...] = mm_nt(du, up[...]).astype(BF)


def final_kernel(h_ref, drr, dna, dnb, xo, xp, gn, dr_out, dg_out):
    i = pl.program_id(0)
    mine = i >= 2
    x = jnp.where(mine, xo[...].astype(F32), xp[...].astype(F32))
    dx, dg = norm_back(x, gn[...], dna[...].astype(F32) + dnb[...].astype(F32))
    dr_out[...] = drr[...].astype(F32) + dx

    @pl.when(i == 0)
    def _():
        dg_out[...] = jnp.zeros_like(dg_out)

    dg_out[...] += jnp.broadcast_to(dg, dg_out.shape)


def spread_kernel(rows_ref, slot_ref, out_ref):
    count = out_ref.shape[0]
    place = lax.broadcasted_iota(jnp.int32, (count, rows_ref.shape[0]), 0)
    place = place + pl.program_id(0) * count
    hot = (place == slot_ref[...]).astype(F32).astype(BF)
    out_ref[...] = mm(hot, rows_ref[...]).astype(BF)


def route_kernel(h_ref, xr, pa, pb, g, slot_ref, x_out, send_out, ms):
    i = pl.program_id(0)
    x = residual_of(xr, pa, pb)
    x_out[...] = x
    xh, _ = norm_stats(x)
    rows = pl.ds(pl.multiple_of(i * BLK, BLK), BLK)
    ms[rows, :] = (xh * g[...]).astype(BF)

    @pl.when(i == pl.num_programs(0) - 1)
    def _():
        count = send_out.shape[0]
        place = lax.broadcasted_iota(jnp.int32, (count, ms.shape[0]), 0)
        hot = (place == slot_ref[...]).astype(F32).astype(BF)
        send_out[...] = mm(hot, ms[...]).astype(BF)


def collect_kernel(table, slot_ref, out_ref):
    count = table.shape[0]
    place = lax.broadcasted_iota(jnp.int32, (out_ref.shape[0], count), 1)
    hot = (place == slot_ref[...]).astype(F32).astype(BF)
    out_ref[...] = mm(hot, table[...]).astype(BF)


def collect_add_kernel(h_ref, table, slot_ref, x_ref, out_ref):
    count = table.shape[0]
    place = lax.broadcasted_iota(jnp.int32, (out_ref.shape[0], count), 1)
    hot = (place == slot_ref[...]).astype(F32).astype(BF)
    out_ref[...] = (x_ref[...] + mm(hot, table[...])).astype(BF)


def expert_kernel(
    half, mo, mp, go, gp_, cen, up, down,
    yo, yp, dmo, dmp, m_all, dy_all, ae_all, due_all, dc_out,
):
    i = pl.program_id(0)
    first = i < half
    m = jnp.where(first, mo[...], mp[...])
    gb = jnp.where(first, go[...], gp_[...]).astype(F32)
    mf = m.astype(F32)
    cf = cen[...].astype(F32)
    gate = jax.nn.sigmoid(jnp.sum(mf * cf, axis=-1, keepdims=True))
    dy = (gate * gb).astype(BF)
    u = mm(m, up[0])
    dact = mm_nt(dy, down[0])
    act, gd = gelu_pair(u)
    act = act.astype(BF)
    y = mm(act, down[0])
    dscore = jnp.sum(gb * y, axis=-1, keepdims=True) * gate * (1.0 - gate)
    due = (dact * gd).astype(BF)
    dm = (mm_nt(due, up[0]) + dscore * cf).astype(BF)
    gy = (gate * y).astype(BF)
    m_all[...] = m
    dy_all[...] = dy
    ae_all[...] = act
    due_all[...] = due

    @pl.when(i == 0)
    def _():
        dc_out[...] = jnp.zeros_like(dc_out)

    dc_out[...] += jnp.broadcast_to(jnp.sum(dscore * mf, axis=0, keepdims=True), dc_out.shape)

    @pl.when(first)
    def _():
        yo[...] = gy
        dmo[...] = dm

    @pl.when(jnp.logical_not(first))
    def _():
        yp[...] = gy
        dmp[...] = dm


def shape(dims, kind):
    return jax.ShapeDtypeStruct(dims, kind)


def fixed(dims):
    zero = (0,) * len(dims)
    return pl.BlockSpec(dims, lambda *a: zero, pipeline_mode=pl.Buffered(1))


def rows_spec(width, index=lambda i: i):
    return pl.BlockSpec((BLK, width), lambda i, *a: (index(i), 0))


def call(
    kernel, grid, in_specs, out_specs, outs, scratch, flops, moved, args, prefetch=None, limit=VLIM
):
    params = pltpu.CompilerParams(
        vmem_limit_bytes=int(limit), dimension_semantics=("arbitrary",)
    )
    cost = pl.CostEstimate(flops=int(flops), bytes_accessed=int(moved), transcendentals=0)
    if prefetch is None:
        spec = pl.GridSpec(
            grid=grid, in_specs=in_specs, out_specs=out_specs, scratch_shapes=scratch
        )
    else:
        spec = pltpu.PrefetchScalarGridSpec(
            num_scalar_prefetch=1,
            grid=grid,
            in_specs=in_specs,
            out_specs=out_specs,
            scratch_shapes=scratch,
        )
        args = (prefetch,) + tuple(args)
    return pl.pallas_call(
        kernel, grid_spec=spec, out_shape=outs, compiler_params=params, cost_estimate=cost
    )(*args)


def attention_forward(h, inputs, split, gain, wqkv, wo, segc, segr):
    length, d = segc.shape[0], wqkv.shape[1]
    c = wqkv.shape[2]
    blocks = length // BLK
    if split:
        ins = [rows_spec(d, lambda i: i % (blocks // 2))] * 2
    else:
        ins = [rows_spec(d)] * 3
    ins += [
        fixed((1, d)),
        fixed((3, d, c)),
        fixed((c, d)),
        pl.BlockSpec((BLK, 1), lambda i, *a: (i, 0)),
        fixed((1, length)),
    ]
    outs = [] if split else [(rows_spec(d), shape((length, d), BF))]
    outs += [
        (rows_spec(d), shape((length, d), BF)),
        (pl.BlockSpec((3, BLK, c), lambda i, *a: (0, i, 0)), shape((3, length, c), BF)),
        (rows_spec(c), shape((length, c), BF)),
        (rows_spec(128), shape((length, 128), F32)),
        (rows_spec(d), shape((length, d), BF)),
    ]
    scratch = [pltpu.VMEM((length, c), BF), pltpu.VMEM((length, c), BF)]
    flops = 2 * length * d * c * 4 + 4 * length * length * c
    return call(
        functools.partial(attn_fwd_kernel, blocks, split),
        (blocks,),
        ins,
        [o[0] for o in outs],
        [o[1] for o in outs],
        scratch,
        flops * 2,
        length * d * 20,
        (*inputs, gain, wqkv, wo, segc, segr),
        prefetch=h,
    )


def attention_probs(qkv, lse, segc, segr):
    length, c = qkv.shape[1:]
    heads = c // HEAD_DIM
    return call(
        functools.partial(probs_kernel, length // BLK),
        (length // BLK,),
        [
            pl.BlockSpec((1, BLK, c), lambda i, *a: (0, i, 0)),
            pl.BlockSpec((1, length, c), lambda i, *a: (1, 0, 0), pipeline_mode=pl.Buffered(1)),
            rows_spec(128),
            pl.BlockSpec((BLK, 1), lambda i, *a: (i, 0)),
            fixed((1, length)),
        ],
        [pl.BlockSpec((heads, BLK, length), lambda i, *a: (0, i, 0))],
        [shape((heads, length, length), BF)],
        [],
        4 * length * length * c,
        2 * heads * length * length,
        (qkv, qkv, lse, segc, segr),
    )[0]


def attention_backward(h, inputs, split, gn, saved, wqkv, wo):
    qkv, o, probs = saved
    length, d = o.shape[0], wqkv.shape[1]
    c = wqkv.shape[2]
    blocks = length // BLK
    back = lambda i: blocks - 1 - i
    if split:
        ins = [rows_spec(d, lambda i: back(i) % (blocks // 2))] * 4 + [rows_spec(d, back)] * 3
    else:
        ins = [rows_spec(d, back)] * 4
    part = lambda n: pl.BlockSpec(
        (1, length, c), lambda i, *a: (n, 0, 0), pipeline_mode=pl.Buffered(1)
    )
    ins += [
        fixed((1, d)),
        pl.BlockSpec((1, BLK, c), lambda i, *a: (0, back(i), 0)),
        part(1),
        part(2),
        rows_spec(c, back),
        pl.BlockSpec((c // HEAD_DIM, BLK, length), lambda i, *a: (0, back(i), 0)),
        fixed((3, d, c)),
        fixed((c, d)),
    ]
    outs = [
        (rows_spec(d, back), shape((length, d), BF)),
        (rows_spec(2 * c, back), shape((length, 2 * c), BF)),
        (rows_spec(c, back), shape((length, c), BF)),
        (rows_spec(d, back), shape((length, d), BF)),
        (fixed((8, d)), shape((8, d), F32)),
    ]
    scratch = [pltpu.VMEM((length, c), F32), pltpu.VMEM((length, c), F32)]
    flops = 2 * length * d * c * 4 + 10 * length * length * c
    return call(
        functools.partial(attn_bwd_kernel, blocks, split),
        (blocks,),
        ins,
        [s[0] for s in outs],
        [s[1] for s in outs],
        scratch,
        flops * 2,
        length * d * 20,
        (*inputs, gn, qkv, qkv, qkv, o, probs, wqkv, wo),
        prefetch=h,
    )


def dense_forward(h, own, peer, pa, pb, gain, up, down):
    length, d = pa.shape
    f = up.shape[1]
    blocks = length // BLK
    half = rows_spec(d, lambda i: lax.rem(i, blocks // 2))
    return call(
        functools.partial(dense_fwd_kernel, blocks),
        (blocks,),
        [half] * 2 + [rows_spec(d)] * 2 + [fixed((1, d)), fixed((d, f)), fixed((f, d))],
        [rows_spec(d), rows_spec(d), rows_spec(f), rows_spec(f), rows_spec(d)],
        [
            shape((length, d), BF),
            shape((length, d), BF),
            shape((length, f), BF),
            shape((length, f), BF),
            shape((length, d), BF),
        ],
        [],
        4 * length * d * f,
        length * d * 20 + 4 * d * f,
        (own, peer, pa, pb, gain, up, down),
        prefetch=h,
    )


def dense_backward(dr, dna, dnb, xn, gn, gp, up, down):
    length, d = dr.shape
    f = up.shape[1]
    return call(
        dense_bwd_kernel,
        (length // BLK,),
        [rows_spec(d)] * 4
        + [fixed((1, d)), rows_spec(f), fixed((d, f)), fixed((f, d))],
        [rows_spec(d), rows_spec(f), rows_spec(d), fixed((8, d))],
        [
            shape((length, d), BF),
            shape((length, f), BF),
            shape((length, d), BF),
            shape((8, d), F32),
        ],
        [],
        4 * length * d * f,
        length * d * 20 + 4 * d * f,
        (dr, dna, dnb, xn, gn, gp, up, down),
    )


def own_last(blocks):
    return lambda i, h: lax.rem(i + (blocks // 2) * (1 - h[0]), blocks)


def final_step(h, dr, dna, dnb, xo, xp, gn):
    length, d = dr.shape
    blocks = length // BLK
    place = own_last(blocks)
    spec = pl.BlockSpec((BLK, d), lambda i, h: (place(i, h), 0))
    late = lambda i, h: (jnp.maximum(i - blocks // 2, 0), 0)
    return call(
        final_kernel,
        (blocks,),
        [spec] * 3
        + [pl.BlockSpec((BLK, d), late)]
        + [pl.BlockSpec((BLK, d), lambda i, h: (lax.rem(i, blocks // 2), 0)), fixed((1, d))],
        [pl.BlockSpec((BLK, d), late), fixed((8, d))],
        [shape((length // 2, d), F32), shape((8, d), F32)],
        [],
        length * d * 40,
        length * d * 14,
        (dr, dna, dnb, xo, xp, gn),
        prefetch=h,
        limit=SMALL,
    )


def route_step(h, x, pa, pb, gain, slot_row, slots):
    length, d = x.shape
    per = length // 2 // BLK
    spec = pl.BlockSpec((BLK, d), lambda i, h: (h[0] * per + i, 0))
    return call(
        route_kernel,
        (per,),
        [spec] * 3 + [fixed((1, d)), fixed((1, length // 2))],
        [rows_spec(d), fixed((slots, d))],
        [shape((length // 2, d), F32), shape((slots, d), BF)],
        [pltpu.VMEM((length // 2, d), BF)],
        length * slots * d,
        length * d * 14,
        (x, pa, pb, gain, slot_row),
        prefetch=h,
        limit=SMALL,
    )


def spread(rows, slot_row, slots):
    count, d = rows.shape
    return call(
        spread_kernel,
        (slots // BLK,),
        [fixed((count, d)), fixed((1, count))],
        [rows_spec(d)],
        [shape((slots, d), BF)],
        [],
        2 * count * slots * d,
        4 * slots * d,
        (rows, slot_row),
        limit=SMALL,
    )[0]


def collect(table, slot_col):
    slots, d = table.shape
    count = slot_col.shape[0]
    return call(
        collect_kernel,
        (count // BLK,),
        [fixed((slots, d)), pl.BlockSpec((BLK, 1), lambda i, *a: (i, 0))],
        [rows_spec(d)],
        [shape((count, d), BF)],
        [],
        2 * count * slots * d,
        4 * slots * d,
        (table, slot_col),
        limit=SMALL,
    )[0]


def collect_add(h, table, slot_col, x):
    slots, d = table.shape
    count = slot_col.shape[0]
    per = count // BLK
    return call(
        collect_add_kernel,
        (per,),
        [
            fixed((slots, d)),
            pl.BlockSpec((BLK, 1), lambda i, *a: (i, 0)),
            rows_spec(d),
        ],
        [rows_spec(d)],
        [shape((count, d), BF)],
        [],
        2 * count * slots * d,
        8 * slots * d,
        (table, slot_col, x),
        prefetch=h,
        limit=SMALL,
    )[0]


def expert_step(mo, mp, go, gp, cen, up, down):
    rows, d = mo.shape
    f = up.shape[2]
    half = rows // BLK
    lo = lambda i: jnp.minimum(i, half - 1)
    hi = lambda i: jnp.maximum(i - half, 0)
    return call(
        functools.partial(expert_kernel, half),
        (2 * half,),
        [rows_spec(d, lo), rows_spec(d, hi), rows_spec(d, lo), rows_spec(d, hi)]
        + [fixed((1, d)), fixed((1, d, f)), fixed((1, f, d))],
        [rows_spec(d, lo), rows_spec(d, hi), rows_spec(d, lo), rows_spec(d, hi)]
        + [rows_spec(d), rows_spec(d), rows_spec(f), rows_spec(f), fixed((8, d))],
        [shape((rows, d), BF)] * 4
        + [shape((2 * rows, d), BF)] * 2
        + [shape((2 * rows, f), BF)] * 2
        + [shape((8, d), F32)],
        [],
        16 * rows * d * f,
        rows * d * 24 + rows * f * 8,
        (mo, mp, go, gp, cen, up, down),
    )


def slot_index(chosen, capacity, experts):
    rows = chosen.shape[0]
    matches = chosen[:, None] == jnp.arange(experts, dtype=jnp.int32)[None, :]
    position = jnp.arange(rows, dtype=jnp.int32)
    earlier = (position[None, :] < position[:, None]).astype(BF)
    before = jnp.dot(earlier, matches.astype(BF), preferred_element_type=F32)
    rank = jnp.sum(jnp.where(matches, before, 0.0), axis=1).astype(jnp.int32)
    return chosen * capacity + rank


def swap(v):
    return lax.ppermute(v, "head", SWAP)


def pick(bit, a, b):
    return jnp.where(bit == 1, a, b)


def total_of(a, b):
    return (a.astype(F32) + b.astype(F32)).astype(BF)


def whole(arrays):
    return [pl.BlockSpec(a.shape, lambda i, *r, n=len(a.shape): (0,) * n) for a in arrays]


def one_step(kernel, bits, args, outs):
    moved = sum(a.size * a.dtype.itemsize for a in (*args, *outs))
    return call(
        kernel,
        (1,),
        whole(args),
        whole(outs),
        outs,
        [],
        moved,
        moved,
        args,
        prefetch=bits,
        limit=2 * moved + 8 * 1024 * 1024,
    )


def sum_kernel(h_ref, a, b, out):
    out[...] = total_of(a[...], b[...])


PLACE = {1: 0, 2: 1, 4: 2, 8: 3}


def fold_kernel(plan, n_in, bits, *refs):
    def get(piece):
        at, lo, n = piece
        return refs[at][lo : lo + n, :]

    def put(piece, value):
        at, lo, n = piece
        refs[n_in + at][lo : lo + n, :] = value

    for kind, ins, outs, place in plan:
        if kind == "copy":
            put(outs[0], get(ins[0]))
        elif kind == "sum":
            put(outs[0], total_of(get(ins[0]), get(ins[1])))
        elif kind == "split":
            (ka, kl, n), (ga, gl, _) = ins
            q = n // 2
            lo = total_of(get((ka, kl, q)), get((ga, gl, q)))
            hi = total_of(get((ka, kl + q, q)), get((ga, gl + q, q)))
            put(outs[0], pick(bits[place], lo, hi))
            put(outs[1], pick(bits[place], hi, lo))
        else:
            p, g = get(ins[0]), get(ins[1])
            at, lo, n = outs[0]
            put((at, lo, n // 2), pick(bits[place], g, p))
            put((at, lo + n // 2, n // 2), pick(bits[place], p, g))


def first_fold_kernel(places, bits, *refs):
    outs = refs[4 * len(places) :]
    for j, place in enumerate(places):
        kl, kh, gl, gh = refs[4 * j : 4 * j + 4]
        lo, hi = total_of(kl[...], gl[...]), total_of(kh[...], gh[...])
        outs[2 * j][...] = pick(bits[place], lo, hi)
        outs[2 * j + 1][...] = pick(bits[place], hi, lo)


def first_fold(bits, parts):
    args, ins, outs, out_specs, places = [], [], [], [], []
    for p in parts:
        keep, got = p.kept[0], p.got[0]
        n, width = keep.shape
        low = pl.BlockSpec((n // 8, width), lambda i, *a: (i, 0))
        high = pl.BlockSpec((n // 8, width), lambda i, *a: (i + 4, 0))
        args += [keep, keep, got, got]
        ins += [low, high, low, high]
        outs += [shape((n // 2, width), BF)] * 2
        out_specs += [low, low]
        places.append(PLACE[p.order[p.phase]])
    moved = sum(a.size * 2 for a in args)
    made = call(
        functools.partial(first_fold_kernel, tuple(places)),
        (4,),
        ins,
        out_specs,
        outs,
        [],
        moved,
        moved,
        args,
        prefetch=bits,
    )
    for j, p in enumerate(parts):
        rows = outs[2 * j].shape[0]
        p.sent, p.kept = (made[2 * j], 0, rows), (made[2 * j + 1], 0, rows)


class Part:
    def __init__(self, order, send, keep=None):
        self.order, self.phase = order, 0
        self.sent = (send, 0, send.shape[0])
        self.kept = None if keep is None else (keep, 0, keep.shape[0])
        self.got = None
        self.fresh = True

    @property
    def live(self):
        return self.phase < len(self.order)


def halving(order):
    return order + order[::-1]


def advance(bits, parts, during=None, inputs=()):
    parts = [p for p in parts if p.live]
    width = parts[0].sent[0].shape[1]
    buffers = {}
    for p in parts:
        buffers.setdefault(p.order[p.phase], p.sent[0])
    steps = sorted(buffers)
    flat, inputs = lax.optimization_barrier(([buffers[s] for s in steps], inputs))
    got = [lax.ppermute(v, "dp", [(i, i ^ s) for i in range(16)]) for v, s in zip(flat, steps)]
    result = during(*inputs) if during else inputs
    (flat, got), result = lax.optimization_barrier(((flat, got), result))
    for p in parts:
        at = steps.index(p.order[p.phase])
        p.sent = (flat[at],) + p.sent[1:]
        p.got = (got[at],) + p.sent[1:]
        p.phase += 1
    return result


def fold(bits, parts):
    args, plan, rows, moved = [], [], {}, []

    def source(piece):
        for j, a in enumerate(args):
            if a is piece[0]:
                return (j,) + piece[1:]
        args.append(piece[0])
        return (len(args) - 1,) + piece[1:]

    def room(name, n):
        lo = rows.get(name, 0)
        rows[name] = lo + n
        return (name, lo, n)

    for p in parts:
        if not p.live:
            continue
        step = p.order[p.phase]
        half = len(p.order) // 2
        if p.phase == 0:
            ins, kind, place = [source(p.sent)], "copy", 0
            outs = [room(step, p.sent[2])]
        elif p.kept is not None and p.kept[0] is None:
            ins, kind, place = [source(p.sent), source(p.got)], "sum", 0
            outs = [room(step, p.sent[2])]
        elif p.phase < half:
            ins, kind, place = [source(p.kept), source(p.got)], "split", PLACE[step]
            n = p.kept[2] // 2
            outs = [room(step, n), room("keep", n)]
        elif p.phase == half:
            ins, kind, place = [source(p.kept), source(p.got)], "sum", 0
            outs = [room(step, p.kept[2])]
        else:
            ins, kind, place = [source(p.sent), source(p.got)], "raise", PLACE[p.order[p.phase - 1]]
            outs = [room(step, 2 * p.sent[2])]
        plan.append((kind, ins, outs, place))
        moved.append(p)
    names = list(rows)
    width = args[0].shape[1]
    shapes = [shape((rows[n], width), BF) for n in names]
    fixed_plan = tuple(
        (kind, tuple(ins), tuple((names.index(o[0]),) + o[1:] for o in outs), place)
        for kind, ins, outs, place in plan
    )
    made = one_step(functools.partial(fold_kernel, fixed_plan, len(args)), bits, args, shapes)
    for p, (_, _, outs, _) in zip(moved, plan):
        p.sent = (made[names.index(outs[0][0])],) + outs[0][1:]
        if len(outs) > 1:
            p.kept = (made[names.index(outs[1][0])],) + outs[1][1:]


def ends(bits, ref_s, ref_g, piece, place):
    lo, n = piece
    a, b = ref_s[lo : lo + n, :].astype(F32), ref_g[lo : lo + n, :].astype(F32)
    return pick(bits[place], b, a), pick(bits[place], a, b)


def put_query_key(qkv, blocks):
    c = qkv.shape[2]
    n = blocks[0].shape[0]
    for j, block in enumerate(blocks):
        qkv[0, j * n : j * n + n, :] = block[:, :c]
        qkv[1, j * n : j * n + n, :] = block[:, c:]


def put_value_out(qkv, out, v, o):
    c = qkv.shape[2]
    n = v.shape[0]
    qkv[2, :n, :] = v[:, :c]
    qkv[2, n:, :] = v[:, c:]
    out[...] = o


def finish_wide_kernel(at, bits, xp, xg, yp, yg, ap, ag, bp, bg, up, down, qkv, out):
    lo, hi = ends(bits, xp, xg, at[0], 0)
    f = lo.shape[1]
    up[:, :f] = lo
    up[:, f:] = hi
    lo, hi = ends(bits, yp, yg, at[1], 1)
    f = lo.shape[0]
    down[:f, :] = lo
    down[f:, :] = hi
    put_query_key(qkv, ends(bits, ap, ag, at[2], 2))
    put_value_out(qkv, out, *ends(bits, bp, bg, at[3], 3))


def finish_narrow_kernel(at, bits, xp, xg, yp, yg, qkv, out):
    put_query_key(qkv, ends(bits, xp, xg, at[0], 0))
    put_value_out(qkv, out, *ends(bits, yp, yg, at[1], 1))


def stack_kernel(bits, *refs):
    out = refs[-1]
    row = lax.broadcasted_iota(jnp.int32, out.shape, 0)
    total = jnp.zeros(out.shape, F32)
    for j, ref in enumerate(refs[:-1]):
        total = jnp.where(row == j, ref[0:1, :], total)
    out[...] = total.astype(BF)


def finish(kernel, bits, parts, arrays, outs):
    at = tuple((p.sent[1], p.sent[2]) for p in parts)
    return one_step(functools.partial(kernel, at), bits, arrays, outs)


def body(
    steps,
    tokens,
    segment_ids,
    routes,
    norm_gains,
    qkv_one,
    out_one,
    up_one,
    down_one,
    qkv_two,
    out_two,
    expert_up,
    expert_down,
    centroids,
    cotangent,
):
    count, d = tokens.shape
    side = lax.axis_index("head")
    h = side.astype(jnp.int32).reshape(1)
    experts = lax.axis_size("dp") * expert_up.shape[0]
    capacity = 2 * count // experts
    slots = experts * capacity
    gains = norm_gains.astype(F32)
    gain = [gains[j : j + 1] for j in range(4)]
    segc, segr = segment_ids[:, None], segment_ids[None, :]

    chosen = lax.dynamic_slice_in_dim(routes[:, 0], side * count, count, 0)
    flat = slot_index(chosen, capacity, experts)
    slot_row, slot_col = flat[None, :], flat[:, None]

    def travel(v):
        box = v.reshape(experts, capacity, d)
        return lax.all_to_all(box, "dp", 0, 0, tiled=True).reshape(slots, d)

    def add(a, b):
        return one_step(sum_kernel, h, (a, b), [shape(a.shape, BF)])[0]

    tokens_peer = swap(tokens)
    n1, qkv1, o1, lse1, p1 = attention_forward(
        h, (tokens, tokens_peer), True, gain[0], qkv_one, out_one, segc, segr
    )
    p1r = swap(p1)
    cot_peer = swap(cotangent)
    p1r, cot_table = lax.optimization_barrier((p1r, spread(cotangent, slot_row, slots)))
    grad_own = travel(cot_table)
    grad_peer = swap(grad_own)
    x1, n2, act, gp, p2 = dense_forward(
        h, tokens, tokens_peer, p1, p1r, gain[1], up_one, down_one
    )
    p2r = swap(p2)
    first, n3, qkv2, o2, lse2, p3 = attention_forward(
        h, (x1, p2, p2r), False, gain[2], qkv_two, out_two, segc, segr
    )
    p3r = swap(p3)
    x2, sent = route_step(h, first, p3, p3r, gain[3], slot_row, slots)
    probs2 = attention_probs(qkv2, lse2, segc, segr)
    probs1 = attention_probs(qkv1, lse1, segc, segr)
    m_own, probs1, probs2 = lax.optimization_barrier((travel(sent), probs1, probs2))
    m_peer = swap(m_own)
    yo, yp, dmo, dmp, m_all, dy_all, ae_all, due_all, dc = expert_step(
        m_own, m_peer, grad_own, grad_peer, centroids, expert_up, expert_down
    )
    dm_sum = add(dmo, swap(dmp))
    y_sum = add(yo, swap(yp))
    up_grad = mm_tn(m_all, due_all)[None]
    down_grad = mm_tn(ae_all, dy_all)[None]
    dm_back, up_grad, down_grad, y_sum = lax.optimization_barrier(
        (travel(dm_sum), up_grad, down_grad, y_sum)
    )
    y_back = travel(y_sum)
    dm_own = collect(dm_back, slot_col)
    dm_peer = swap(dm_own)
    dc = dc[:1]
    cen_grad = dc + swap(dc)

    da2, dqk2, dv2, dn2, dg3 = attention_backward(
        h,
        (cotangent, cot_peer, dm_own, dm_peer, first, p3, p3r),
        True,
        gain[3],
        (qkv2, o2, probs2),
        qkv_two,
        out_two,
    )
    dn2r = swap(dn2)
    f = up_one.shape[1]
    c = qkv_one.shape[2]

    def grad(a, b):
        return mm_tn(a, b).astype(BF)

    def value_sides(n, dv):
        w = grad(n, dv)
        return jnp.concatenate([w[: d // 2], w[d // 2 :]], axis=1)

    def last_step(dr, dna, dnb):
        return final_step(h, dr, dna, dnb, tokens, tokens_peer, gain[0])

    def gather_y(y):
        return collect_add(h, y, slot_col, x2)

    def stack_gains(dg0):
        return jnp.concatenate([dg0[:1], dg1[:1], dg2[:1], dg3[:1]], axis=0)

    def last_attention(dr, dna, dnb):
        return attention_backward(
            h, (dr, dna, dnb, x1), False, gain[1], (qkv1, o1, probs1), qkv_one, out_one
        )

    if steps is None:
        df, du, dnd, dg2 = dense_backward(
            da2, dn2, dn2r, first, gain[2], gp, up_one, down_one
        )
        da1, dqk1, dv1, dn1, dg1 = last_attention(df, dnd, swap(dnd))
        input_grad, dg0 = last_step(da1, dn1, swap(dn1))
        second = gather_y(y_back)
        up_first, down_first, qk_two, v_two, wo_two, qk_one, v_one, wo_one, gain_grads = lax.psum(
            (
                grad(n2, du),
                grad(act, df),
                grad(n3, dqk2),
                grad(n3, dv2),
                grad(o2, da2),
                grad(n1, dqk1),
                grad(n1, dv1),
                grad(o1, da1),
                stack_gains(dg0),
            ),
            "dp",
        )

        def unpack(qk, v):
            return jnp.stack([qk[:, :c], qk[:, c:], v]).astype(F32)

        up_first, down_first = up_first.astype(F32), down_first.astype(F32)
        qkv_second, out_second = unpack(qk_two, v_two), wo_two.astype(F32)
        qkv_first, out_first = unpack(qk_one, v_one), wo_one.astype(F32)
    else:
        me = lax.axis_index("dp")
        bits = jnp.stack([(me // s) % 2 for s in (1, 2, 4, 8)]).astype(jnp.int32)

        def columns(v, bit):
            half = v.shape[1] // 2
            return lax.dynamic_slice_in_dim(v, bit * half, half, 1)

        def query_key(n, dqk, bit):
            return grad(columns(n, bit), dqk)

        def value_out(n, dv, o, da, bit):
            v, wo = value_sides(n, dv), grad(o, da)
            return jnp.where(bit == 1, v, wo), jnp.where(bit == 1, wo, v)

        qk_send = query_key(n3, dqk2, 1 - bits[2])
        qk_keep = query_key(n3, dqk2, bits[2])
        vo_send, vo_keep = value_out(n3, dv2, o2, da2, bits[3])
        (qk_send, qk_keep, vo_send, vo_keep), da2, dn2, dn2r, y_back = lax.optimization_barrier(
            ((qk_send, qk_keep, vo_send, vo_keep), da2, dn2, dn2r, y_back)
        )
        df, du, dnd, dg2 = dense_backward(
            da2, dn2, dn2r, first, gain[2], gp, up_one, down_one
        )
        dndr = swap(dnd)

        def gather_all(y, *dgs):
            stacked = one_step(stack_kernel, bits, dgs, [shape((16, d), BF)])[0]
            return gather_y(y), stacked

        def heavy(dr, dna, dnb, n, g, a, b):
            kept = grad(n, columns(g, bits[0])), grad(columns(a, bits[1]), b)
            kept, dr, dna, dnb = lax.optimization_barrier((kept, dr, dna, dnb))
            return last_attention(dr, dna, dnb), *kept

        orders = [halving(o) for o in ((1, 2, 4, 8), (2, 1, 8, 4), (4, 8, 1, 2), (8, 4, 2, 1))]
        big = [
            Part(orders[0], grad(n2, columns(du, 1 - bits[0]))),
            Part(orders[1], grad(columns(act, 1 - bits[1]), df)),
            Part(orders[2], qk_send, qk_keep),
            Part(orders[3], vo_send, vo_keep),
        ]
        last, up_keep, down_keep = advance(bits, big, heavy, (df, dnd, dndr, n2, du, act, df))
        da1, dqk1, dv1, dn1, dg1 = last
        dn1r = swap(dn1)
        big[0].kept = (up_keep, 0, up_keep.shape[0])
        big[1].kept = (down_keep, 0, down_keep.shape[0])
        first_fold(bits, big)

        def narrow_grads(n, dqk, dv, o, da):
            return (
                query_key(n, dqk, 1 - bits[0]),
                query_key(n, dqk, bits[0]),
                value_out(n, dv, o, da, bits[1]),
            )

        qk_send, qk_keep, (vo_send, vo_keep) = advance(
            bits, big, narrow_grads, (n1, dqk1, dv1, o1, da1)
        )
        small = [Part(orders[0], qk_send, qk_keep), Part(orders[1], vo_send, vo_keep)]
        parts = big + small
        fold(bits, parts)
        input_grad, dg0 = advance(bits, parts, last_step, (da1, dn1, dn1r))
        fold(bits, parts)
        second, gains_own = advance(bits, parts, gather_all, (y_back, dg0, dg1, dg2, dg3))
        tail = Part((1, 2, 4, 8), gains_own)
        tail.kept = (None, 0, 0)
        parts.append(tail)
        while big[0].live:
            fold(bits, parts)
            advance(bits, parts)
        fold(bits, parts)
        arrays = [x for p in big for x in (p.sent[0], p.got[0])]

        def finish_wide(*arrays):
            return finish(
                finish_wide_kernel,
                bits,
                big,
                arrays,
                [
                    shape((d, f), F32),
                    shape((f, d), F32),
                    shape((3, d, c), F32),
                    shape((c, d), F32),
                ],
            )

        up_first, down_first, qkv_second, out_second = advance(bits, small, finish_wide, arrays)
        while small[0].live:
            fold(bits, small)
            advance(bits, small)
        gain_grads = (tail.sent[0], tail.got[0])
        lo = tail.sent[1]
        gain_grads = sum(v[lo : lo + 4].astype(F32) for v in gain_grads)
        qkv_first, out_first = finish(
            finish_narrow_kernel,
            bits,
            small,
            [x for p in small for x in (p.sent[0], p.got[0])],
            [shape((3, d, c), F32), shape((c, d), F32)],
        )
    first_own = lax.dynamic_slice_in_dim(first, side * count, count, 0)
    return (
        first_own,
        second,
        input_grad,
        gain_grads,
        qkv_first,
        out_first,
        up_first,
        down_first,
        qkv_second,
        out_second,
        up_grad,
        down_grad,
        cen_grad,
    )


def solution(mesh):
    rows = P(("dp", "head"), None)
    shared = (
        P(None, None, "head"),
        P("head", None),
        P(None, "head"),
        P("head", None),
        P(None, None, "head"),
        P("head", None),
        P("dp", None, "head"),
        P("dp", "head", None),
        P("dp", None),
    )
    steps = 16 if mesh.shape["dp"] == 16 else None
    return jax.shard_map(
        functools.partial(body, steps),
        mesh=mesh,
        in_specs=(rows, P("dp"), P("dp", None), P(), *shared, rows),
        out_specs=(rows, rows, rows, P(), *shared),
        check_vma=False,
    )
```

```python
import functools

import jax
import jax.numpy as jnp
from jax import lax
from jax.experimental import pallas as pl
from jax.experimental.pallas import tpu as pltpu
from jax.sharding import PartitionSpec as P

BF = jnp.bfloat16
F32 = jnp.float32
EPS = 1e-05
MASKED = -1e30
BLK = 256
HEAD_DIM = 64
SWAP = [(0, 1), (1, 0)]
VLIM = 56 * 1024 * 1024
SMALL = 16 * 1024 * 1024


def mm(a, b):
    return lax.dot_general(a, b, (((1,), (0,)), ((), ())), preferred_element_type=F32)


def mm_nt(a, b):
    return lax.dot_general(a, b, (((1,), (1,)), ((), ())), preferred_element_type=F32)


def mm_tn(a, b):
    return lax.dot_general(a, b, (((0,), (0,)), ((), ())), preferred_element_type=F32)


def norm_stats(x):
    c = x - jnp.mean(x, axis=-1, keepdims=True)
    r = lax.rsqrt(jnp.mean(c * c, axis=-1, keepdims=True) + EPS)
    return c * r, r


def norm_back(x, gain, dn):
    xh, r = norm_stats(x)
    dxh = dn * gain
    a = jnp.mean(dxh, axis=-1, keepdims=True)
    b = jnp.mean(dxh * xh, axis=-1, keepdims=True)
    return r * (dxh - a - xh * b), jnp.sum(dn * xh, axis=0, keepdims=True)


def gelu_pair(u):
    z = jnp.abs(u) * 0.7071067811865476
    t = 1.0 / (1.0 + 0.3275911 * z)
    ex = jnp.exp(-(z * z))
    poly = t * (
        0.254829592
        + t * (-0.284496736 + t * (1.421413741 + t * (-1.453152027 + t * 1.061405429)))
    )
    tail = 0.5 * poly * ex
    phi = jnp.where(u >= 0.0, 1.0 - tail, tail)
    return u * phi, phi + u * (ex * 0.3989422804014327)


def mask_bias(segc, segr, b, keys):
    row = lax.broadcasted_iota(jnp.int32, (BLK, keys), 0) + b * BLK
    col = lax.broadcasted_iota(jnp.int32, (BLK, keys), 1)
    return jnp.where((segc == segr[:, :keys]) & (col <= row), 0.0, MASKED)


def half_lane(hh):
    lane = lax.broadcasted_iota(jnp.int32, (BLK, 128), 1)
    return (lane >= 64) if hh else (lane < 64)


def residual_of(xr, pa, pb):
    return xr[...].astype(F32) + (pa[...].astype(F32) + pb[...].astype(F32))


def attn_fwd_kernel(blocks, split, h_ref, *refs):
    if split:
        own, peer, g, wqkv, wo, segc, segr = refs[:7]
        outs = refs[7:]
    else:
        xr, pa, pb, g, wqkv, wo, segc, segr = refs[:8]
        outs = refs[8:]
    x_out = None
    if not split:
        x_out, *outs = outs
    n_out, qkv_out, o_out, lse_out, p_out, ks, vs = outs
    i = pl.program_id(0)
    if split:
        mine = (i // (blocks // 2)) == h_ref[0]
        x = jnp.where(mine, own[...].astype(F32), peer[...].astype(F32))
    else:
        x = residual_of(xr, pa, pb)
        x_out[...] = x.astype(BF)
    xh, _ = norm_stats(x)
    n = (xh * g[...]).astype(BF)
    n_out[...] = n
    q = (mm(n, wqkv[0]).astype(BF).astype(F32) * 0.125).astype(BF)
    k = mm(n, wqkv[1]).astype(BF)
    v = mm(n, wqkv[2]).astype(BF)
    qkv_out[0] = q
    qkv_out[1] = k
    qkv_out[2] = v
    rows = pl.ds(pl.multiple_of(i * BLK, BLK), BLK)
    ks[rows, :] = k
    vs[rows, :] = v
    pairs = q.shape[1] // 128
    for b in range(blocks):

        @pl.when(i == b)
        def _(b=b):
            keys = BLK * (b + 1)
            bias = mask_bias(segc[...], segr[...], b, keys)
            lse = jnp.zeros((BLK, 128), F32)
            lanes = lax.broadcasted_iota(jnp.int32, (BLK, 128), 1)
            total = jnp.zeros((BLK, wo.shape[1]), F32)
            for pr in range(pairs):
                cols = slice(pr * 128, pr * 128 + 128)
                qp = qkv_out[0, :, cols]
                kp = ks[0:keys, cols]
                vp = vs[0:keys, cols]
                res = []
                for hh in range(2):
                    qh = jnp.where(half_lane(hh), qp, jnp.zeros_like(qp))
                    s = mm_nt(qh, kp) + bias
                    m = jnp.max(s, axis=-1, keepdims=True)
                    e = jnp.exp(s - m)
                    l = jnp.sum(e, axis=-1, keepdims=True)
                    res.append(mm(e.astype(BF), vp) * (1.0 / l))
                    lse = jnp.where(lanes == pr * 2 + hh, m + jnp.log(l), lse)
                ob = jnp.where(half_lane(0), res[0], res[1]).astype(BF)
                o_out[:, cols] = ob
                total = total + mm(ob, wo[cols, :])
            lse_out[...] = lse
            p_out[...] = total.astype(BF)


def probs_kernel(blocks, qr, kf, lser, segc, segr, p_out):
    i = pl.program_id(0)
    pairs = kf.shape[2] // 128
    for b in range(blocks):

        @pl.when(i == b)
        def _(b=b):
            keys = BLK * (b + 1)
            bias = mask_bias(segc[...], segr[...], b, keys)
            lse = lser[...]
            for pr in range(pairs):
                cols = slice(pr * 128, pr * 128 + 128)
                qp = qr[0, :, cols]
                kp = kf[0, 0:keys, cols]
                for hh in range(2):
                    h = pr * 2 + hh
                    qh = jnp.where(half_lane(hh), qp, jnp.zeros_like(qp))
                    p = jnp.exp(mm_nt(qh, kp) + bias - lse[:, h : h + 1])
                    p_out[h, :, 0:keys] = p.astype(BF)


def attn_bwd_kernel(blocks, split, h_ref, *refs):
    if split:
        dro, drp, dno, dnp_ = refs[:4]
    else:
        drr, dna, dnb = refs[:3]
    if split:
        xr, pa, pb = refs[4:7]
        xn = residual_of(xr, pa, pb)
        rest = refs[7:]
    else:
        xn = refs[3][...].astype(F32)
        rest = refs[4:]
    gn, qr, kf, vf, orf, pr_in, wqkv, wo = rest[:8]
    da_out, dqk_out, dv_out, dn_out, dg_out, dks, dvs = rest[8:]
    i = pl.program_id(0)
    blk = blocks - 1 - i
    if split:
        mine = (blk // (blocks // 2)) == h_ref[0]
        dr = jnp.where(mine, dro[...].astype(F32), drp[...].astype(F32))
        dn = jnp.where(mine, dno[...].astype(F32), dnp_[...].astype(F32))
    else:
        dr = drr[...].astype(F32)
        dn = dna[...].astype(F32) + dnb[...].astype(F32)
    dx, dg = norm_back(xn, gn[...], dn)
    da = (dr + dx).astype(BF)
    da_out[...] = da

    @pl.when(i == 0)
    def _():
        dks[...] = jnp.zeros_like(dks)
        dvs[...] = jnp.zeros_like(dvs)
        dg_out[...] = jnp.zeros_like(dg_out)

    dg_out[...] += jnp.broadcast_to(dg, dg_out.shape)
    do = mm_nt(da, wo[...]).astype(BF)
    pairs = wo.shape[0] // 128
    for b in range(blocks):

        @pl.when(blk == b)
        def _(b=b):
            keys = BLK * (b + 1)
            here = slice(b * BLK, b * BLK + BLK)
            for pr in range(pairs):
                cols = slice(pr * 128, pr * 128 + 128)
                qp = qr[0, :, cols]
                kp = kf[0, 0:keys, cols]
                vp = vf[0, 0:keys, cols]
                dop = do[:, cols]
                prod = dop.astype(F32) * orf[:, cols].astype(F32)
                dqs, dss, ps, qs, dos = [], [], [], [], []
                for hh in range(2):
                    hm = half_lane(hh)
                    qh = jnp.where(hm, qp, jnp.zeros_like(qp))
                    doh = jnp.where(hm, dop, jnp.zeros_like(dop))
                    delta = jnp.sum(jnp.where(hm, prod, 0.0), axis=-1, keepdims=True)
                    h = pr * 2 + hh
                    p = pr_in[h, :, 0:keys]
                    dp = mm_nt(doh, vp)
                    ds = (p.astype(F32) * (dp - delta)).astype(BF)
                    dqs.append(mm(ds, kp))
                    dks[0:keys, cols] += mm_tn(ds, qh)
                    dvs[0:keys, cols] += mm_tn(p, doh)
                dq = jnp.where(half_lane(0), dqs[0], dqs[1]) * 0.125
                dqk_out[:, cols] = dq.astype(BF)
            dqk_out[:, pairs * 128 :] = dks[here, :].astype(BF)
            dv_out[...] = dvs[here, :].astype(BF)

    c = pairs * 128
    dn_out[...] = (
        mm_nt(dqk_out[:, :c], wqkv[0]) + mm_nt(dqk_out[:, c:], wqkv[1]) + mm_nt(dv_out[...], wqkv[2])
    ).astype(BF)


def dense_fwd_kernel(
    blocks, h_ref, own, peer, pa, pb, g, up, down, x_out, n_out, act_out, gp_out, p_out
):
    mine = (pl.program_id(0) // (blocks // 2)) == h_ref[0]
    x = jnp.where(mine, own[...].astype(F32), peer[...].astype(F32))
    x = x + (pa[...].astype(F32) + pb[...].astype(F32))
    x_out[...] = x.astype(BF)
    xh, _ = norm_stats(x)
    n = (xh * g[...]).astype(BF)
    n_out[...] = n
    act, gp = gelu_pair(mm(n, up[...]))
    act = act.astype(BF)
    act_out[...] = act
    gp_out[...] = gp.astype(BF)
    p_out[...] = mm(act, down[...]).astype(BF)


def dense_bwd_kernel(drr, dna, dnb, xn, gn, gp, up, down, df_out, du_out, dn_out, dg_out):
    dx, dg = norm_back(xn[...].astype(F32), gn[...], dna[...].astype(F32) + dnb[...].astype(F32))
    df = (drr[...].astype(F32) + dx).astype(BF)
    df_out[...] = df

    @pl.when(pl.program_id(0) == 0)
    def _():
        dg_out[...] = jnp.zeros_like(dg_out)

    dg_out[...] += jnp.broadcast_to(dg, dg_out.shape)
    du = (mm_nt(df, down[...]) * gp[...].astype(F32)).astype(BF)
    du_out[...] = du
    dn_out[...] = mm_nt(du, up[...]).astype(BF)


def final_kernel(h_ref, drr, dna, dnb, xo, xp, gn, dr_out, dg_out):
    i = pl.program_id(0)
    mine = i >= 2
    x = jnp.where(mine, xo[...].astype(F32), xp[...].astype(F32))
    dx, dg = norm_back(x, gn[...], dna[...].astype(F32) + dnb[...].astype(F32))
    dr_out[...] = drr[...].astype(F32) + dx

    @pl.when(i == 0)
    def _():
        dg_out[...] = jnp.zeros_like(dg_out)

    dg_out[...] += jnp.broadcast_to(dg, dg_out.shape)


def spread_kernel(rows_ref, slot_ref, out_ref):
    count = out_ref.shape[0]
    place = lax.broadcasted_iota(jnp.int32, (count, rows_ref.shape[0]), 0)
    place = place + pl.program_id(0) * count
    hot = (place == slot_ref[...]).astype(F32).astype(BF)
    out_ref[...] = mm(hot, rows_ref[...]).astype(BF)


def route_kernel(h_ref, xr, pa, pb, g, slot_ref, x_out, send_out, ms):
    i = pl.program_id(0)
    x = residual_of(xr, pa, pb)
    x_out[...] = x
    xh, _ = norm_stats(x)
    rows = pl.ds(pl.multiple_of(i * BLK, BLK), BLK)
    ms[rows, :] = (xh * g[...]).astype(BF)

    @pl.when(i == pl.num_programs(0) - 1)
    def _():
        count = send_out.shape[0]
        place = lax.broadcasted_iota(jnp.int32, (count, ms.shape[0]), 0)
        hot = (place == slot_ref[...]).astype(F32).astype(BF)
        send_out[...] = mm(hot, ms[...]).astype(BF)


def collect_kernel(table, slot_ref, out_ref):
    count = table.shape[0]
    place = lax.broadcasted_iota(jnp.int32, (out_ref.shape[0], count), 1)
    hot = (place == slot_ref[...]).astype(F32).astype(BF)
    out_ref[...] = mm(hot, table[...]).astype(BF)


def collect_add_kernel(h_ref, table, slot_ref, x_ref, out_ref):
    count = table.shape[0]
    place = lax.broadcasted_iota(jnp.int32, (out_ref.shape[0], count), 1)
    hot = (place == slot_ref[...]).astype(F32).astype(BF)
    out_ref[...] = (x_ref[...] + mm(hot, table[...])).astype(BF)


def expert_kernel(
    half, mo, mp, go, gp_, cen, up, down,
    yo, yp, dmo, dmp, m_all, dy_all, ae_all, due_all, dc_out,
):
    i = pl.program_id(0)
    first = i < half
    m = jnp.where(first, mo[...], mp[...])
    gb = jnp.where(first, go[...], gp_[...]).astype(F32)
    mf = m.astype(F32)
    cf = cen[...].astype(F32)
    gate = jax.nn.sigmoid(jnp.sum(mf * cf, axis=-1, keepdims=True))
    dy = (gate * gb).astype(BF)
    u = mm(m, up[0])
    dact = mm_nt(dy, down[0])
    act, gd = gelu_pair(u)
    act = act.astype(BF)
    y = mm(act, down[0])
    dscore = jnp.sum(gb * y, axis=-1, keepdims=True) * gate * (1.0 - gate)
    due = (dact * gd).astype(BF)
    dm = (mm_nt(due, up[0]) + dscore * cf).astype(BF)
    gy = (gate * y).astype(BF)
    m_all[...] = m
    dy_all[...] = dy
    ae_all[...] = act
    due_all[...] = due

    @pl.when(i == 0)
    def _():
        dc_out[...] = jnp.zeros_like(dc_out)

    dc_out[...] += jnp.broadcast_to(jnp.sum(dscore * mf, axis=0, keepdims=True), dc_out.shape)

    @pl.when(first)
    def _():
        yo[...] = gy
        dmo[...] = dm

    @pl.when(jnp.logical_not(first))
    def _():
        yp[...] = gy
        dmp[...] = dm


def shape(dims, kind):
    return jax.ShapeDtypeStruct(dims, kind)


def fixed(dims):
    zero = (0,) * len(dims)
    return pl.BlockSpec(dims, lambda *a: zero, pipeline_mode=pl.Buffered(1))


def rows_spec(width, index=lambda i: i):
    return pl.BlockSpec((BLK, width), lambda i, *a: (index(i), 0))


def call(
    kernel, grid, in_specs, out_specs, outs, scratch, flops, moved, args, prefetch=None, limit=VLIM
):
    params = pltpu.CompilerParams(
        vmem_limit_bytes=int(limit), dimension_semantics=("arbitrary",)
    )
    cost = pl.CostEstimate(flops=int(flops), bytes_accessed=int(moved), transcendentals=0)
    if prefetch is None:
        spec = pl.GridSpec(
            grid=grid, in_specs=in_specs, out_specs=out_specs, scratch_shapes=scratch
        )
    else:
        spec = pltpu.PrefetchScalarGridSpec(
            num_scalar_prefetch=1,
            grid=grid,
            in_specs=in_specs,
            out_specs=out_specs,
            scratch_shapes=scratch,
        )
        args = (prefetch,) + tuple(args)
    return pl.pallas_call(
        kernel, grid_spec=spec, out_shape=outs, compiler_params=params, cost_estimate=cost
    )(*args)


def attention_forward(h, inputs, split, gain, wqkv, wo, segc, segr):
    length, d = segc.shape[0], wqkv.shape[1]
    c = wqkv.shape[2]
    blocks = length // BLK
    if split:
        ins = [rows_spec(d, lambda i: i % (blocks // 2))] * 2
    else:
        ins = [rows_spec(d)] * 3
    ins += [
        fixed((1, d)),
        fixed((3, d, c)),
        fixed((c, d)),
        pl.BlockSpec((BLK, 1), lambda i, *a: (i, 0)),
        fixed((1, length)),
    ]
    outs = [] if split else [(rows_spec(d), shape((length, d), BF))]
    outs += [
        (rows_spec(d), shape((length, d), BF)),
        (pl.BlockSpec((3, BLK, c), lambda i, *a: (0, i, 0)), shape((3, length, c), BF)),
        (rows_spec(c), shape((length, c), BF)),
        (rows_spec(128), shape((length, 128), F32)),
        (rows_spec(d), shape((length, d), BF)),
    ]
    scratch = [pltpu.VMEM((length, c), BF), pltpu.VMEM((length, c), BF)]
    flops = 2 * length * d * c * 4 + 4 * length * length * c
    return call(
        functools.partial(attn_fwd_kernel, blocks, split),
        (blocks,),
        ins,
        [o[0] for o in outs],
        [o[1] for o in outs],
        scratch,
        flops * 2,
        length * d * 20,
        (*inputs, gain, wqkv, wo, segc, segr),
        prefetch=h,
    )


def attention_probs(qkv, lse, segc, segr):
    length, c = qkv.shape[1:]
    heads = c // HEAD_DIM
    return call(
        functools.partial(probs_kernel, length // BLK),
        (length // BLK,),
        [
            pl.BlockSpec((1, BLK, c), lambda i, *a: (0, i, 0)),
            pl.BlockSpec((1, length, c), lambda i, *a: (1, 0, 0), pipeline_mode=pl.Buffered(1)),
            rows_spec(128),
            pl.BlockSpec((BLK, 1), lambda i, *a: (i, 0)),
            fixed((1, length)),
        ],
        [pl.BlockSpec((heads, BLK, length), lambda i, *a: (0, i, 0))],
        [shape((heads, length, length), BF)],
        [],
        4 * length * length * c,
        2 * heads * length * length,
        (qkv, qkv, lse, segc, segr),
    )[0]


def attention_backward(h, inputs, split, gn, saved, wqkv, wo):
    qkv, o, probs = saved
    length, d = o.shape[0], wqkv.shape[1]
    c = wqkv.shape[2]
    blocks = length // BLK
    back = lambda i: blocks - 1 - i
    if split:
        ins = [rows_spec(d, lambda i: back(i) % (blocks // 2))] * 4 + [rows_spec(d, back)] * 3
    else:
        ins = [rows_spec(d, back)] * 4
    part = lambda n: pl.BlockSpec(
        (1, length, c), lambda i, *a: (n, 0, 0), pipeline_mode=pl.Buffered(1)
    )
    ins += [
        fixed((1, d)),
        pl.BlockSpec((1, BLK, c), lambda i, *a: (0, back(i), 0)),
        part(1),
        part(2),
        rows_spec(c, back),
        pl.BlockSpec((c // HEAD_DIM, BLK, length), lambda i, *a: (0, back(i), 0)),
        fixed((3, d, c)),
        fixed((c, d)),
    ]
    outs = [
        (rows_spec(d, back), shape((length, d), BF)),
        (rows_spec(2 * c, back), shape((length, 2 * c), BF)),
        (rows_spec(c, back), shape((length, c), BF)),
        (rows_spec(d, back), shape((length, d), BF)),
        (fixed((8, d)), shape((8, d), F32)),
    ]
    scratch = [pltpu.VMEM((length, c), F32), pltpu.VMEM((length, c), F32)]
    flops = 2 * length * d * c * 4 + 10 * length * length * c
    return call(
        functools.partial(attn_bwd_kernel, blocks, split),
        (blocks,),
        ins,
        [s[0] for s in outs],
        [s[1] for s in outs],
        scratch,
        flops * 2,
        length * d * 20,
        (*inputs, gn, qkv, qkv, qkv, o, probs, wqkv, wo),
        prefetch=h,
    )


def dense_forward(h, own, peer, pa, pb, gain, up, down):
    length, d = pa.shape
    f = up.shape[1]
    blocks = length // BLK
    half = rows_spec(d, lambda i: lax.rem(i, blocks // 2))
    return call(
        functools.partial(dense_fwd_kernel, blocks),
        (blocks,),
        [half] * 2 + [rows_spec(d)] * 2 + [fixed((1, d)), fixed((d, f)), fixed((f, d))],
        [rows_spec(d), rows_spec(d), rows_spec(f), rows_spec(f), rows_spec(d)],
        [
            shape((length, d), BF),
            shape((length, d), BF),
            shape((length, f), BF),
            shape((length, f), BF),
            shape((length, d), BF),
        ],
        [],
        4 * length * d * f,
        length * d * 20 + 4 * d * f,
        (own, peer, pa, pb, gain, up, down),
        prefetch=h,
    )


def dense_backward(dr, dna, dnb, xn, gn, gp, up, down):
    length, d = dr.shape
    f = up.shape[1]
    return call(
        dense_bwd_kernel,
        (length // BLK,),
        [rows_spec(d)] * 4
        + [fixed((1, d)), rows_spec(f), fixed((d, f)), fixed((f, d))],
        [rows_spec(d), rows_spec(f), rows_spec(d), fixed((8, d))],
        [
            shape((length, d), BF),
            shape((length, f), BF),
            shape((length, d), BF),
            shape((8, d), F32),
        ],
        [],
        4 * length * d * f,
        length * d * 20 + 4 * d * f,
        (dr, dna, dnb, xn, gn, gp, up, down),
    )


def own_last(blocks):
    return lambda i, h: lax.rem(i + (blocks // 2) * (1 - h[0]), blocks)


def final_step(h, dr, dna, dnb, xo, xp, gn):
    length, d = dr.shape
    blocks = length // BLK
    place = own_last(blocks)
    spec = pl.BlockSpec((BLK, d), lambda i, h: (place(i, h), 0))
    late = lambda i, h: (jnp.maximum(i - blocks // 2, 0), 0)
    return call(
        final_kernel,
        (blocks,),
        [spec] * 3
        + [pl.BlockSpec((BLK, d), late)]
        + [pl.BlockSpec((BLK, d), lambda i, h: (lax.rem(i, blocks // 2), 0)), fixed((1, d))],
        [pl.BlockSpec((BLK, d), late), fixed((8, d))],
        [shape((length // 2, d), F32), shape((8, d), F32)],
        [],
        length * d * 40,
        length * d * 14,
        (dr, dna, dnb, xo, xp, gn),
        prefetch=h,
        limit=SMALL,
    )


def route_step(h, x, pa, pb, gain, slot_row, slots):
    length, d = x.shape
    per = length // 2 // BLK
    spec = pl.BlockSpec((BLK, d), lambda i, h: (h[0] * per + i, 0))
    return call(
        route_kernel,
        (per,),
        [spec] * 3 + [fixed((1, d)), fixed((1, length // 2))],
        [rows_spec(d), fixed((slots, d))],
        [shape((length // 2, d), F32), shape((slots, d), BF)],
        [pltpu.VMEM((length // 2, d), BF)],
        length * slots * d,
        length * d * 14,
        (x, pa, pb, gain, slot_row),
        prefetch=h,
        limit=SMALL,
    )


def spread(rows, slot_row, slots):
    count, d = rows.shape
    return call(
        spread_kernel,
        (slots // BLK,),
        [fixed((count, d)), fixed((1, count))],
        [rows_spec(d)],
        [shape((slots, d), BF)],
        [],
        2 * count * slots * d,
        4 * slots * d,
        (rows, slot_row),
        limit=SMALL,
    )[0]


def collect(table, slot_col):
    slots, d = table.shape
    count = slot_col.shape[0]
    return call(
        collect_kernel,
        (count // BLK,),
        [fixed((slots, d)), pl.BlockSpec((BLK, 1), lambda i, *a: (i, 0))],
        [rows_spec(d)],
        [shape((count, d), BF)],
        [],
        2 * count * slots * d,
        4 * slots * d,
        (table, slot_col),
        limit=SMALL,
    )[0]


def collect_add(h, table, slot_col, x):
    slots, d = table.shape
    count = slot_col.shape[0]
    per = count // BLK
    return call(
        collect_add_kernel,
        (per,),
        [
            fixed((slots, d)),
            pl.BlockSpec((BLK, 1), lambda i, *a: (i, 0)),
            rows_spec(d),
        ],
        [rows_spec(d)],
        [shape((count, d), BF)],
        [],
        2 * count * slots * d,
        8 * slots * d,
        (table, slot_col, x),
        prefetch=h,
        limit=SMALL,
    )[0]


def expert_step(mo, mp, go, gp, cen, up, down):
    rows, d = mo.shape
    f = up.shape[2]
    half = rows // BLK
    lo = lambda i: jnp.minimum(i, half - 1)
    hi = lambda i: jnp.maximum(i - half, 0)
    return call(
        functools.partial(expert_kernel, half),
        (2 * half,),
        [rows_spec(d, lo), rows_spec(d, hi), rows_spec(d, lo), rows_spec(d, hi)]
        + [fixed((1, d)), fixed((1, d, f)), fixed((1, f, d))],
        [rows_spec(d, lo), rows_spec(d, hi), rows_spec(d, lo), rows_spec(d, hi)]
        + [rows_spec(d), rows_spec(d), rows_spec(f), rows_spec(f), fixed((8, d))],
        [shape((rows, d), BF)] * 4
        + [shape((2 * rows, d), BF)] * 2
        + [shape((2 * rows, f), BF)] * 2
        + [shape((8, d), F32)],
        [],
        16 * rows * d * f,
        rows * d * 24 + rows * f * 8,
        (mo, mp, go, gp, cen, up, down),
    )


def slot_index(chosen, capacity, experts):
    rows = chosen.shape[0]
    matches = chosen[:, None] == jnp.arange(experts, dtype=jnp.int32)[None, :]
    position = jnp.arange(rows, dtype=jnp.int32)
    earlier = (position[None, :] < position[:, None]).astype(BF)
    before = jnp.dot(earlier, matches.astype(BF), preferred_element_type=F32)
    rank = jnp.sum(jnp.where(matches, before, 0.0), axis=1).astype(jnp.int32)
    return chosen * capacity + rank


def swap(v):
    return lax.ppermute(v, "head", SWAP)


def pick(bit, a, b):
    return jnp.where(bit == 1, a, b)


def total_of(a, b):
    return (a.astype(F32) + b.astype(F32)).astype(BF)


def whole(arrays):
    return [pl.BlockSpec(a.shape, lambda i, *r, n=len(a.shape): (0,) * n) for a in arrays]


def one_step(kernel, bits, args, outs):
    moved = sum(a.size * a.dtype.itemsize for a in (*args, *outs))
    return call(
        kernel,
        (1,),
        whole(args),
        whole(outs),
        outs,
        [],
        moved,
        moved,
        args,
        prefetch=bits,
        limit=2 * moved + 8 * 1024 * 1024,
    )


def sum_kernel(h_ref, a, b, out):
    out[...] = total_of(a[...], b[...])


PLACE = {1: 0, 2: 1, 4: 2, 8: 3}


def fold_kernel(plan, n_in, bits, *refs):
    def get(piece):
        at, lo, n = piece
        return refs[at][lo : lo + n, :]

    def put(piece, value):
        at, lo, n = piece
        refs[n_in + at][lo : lo + n, :] = value

    for kind, ins, outs, place in plan:
        if kind == "copy":
            put(outs[0], get(ins[0]))
        elif kind == "sum":
            put(outs[0], total_of(get(ins[0]), get(ins[1])))
        elif kind == "split":
            (ka, kl, n), (ga, gl, _) = ins
            q = n // 2
            lo = total_of(get((ka, kl, q)), get((ga, gl, q)))
            hi = total_of(get((ka, kl + q, q)), get((ga, gl + q, q)))
            put(outs[0], pick(bits[place], lo, hi))
            put(outs[1], pick(bits[place], hi, lo))
        else:
            p, g = get(ins[0]), get(ins[1])
            at, lo, n = outs[0]
            put((at, lo, n // 2), pick(bits[place], g, p))
            put((at, lo + n // 2, n // 2), pick(bits[place], p, g))


def first_fold_kernel(places, bits, *refs):
    outs = refs[4 * len(places) :]
    for j, place in enumerate(places):
        kl, kh, gl, gh = refs[4 * j : 4 * j + 4]
        lo, hi = total_of(kl[...], gl[...]), total_of(kh[...], gh[...])
        outs[2 * j][...] = pick(bits[place], lo, hi)
        outs[2 * j + 1][...] = pick(bits[place], hi, lo)


def first_fold(bits, parts):
    args, ins, outs, out_specs, places = [], [], [], [], []
    for p in parts:
        keep, got = p.kept[0], p.got[0]
        n, width = keep.shape
        low = pl.BlockSpec((n // 8, width), lambda i, *a: (i, 0))
        high = pl.BlockSpec((n // 8, width), lambda i, *a: (i + 4, 0))
        args += [keep, keep, got, got]
        ins += [low, high, low, high]
        outs += [shape((n // 2, width), BF)] * 2
        out_specs += [low, low]
        places.append(PLACE[p.order[p.phase]])
    moved = sum(a.size * 2 for a in args)
    made = call(
        functools.partial(first_fold_kernel, tuple(places)),
        (4,),
        ins,
        out_specs,
        outs,
        [],
        moved,
        moved,
        args,
        prefetch=bits,
    )
    for j, p in enumerate(parts):
        rows = outs[2 * j].shape[0]
        p.sent, p.kept = (made[2 * j], 0, rows), (made[2 * j + 1], 0, rows)


class Part:
    def __init__(self, order, send, keep=None):
        self.order, self.phase = order, 0
        self.sent = (send, 0, send.shape[0])
        self.kept = None if keep is None else (keep, 0, keep.shape[0])
        self.got = None
        self.fresh = True

    @property
    def live(self):
        return self.phase < len(self.order)


def halving(order):
    return order + order[::-1]


def advance(bits, parts, during=None, inputs=()):
    parts = [p for p in parts if p.live]
    width = parts[0].sent[0].shape[1]
    buffers = {}
    for p in parts:
        buffers.setdefault(p.order[p.phase], p.sent[0])
    steps = sorted(buffers)
    flat, inputs = lax.optimization_barrier(([buffers[s] for s in steps], inputs))
    got = [lax.ppermute(v, "dp", [(i, i ^ s) for i in range(16)]) for v, s in zip(flat, steps)]
    result = during(*inputs) if during else inputs
    (flat, got), result = lax.optimization_barrier(((flat, got), result))
    for p in parts:
        at = steps.index(p.order[p.phase])
        p.sent = (flat[at],) + p.sent[1:]
        p.got = (got[at],) + p.sent[1:]
        p.phase += 1
    return result


def fold(bits, parts):
    args, plan, rows, moved = [], [], {}, []

    def source(piece):
        for j, a in enumerate(args):
            if a is piece[0]:
                return (j,) + piece[1:]
        args.append(piece[0])
        return (len(args) - 1,) + piece[1:]

    def room(name, n):
        lo = rows.get(name, 0)
        rows[name] = lo + n
        return (name, lo, n)

    for p in parts:
        if not p.live:
            continue
        step = p.order[p.phase]
        half = len(p.order) // 2
        if p.phase == 0:
            ins, kind, place = [source(p.sent)], "copy", 0
            outs = [room(step, p.sent[2])]
        elif p.kept is not None and p.kept[0] is None:
            ins, kind, place = [source(p.sent), source(p.got)], "sum", 0
            outs = [room(step, p.sent[2])]
        elif p.phase < half:
            ins, kind, place = [source(p.kept), source(p.got)], "split", PLACE[step]
            n = p.kept[2] // 2
            outs = [room(step, n), room("keep", n)]
        elif p.phase == half:
            ins, kind, place = [source(p.kept), source(p.got)], "sum", 0
            outs = [room(step, p.kept[2])]
        else:
            ins, kind, place = [source(p.sent), source(p.got)], "raise", PLACE[p.order[p.phase - 1]]
            outs = [room(step, 2 * p.sent[2])]
        plan.append((kind, ins, outs, place))
        moved.append(p)
    names = list(rows)
    width = args[0].shape[1]
    shapes = [shape((rows[n], width), BF) for n in names]
    fixed_plan = tuple(
        (kind, tuple(ins), tuple((names.index(o[0]),) + o[1:] for o in outs), place)
        for kind, ins, outs, place in plan
    )
    made = one_step(functools.partial(fold_kernel, fixed_plan, len(args)), bits, args, shapes)
    for p, (_, _, outs, _) in zip(moved, plan):
        p.sent = (made[names.index(outs[0][0])],) + outs[0][1:]
        if len(outs) > 1:
            p.kept = (made[names.index(outs[1][0])],) + outs[1][1:]


def ends(bits, ref_s, ref_g, piece, place):
    lo, n = piece
    a, b = ref_s[lo : lo + n, :].astype(F32), ref_g[lo : lo + n, :].astype(F32)
    return pick(bits[place], b, a), pick(bits[place], a, b)


def put_query_key(qkv, blocks):
    c = qkv.shape[2]
    n = blocks[0].shape[0]
    for j, block in enumerate(blocks):
        qkv[0, j * n : j * n + n, :] = block[:, :c]
        qkv[1, j * n : j * n + n, :] = block[:, c:]


def put_value_out(qkv, out, v, o):
    c = qkv.shape[2]
    n = v.shape[0]
    qkv[2, :n, :] = v[:, :c]
    qkv[2, n:, :] = v[:, c:]
    out[...] = o


def finish_wide_kernel(at, bits, xp, xg, yp, yg, ap, ag, bp, bg, up, down, qkv, out):
    lo, hi = ends(bits, xp, xg, at[0], 0)
    f = lo.shape[1]
    up[:, :f] = lo
    up[:, f:] = hi
    lo, hi = ends(bits, yp, yg, at[1], 1)
    f = lo.shape[0]
    down[:f, :] = lo
    down[f:, :] = hi
    put_query_key(qkv, ends(bits, ap, ag, at[2], 2))
    put_value_out(qkv, out, *ends(bits, bp, bg, at[3], 3))


def finish_narrow_kernel(at, bits, xp, xg, yp, yg, qkv, out):
    put_query_key(qkv, ends(bits, xp, xg, at[0], 0))
    put_value_out(qkv, out, *ends(bits, yp, yg, at[1], 1))


def stack_kernel(bits, *refs):
    out = refs[-1]
    row = lax.broadcasted_iota(jnp.int32, out.shape, 0)
    total = jnp.zeros(out.shape, F32)
    for j, ref in enumerate(refs[:-1]):
        total = jnp.where(row == j, ref[0:1, :], total)
    out[...] = total.astype(BF)


def finish(kernel, bits, parts, arrays, outs):
    at = tuple((p.sent[1], p.sent[2]) for p in parts)
    return one_step(functools.partial(kernel, at), bits, arrays, outs)


def body(
    steps,
    tokens,
    segment_ids,
    routes,
    norm_gains,
    qkv_one,
    out_one,
    up_one,
    down_one,
    qkv_two,
    out_two,
    expert_up,
    expert_down,
    centroids,
    cotangent,
):
    count, d = tokens.shape
    side = lax.axis_index("head")
    h = side.astype(jnp.int32).reshape(1)
    experts = lax.axis_size("dp") * expert_up.shape[0]
    capacity = 2 * count // experts
    slots = experts * capacity
    gains = norm_gains.astype(F32)
    gain = [gains[j : j + 1] for j in range(4)]
    segc, segr = segment_ids[:, None], segment_ids[None, :]

    chosen = lax.dynamic_slice_in_dim(routes[:, 0], side * count, count, 0)
    flat = slot_index(chosen, capacity, experts)
    slot_row, slot_col = flat[None, :], flat[:, None]

    def travel(v):
        box = v.reshape(experts, capacity, d)
        return lax.all_to_all(box, "dp", 0, 0, tiled=True).reshape(slots, d)

    def add(a, b):
        return one_step(sum_kernel, h, (a, b), [shape(a.shape, BF)])[0]

    tokens_peer = swap(tokens)
    n1, qkv1, o1, lse1, p1 = attention_forward(
        h, (tokens, tokens_peer), True, gain[0], qkv_one, out_one, segc, segr
    )
    p1r = swap(p1)
    cot_peer = swap(cotangent)
    p1r, cot_table = lax.optimization_barrier((p1r, spread(cotangent, slot_row, slots)))
    grad_own = travel(cot_table)
    grad_peer = swap(grad_own)
    x1, n2, act, gp, p2 = dense_forward(
        h, tokens, tokens_peer, p1, p1r, gain[1], up_one, down_one
    )
    p2r = swap(p2)
    first, n3, qkv2, o2, lse2, p3 = attention_forward(
        h, (x1, p2, p2r), False, gain[2], qkv_two, out_two, segc, segr
    )
    p3r = swap(p3)
    x2, sent = route_step(h, first, p3, p3r, gain[3], slot_row, slots)
    probs2 = attention_probs(qkv2, lse2, segc, segr)
    probs1 = attention_probs(qkv1, lse1, segc, segr)
    m_own, probs1, probs2 = lax.optimization_barrier((travel(sent), probs1, probs2))
    m_peer = swap(m_own)
    yo, yp, dmo, dmp, m_all, dy_all, ae_all, due_all, dc = expert_step(
        m_own, m_peer, grad_own, grad_peer, centroids, expert_up, expert_down
    )
    dm_sum = add(dmo, swap(dmp))
    y_sum = add(yo, swap(yp))
    up_grad = mm_tn(m_all, due_all)[None]
    down_grad = mm_tn(ae_all, dy_all)[None]
    dm_back, up_grad, down_grad, y_sum = lax.optimization_barrier(
        (travel(dm_sum), up_grad, down_grad, y_sum)
    )
    y_back = travel(y_sum)
    dm_own = collect(dm_back, slot_col)
    dm_peer = swap(dm_own)
    dc = dc[:1]
    cen_grad = dc + swap(dc)

    da2, dqk2, dv2, dn2, dg3 = attention_backward(
        h,
        (cotangent, cot_peer, dm_own, dm_peer, first, p3, p3r),
        True,
        gain[3],
        (qkv2, o2, probs2),
        qkv_two,
        out_two,
    )
    dn2r = swap(dn2)
    f = up_one.shape[1]
    c = qkv_one.shape[2]

    def grad(a, b):
        return mm_tn(a, b).astype(BF)

    def value_sides(n, dv):
        w = grad(n, dv)
        return jnp.concatenate([w[: d // 2], w[d // 2 :]], axis=1)

    def last_step(dr, dna, dnb):
        return final_step(h, dr, dna, dnb, tokens, tokens_peer, gain[0])

    def gather_y(y):
        return collect_add(h, y, slot_col, x2)

    def stack_gains(dg0):
        return jnp.concatenate([dg0[:1], dg1[:1], dg2[:1], dg3[:1]], axis=0)

    def last_attention(dr, dna, dnb):
        return attention_backward(
            h, (dr, dna, dnb, x1), False, gain[1], (qkv1, o1, probs1), qkv_one, out_one
        )

    if steps is None:
        df, du, dnd, dg2 = dense_backward(
            da2, dn2, dn2r, first, gain[2], gp, up_one, down_one
        )
        da1, dqk1, dv1, dn1, dg1 = last_attention(df, dnd, swap(dnd))
        input_grad, dg0 = last_step(da1, dn1, swap(dn1))
        second = gather_y(y_back)
        up_first, down_first, qk_two, v_two, wo_two, qk_one, v_one, wo_one, gain_grads = lax.psum(
            (
                grad(n2, du),
                grad(act, df),
                grad(n3, dqk2),
                grad(n3, dv2),
                grad(o2, da2),
                grad(n1, dqk1),
                grad(n1, dv1),
                grad(o1, da1),
                stack_gains(dg0),
            ),
            "dp",
        )

        def unpack(qk, v):
            return jnp.stack([qk[:, :c], qk[:, c:], v]).astype(F32)

        up_first, down_first = up_first.astype(F32), down_first.astype(F32)
        qkv_second, out_second = unpack(qk_two, v_two), wo_two.astype(F32)
        qkv_first, out_first = unpack(qk_one, v_one), wo_one.astype(F32)
    else:
        me = lax.axis_index("dp")
        bits = jnp.stack([(me // s) % 2 for s in (1, 2, 4, 8)]).astype(jnp.int32)

        def columns(v, bit):
            half = v.shape[1] // 2
            return lax.dynamic_slice_in_dim(v, bit * half, half, 1)

        def query_key(n, dqk, bit):
            return grad(columns(n, bit), dqk)

        def value_out(n, dv, o, da, bit):
            v, wo = value_sides(n, dv), grad(o, da)
            return jnp.where(bit == 1, v, wo), jnp.where(bit == 1, wo, v)

        qk_send = query_key(n3, dqk2, 1 - bits[2])
        qk_keep = query_key(n3, dqk2, bits[2])
        vo_send, vo_keep = value_out(n3, dv2, o2, da2, bits[3])
        (qk_send, qk_keep, vo_send, vo_keep), da2, dn2, dn2r, y_back = lax.optimization_barrier(
            ((qk_send, qk_keep, vo_send, vo_keep), da2, dn2, dn2r, y_back)
        )
        df, du, dnd, dg2 = dense_backward(
            da2, dn2, dn2r, first, gain[2], gp, up_one, down_one
        )
        dndr = swap(dnd)

        def gather_all(y, *dgs):
            stacked = one_step(stack_kernel, bits, dgs, [shape((16, d), BF)])[0]
            return gather_y(y), stacked

        def heavy(dr, dna, dnb, n, g, a, b):
            return last_attention(dr, dna, dnb), n, g, a, b

        orders = [halving(o) for o in ((1, 2, 4, 8), (2, 1, 8, 4), (4, 8, 1, 2), (8, 4, 2, 1))]
        big = [
            Part(orders[0], grad(n2, columns(du, 1 - bits[0]))),
            Part(orders[1], grad(columns(act, 1 - bits[1]), df)),
            Part(orders[2], qk_send, qk_keep),
            Part(orders[3], vo_send, vo_keep),
        ]
        last, n2, du, act, df = advance(bits, big, heavy, (df, dnd, dndr, n2, du, act, df))
        up_keep = grad(n2, columns(du, bits[0]))
        down_keep = grad(columns(act, bits[1]), df)
        da1, dqk1, dv1, dn1, dg1 = last
        dn1r = swap(dn1)
        big[0].kept = (up_keep, 0, up_keep.shape[0])
        big[1].kept = (down_keep, 0, down_keep.shape[0])
        first_fold(bits, big)

        def narrow_grads(n, dqk, dv, o, da):
            return (
                query_key(n, dqk, 1 - bits[0]),
                query_key(n, dqk, bits[0]),
                value_out(n, dv, o, da, bits[1]),
            )

        qk_send, qk_keep, (vo_send, vo_keep) = advance(
            bits, big, narrow_grads, (n1, dqk1, dv1, o1, da1)
        )
        small = [Part(orders[0], qk_send, qk_keep), Part(orders[1], vo_send, vo_keep)]
        parts = big + small
        fold(bits, parts)
        input_grad, dg0 = advance(bits, parts, last_step, (da1, dn1, dn1r))
        fold(bits, parts)
        second, gains_own = advance(bits, parts, gather_all, (y_back, dg0, dg1, dg2, dg3))
        tail = Part((1, 2, 4, 8), gains_own)
        tail.kept = (None, 0, 0)
        parts.append(tail)
        while big[0].live:
            fold(bits, parts)
            advance(bits, parts)
        fold(bits, parts)
        arrays = [x for p in big for x in (p.sent[0], p.got[0])]

        def finish_wide(*arrays):
            return finish(
                finish_wide_kernel,
                bits,
                big,
                arrays,
                [
                    shape((d, f), F32),
                    shape((f, d), F32),
                    shape((3, d, c), F32),
                    shape((c, d), F32),
                ],
            )

        up_first, down_first, qkv_second, out_second = advance(bits, small, finish_wide, arrays)
        while small[0].live:
            fold(bits, small)
            advance(bits, small)
        gain_grads = (tail.sent[0], tail.got[0])
        lo = tail.sent[1]
        gain_grads = sum(v[lo : lo + 4].astype(F32) for v in gain_grads)
        qkv_first, out_first = finish(
            finish_narrow_kernel,
            bits,
            small,
            [x for p in small for x in (p.sent[0], p.got[0])],
            [shape((3, d, c), F32), shape((c, d), F32)],
        )
    first_own = lax.dynamic_slice_in_dim(first, side * count, count, 0)
    return (
        first_own,
        second,
        input_grad,
        gain_grads,
        qkv_first,
        out_first,
        up_first,
        down_first,
        qkv_second,
        out_second,
        up_grad,
        down_grad,
        cen_grad,
    )


def solution(mesh):
    rows = P(("dp", "head"), None)
    shared = (
        P(None, None, "head"),
        P("head", None),
        P(None, "head"),
        P("head", None),
        P(None, None, "head"),
        P("head", None),
        P("dp", None, "head"),
        P("dp", "head", None),
        P("dp", None),
    )
    steps = 16 if mesh.shape["dp"] == 16 else None
    return jax.shard_map(
        functools.partial(body, steps),
        mesh=mesh,
        in_specs=(rows, P("dp"), P("dp", None), P(), *shared, rows),
        out_specs=(rows, rows, rows, P(), *shared),
        check_vma=False,
    )
```
